32 devices in a mesh: section: 4 (over y, core), dp: 8 (over z, x).
Axes of the slice: x: 2, y: 2, z: 4, core: 2. Of those that a mesh axis runs over, the one named last changes fastest.
Arguments:
- hidden: bfloat16 [4, 384, 8192], P('section', None, 'dp'), may hold values from -6 to 6
- norm_gain: bfloat16 [8192], P('dp'), may hold values from 0.25 to 1.75
- head: bfloat16 [8192, 8192], P(None, ('section', 'dp')), may hold values from -0.13258252 to 0.13258252
- reward_head: bfloat16 [8192], P('dp'), may hold values from -0.5 to 0.5
- tokens: int32 [4, 384], replicated, may hold values from 0 to 8191
- lengths: int32 [4], replicated, may hold values from 1 to 384, 1152 in all
Outputs:
- logprobs: float32 [4, 384], P('section')
- scores: float32 [4], P('section')
The draws below stay inside these ranges and needn't reach their ends.
Inputs may be any that keep to these rules, and one draw needn't show every extreme that they name: `lengths`: some span has length exactly 384.
All inputs are finite; a program needn't handle non-finite values.
Results may differ from the reference program's by a relative error of at most 0.0028.
Values may be sent and summed in bfloat16 or wider, within the bound.
No kernel may reach another device: no remote copies, remote signals or barrier semaphores. Data moves between devices by JAX's collectives and lax.ppermute only.
A program may use at most 128 MiB of HBM per device.

```python
import math
import jax
import jax.numpy as jnp
import numpy as np
from jax import lax

D = 8192
LEN = 384
SPANS = 4
V = 8192


def draw_head(key, part):
    stream = jax.random.fold_in(key, 11)
    values = jnp.clip(jax.random.normal(stream, (D, V), jnp.float32), -6.0, 6.0) * (2.0 / math.sqrt(D))
    return values.astype(jnp.bfloat16)


def draw_hidden(key, part):
    stream = jax.random.fold_in(key, 12)
    values = jnp.clip(jax.random.normal(stream, (SPANS, LEN, D), jnp.float32), -6.0, 6.0)
    return values.astype(jnp.bfloat16)


def touch_ends(values, key, low, high):
    longest = values.shape.index(max(values.shape))
    spots = []
    for shift in (0, 1):
        where = [jax.random.randint(jax.random.fold_in(key, axis), (), 0, length) for axis, length in enumerate(values.shape)]
        where[longest] = (where[longest] + shift) % values.shape[longest]
        spots.append(tuple(where))
    return values.at[spots[0]].set(low).at[spots[1]].set(high)


def shard_levels(stream_key, shape, pieces, low, high):
    loudness, own = 1.0, jax.random.fold_in(stream_key, 6)
    for dim, parts in pieces:
        heights = jnp.exp(jax.random.uniform(jax.random.fold_in(own, dim), (parts,), jnp.float32, low / len(pieces), high / len(pieces)))
        loudness = loudness * jnp.repeat(heights, shape[dim] // parts).reshape([-1 if axis == dim else 1 for axis in range(len(shape))])
    return loudness


def split_up(amount, total, limit, lean):
    weights = [(1 << 20) // math.isqrt(rank ** lean) + 1 for rank in range(2, amount + 1)]
    surplus, holding = total - limit - (amount - 1), [1] * (amount - 1)
    while surplus > 0:
        movable = [i for i in range(amount - 1) if holding[i] < limit]
        mass, remaining = sum([weights[i] for i in movable]), surplus
        for i in movable:
            extra = min(limit - holding[i], max(1, remaining * weights[i] // mass), surplus)
            holding[i] = holding[i] + extra
            surplus = surplus - extra
    return np.array([limit] + holding)


def uneven_parts(rng, amount, total, bound, skew):
    if amount == 2:
        one = jax.random.randint(rng, (), max(1, total - bound), min(bound, total - 1) + 1)
        return jnp.stack([one, total - one])
    sizes = jnp.asarray(split_up(amount, total, bound, skew), jnp.int32)
    pairs = (amount - 1) // 2
    source_of, taker = sizes[1:1 + 2 * pairs:2], sizes[2:2 + 2 * pairs:2]
    slack = jnp.minimum(source_of - 1, bound - taker)
    moved = jax.random.randint(jax.random.fold_in(rng, 1), (pairs,), 0, 1 << 20) % (slack + 1)
    sizes = sizes.at[1:1 + 2 * pairs:2].set(source_of - moved).at[2:2 + 2 * pairs:2].set(taker + moved)
    return sizes[jax.random.permutation(jax.random.fold_in(rng, 2), amount)]


def bell_draw(rng, dims, scale, bound, shards=(), kind=jnp.bfloat16):
    values = jax.random.normal(rng, dims, jnp.float32) * scale
    if len(shards) > 0:
        values = shard_levels(rng, dims, shards, -0.22, 0.18) * values
    return jnp.clip(values, min=-bound, max=bound).astype(kind)


def setup_inputs(seed: int = 0) -> dict:
    streams_of = jax.random.split(jax.random.key(seed), 7)
    return {
        "hidden": draw_hidden(jax.random.fold_in(streams_of[6], 71), 0),
        "norm_gain": jnp.clip(1.0 + 0.15 * jax.random.normal(streams_of[1], (D,), jnp.float32), 0.25, 1.75).astype(jnp.bfloat16),
        "head": draw_head(jax.random.fold_in(streams_of[6], 71), 0),
        "reward_head": bell_draw(streams_of[3], (D,), (max(D // 64, 1)) ** -0.5, 0.5, ((0, 8),)),
        "tokens": touch_ends(jax.random.randint(streams_of[4], (SPANS, LEN), 0, V), jax.random.fold_in(streams_of[4], 1), 0, V - 1).astype(jnp.int32),
        "lengths": uneven_parts(streams_of[5], SPANS, 3 * LEN * SPANS // 4, LEN, 2).astype(jnp.int32),
    }


def reference(hidden, norm_gain, head, reward_head, tokens, lengths):
    width = hidden.shape[2]

    def one_span(inputs):
        row_block, token_ids, length = inputs
        widened = row_block.astype(jnp.float32)
        inverse_rms = lax.rsqrt(lax.optimization_barrier(jnp.sum(widened * widened, axis=1)) / width + 1e-05)
        scaled = (widened * norm_gain.astype(jnp.float32)).astype(jnp.bfloat16)
        logits = inverse_rms[:, None] * jnp.dot(scaled, head, preferred_element_type=jnp.float32)
        totals = jax.nn.logsumexp(logits, axis=1)
        picked = jnp.take_along_axis(logits, token_ids[:, None].astype(jnp.int32), axis=1)[:, 0]
        inside = jnp.arange(row_block.shape[0], dtype=jnp.int32) < length
        logprob = jnp.where(inside, picked - totals, jnp.float32(0.0))
        reward = inverse_rms * jnp.dot(scaled, reward_head, preferred_element_type=jnp.float32)
        score = jnp.sum(jnp.where(inside, reward, jnp.float32(0.0))) / length.astype(jnp.float32)
        return (logprob, score)
    logprobs, scores = lax.map(one_span, (hidden, tokens, lengths))
    return (logprobs, scores)
```

```python
import jax
import jax.numpy as jnp
from jax import lax
from jax.sharding import PartitionSpec as P

AXES = ("section", "dp")
F32 = jnp.float32
BF16 = jnp.bfloat16


def combine(parts):
    top = parts[0][0]
    for part in parts[1:]:
        top = jnp.maximum(top, part[0])
    total = sum(part[1] * jnp.exp(part[0] - top) for part in parts)
    target = sum(part[2] for part in parts)
    return jnp.stack([top, total, target])


def summary(logits, vocab_ids, token_ids):
    top = jnp.max(logits, axis=-1)
    total = jnp.sum(jnp.exp(logits - top[:, None]), axis=-1)
    target = jnp.sum(jnp.where(vocab_ids[None, :] == token_ids[:, None], logits, F32(0.0)), axis=-1)
    return jnp.stack([top, total, target])


def row_map(lengths, section, count, half):
    pair, core = section // 2, section % 2
    first, second = lengths[2 * pair], lengths[2 * pair + 1]
    other_first = lengths[2 - 2 * pair]
    j = core * count + jnp.arange(count, dtype=jnp.int32)
    in_first = j < first
    in_second = j < first + second
    span = jnp.where(in_first, 2 * pair, jnp.where(in_second, 2 * pair + 1, 3 - 2 * pair))
    place = jnp.where(
        in_first, j, jnp.where(in_second, j - first, 2 * count - other_first + j - first - second)
    )
    return span, place


def per_device(groups, hidden, norm_gain, head, reward_head, tokens, lengths):
    section = lax.axis_index("section")
    dp_index = lax.axis_index("dp")
    core, pair = section % 2, section // 2
    sections = lax.axis_size("section")
    spans, positions = tokens.shape
    block, width, part = head.shape[1], head.shape[0], hidden.shape[2]
    count = 3 * spans * positions // 4 // sections
    half = positions // 2
    rows = hidden[0]

    swap = [(s, s ^ 1) for s in range(sections)]
    sibling = lax.ppermute(rows, "section", swap)
    extra = lax.ppermute(rows[half:], "section", [(1, 3), (3, 1)])
    head_sibling = lax.ppermute(head, "section", swap)

    span, place = row_map(lengths, section, count, half)
    own = (span == section)
    sib = (span == section + 1 - 2 * core)
    away = ~(own | sib)
    ids = jnp.arange(positions, dtype=jnp.int32)[None, :]
    pick_own = (own[:, None] & (ids == place[:, None])).astype(BF16)
    pick_sib = (sib[:, None] & (ids == place[:, None])).astype(BF16)
    pick_away = (away[:, None] & (ids[:, half:] == place[:, None])).astype(BF16)
    picked = (
        jnp.dot(pick_own, rows, preferred_element_type=F32)
        + jnp.dot(pick_sib, sibling, preferred_element_type=F32)
        + jnp.dot(pick_away, extra, preferred_element_type=F32)
    )
    mine = (picked * norm_gain.astype(F32)).astype(BF16)
    square_part = jnp.sum(picked * picked, axis=1)
    reward_part = jnp.sum(mine.astype(F32) * reward_head.astype(F32), axis=1)
    partial = jnp.stack([square_part, reward_part])
    slot = (jnp.arange(sections) == section)[:, None, None]
    sums = lax.psum(jnp.where(slot, partial[None], F32(0.0)), AXES)
    scales = lax.rsqrt(sums[:, 0] / width + 1e-05)
    rewards = scales * sums[:, 1]

    def mesh_perm(move):
        pairs = []
        for s in range(sections):
            for d in range(groups):
                s2, d2 = move(s, d)
                pairs.append((s * groups + d, s2 * groups + d2))
        return pairs

    if groups == 8:
        perm_a = mesh_perm(lambda s, d: (s, d ^ 1) if s % 2 == 0 else (s ^ 2, d))
        perm_b = mesh_perm(lambda s, d: (s ^ 2, d) if s % 2 == 0 else (s, d ^ 1))
        perm_z1 = mesh_perm(lambda s, d: (s, d ^ 2))
        perm_z3 = mesh_perm(lambda s, d: (s, d ^ 6))
        send = lambda value, perm: lax.ppermute(value, AXES, perm)
        big = (count * 7 // 9) // 16 * 16
        g, small = mine[:big], mine[big:]
        zero = core == 0

        a3 = send(small, perm_a)
        z1 = send(g, perm_z1)
        z3 = send(g, perm_z3)
        a0 = send(g, perm_a)
        b3 = send(jnp.concatenate([small, a3]), perm_b)
        b0 = send(g, perm_b)
        c0 = send(a0, perm_b)
        n3 = small.shape[0]
        wide = jnp.concatenate(
            [small, jnp.where(zero, b3[:n3], a3), jnp.where(zero, a3, b3[:n3]), b3[n3:]]
        )
        z2 = send(z3, perm_z1)
        a1 = send(z1, perm_a)
        b1 = send(z1, perm_b)
        c1 = send(a1, perm_b)
        w1 = send(wide, perm_z1)
        w3 = send(wide, perm_z3)
        a_3 = send(z3, perm_a)
        b_3 = send(z3, perm_b)
        c_3 = send(a_3, perm_b)
        a_2 = send(z2, perm_a)
        b_2 = send(z2, perm_b)
        c_2 = send(a_2, perm_b)
        w2 = send(w3, perm_z1)

        def times(value, where):
            start = where * part
            return jnp.concatenate(
                [
                    jnp.dot(value, lax.dynamic_slice_in_dim(h, start, part, 0), preferred_element_type=F32)
                    for h in (head, head_sibling)
                ],
                axis=1,
            )

        acc = [0.0, 0.0, 0.0, 0.0, 0.0, 0.0]
        order = [
            (0, g, a0, b0, c0, wide), (1, z1, a1, b1, c1, w1), (3, z3, a_3, b_3, c_3, w3), (2, z2, a_2, b_2, c_2, w2)
        ]
        for k, z_k, a_k, b_k, c_k, w_k in order:
            near = dp_index ^ (2 * k)
            far = near ^ 1
            acc[0] += times(z_k, near)
            acc[1] += times(a_k, jnp.where(zero, far, near))
            acc[2] += times(b_k, jnp.where(zero, near, far))
            acc[3] += times(c_k, far)
            acc[4] += times(w_k[: 2 * n3], near)
            acc[5] += times(w_k[2 * n3 :], far)
        low = acc[4] + acc[5]
        here = jnp.concatenate([acc[0] + jnp.where(zero, acc[1], acc[2]), low[:n3]])
        there = jnp.concatenate([acc[3] + jnp.where(zero, acc[2], acc[1]), low[n3:]])
    else:
        across = lax.ppermute(mine, "section", [(s, s ^ 2) for s in range(sections)])
        everything = lax.all_gather(jnp.concatenate([mine, across]), "dp", axis=1, tiled=True)
        both = jnp.concatenate(
            [jnp.dot(everything, h, preferred_element_type=F32) for h in (head, head_sibling)], axis=1
        )
        here, there = both[:count], both[count:]

    top_pair = pair == 0
    logits = jnp.concatenate([jnp.where(top_pair, here, there), jnp.where(top_pair, there, here)])
    flat_tokens = tokens.reshape(-1)
    all_ids = jnp.arange(spans * positions, dtype=jnp.int32)[None, :]
    token_ids, row_scales = [], []
    for p in range(2):
        s_, t_ = row_map(lengths, 2 * p + core, count, half)
        flat = s_ * positions + t_
        token_ids.append(jnp.sum(jnp.where(all_ids == flat[:, None], flat_tokens[None, :], 0), axis=1))
        row_scales.append(lax.dynamic_index_in_dim(scales, 2 * p + core, 0, keepdims=False))
    token_ids = jnp.concatenate(token_ids)
    logits = logits * jnp.concatenate(row_scales)[:, None]
    lane = jnp.arange(block, dtype=jnp.int32)
    vocab_ids = jnp.concatenate(
        [(section * groups + dp_index) * block + lane, ((section + 1 - 2 * core) * groups + dp_index) * block + lane]
    )
    stats = summary(logits, vocab_ids, token_ids)
    if groups == 8:
        stats = combine([stats] + [send(stats, mesh_perm(lambda s, d, k=k: (s, d ^ (2 * k)))) for k in (1, 2, 3)])
        stats = combine(
            [stats]
            + [send(stats, mesh_perm(lambda s, d, m=m: (s ^ m[0], d ^ m[1]))) for m in ((0, 1), (2, 0), (2, 1))]
        )
    else:
        gathered = lax.all_gather(stats, "dp")
        stats = combine([gathered[i] for i in range(groups)])
        stats = combine([stats, lax.ppermute(stats, "section", [(s, s ^ 2) for s in range(sections)])])
    logprob_list = stats[2] - (stats[0] + jnp.log(stats[1]))
    other_list = lax.ppermute(logprob_list, "section", swap)
    by_core = jnp.stack([jnp.where(core == 0, logprob_list, other_list), jnp.where(core == 0, other_list, logprob_list)])
    span_all, place_all = [], []
    for c in range(2):
        for p in range(2):
            s_, t_ = row_map(lengths, 2 * p + c, count, half)
            span_all.append(s_)
            place_all.append(t_)
    span_all, place_all = jnp.concatenate(span_all), jnp.concatenate(place_all)
    hit = (span_all == section)[None, :] & (place_all[None, :] == jnp.arange(positions, dtype=jnp.int32)[:, None])
    logprob = jnp.sum(jnp.where(hit, by_core.reshape(-1)[None, :], F32(0.0)), axis=1)
    span_sec = jnp.stack([row_map(lengths, s, count, half)[0] for s in range(sections)])
    score = jnp.sum(jnp.where(span_sec == section, rewards, F32(0.0))) / lengths[section].astype(F32)
    return (logprob[None], score[None])


def solution(mesh):
    groups = mesh.shape["dp"]
    return jax.shard_map(
        lambda *args: per_device(groups, *args),
        mesh=mesh,
        in_specs=(P("section", None, "dp"), P("dp"), P(None, ("section", "dp")), P("dp"), P(), P()),
        out_specs=(P("section", None), P("section")),
        check_vma=False,
    )
```

```python
import functools

import jax
import jax.numpy as jnp
from jax import lax
from jax.experimental import pallas as pl
from jax.experimental.pallas import tpu as pltpu
from jax.sharding import PartitionSpec as P

AXES = ("section", "dp")
F32 = jnp.float32
BF16 = jnp.bfloat16
I32 = jnp.int32
LANES = 128
VMEM = pl.BlockSpec(memory_space=pltpu.VMEM)
SMEM = pl.BlockSpec(memory_space=pltpu.SMEM)


def row_map(lengths, pair, core, index, count):
    first, second = lengths[2 * pair], lengths[2 * pair + 1]
    other_first = lengths[2 - 2 * pair]
    j = core * count + index
    in_first = j < first
    in_second = j < first + second
    span = jnp.where(in_first, 2 * pair, jnp.where(in_second, 2 * pair + 1, 3 - 2 * pair))
    place = jnp.where(
        in_first, j, jnp.where(in_second, j - first, 2 * count - other_first + j - first - second)
    )
    return span, place


def as_rows(columns, count):
    lane = lax.broadcasted_iota(I32, (count, LANES), 1)
    wide = jnp.zeros((count, LANES), F32)
    for i, column in enumerate(columns):
        wide = jnp.where(lane == i, column, wide)
    return jnp.transpose(wide)[:8]


def as_column(rows, which):
    full = jnp.concatenate([rows, jnp.zeros((LANES - 8, rows.shape[1]), F32)], axis=0)
    return jnp.transpose(full)[:, which : which + 1]


def pick_kernel(count, lengths, rows, sibling, extra, gain, reward, big, small, partial):
    section = lax.axis_index("section")
    core, pair = lax.rem(section, 2), lax.div(section, 2)
    positions, half = rows.shape[0], extra.shape[0]
    index = lax.broadcasted_iota(I32, (count, 1), 0)
    span, place = row_map(lengths, pair, core, index, count)
    source = jnp.where(span == section, place, place + positions)
    source = jnp.where(span // 2 == pair, source, place + (2 * positions - (positions - half)))
    lane = lax.broadcasted_iota(I32, (count, 2 * positions + half), 1)
    pick = jnp.where(lane == source, F32(1.0), F32(0.0)).astype(BF16)
    picked = jnp.dot(pick[:, :positions], rows[...], preferred_element_type=F32)
    picked += jnp.dot(pick[:, positions : 2 * positions], sibling[...], preferred_element_type=F32)
    picked += jnp.dot(pick[:, 2 * positions :], extra[...], preferred_element_type=F32)
    scaled = (picked * gain[...].astype(F32)).astype(BF16)
    n = big.shape[0]
    big[...] = scaled[:n]
    small[...] = scaled[n:]
    squares = jnp.sum(picked * picked, axis=1, keepdims=True)
    rewards = jnp.sum(scaled.astype(F32) * reward[...].astype(F32), axis=1, keepdims=True)
    padded = partial.shape[1]
    zeros = jnp.zeros((padded - count, 1), F32)
    partial[...] = as_rows(
        [jnp.concatenate([squares, zeros]), jnp.concatenate([rewards, zeros])], padded
    )


def token_kernel(count, n, lengths, tokens, out):
    core = lax.rem(lax.axis_index("section"), 2)
    spans, positions = tokens.shape
    for pair in range(2):
        index = lax.broadcasted_iota(I32, (count, 1), 0)
        span, place = row_map(lengths, pair, core, index, count)
        lane = lax.broadcasted_iota(I32, (count, positions), 1)
        ids = jnp.zeros((count, 1), F32)
        for s in range(spans):
            hit = (lane == place) & (span == s)
            ids += jnp.sum(jnp.where(hit, tokens[s : s + 1, :].astype(F32), F32(0.0)), axis=1, keepdims=True)
        ids = ids.astype(I32)
        m = count - n
        out[pair * n : pair * n + n, :] = ids[:n]
        out[2 * n + pair * m : 2 * n + pair * m + m, :] = ids[n:]


def offsets(k, n, m):
    section, dp_index = lax.axis_index("section"), lax.axis_index("dp")
    core, pair = lax.rem(section, 2), lax.div(section, 2)
    near = jnp.bitwise_xor(dp_index, 2 * k)
    far = jnp.bitwise_xor(near, 1)
    mine = pl.ds(pl.multiple_of(pair * n, n), n)
    others = pl.ds(pl.multiple_of((1 - pair) * n, n), n)
    small_mine = pl.ds(pl.multiple_of(2 * n + pair * m, 16), m)
    small_others = pl.ds(pl.multiple_of(2 * n + (1 - pair) * m, 16), m)
    return core, near, far, mine, others, small_mine, small_others


def add(acc, rows, value, first):
    for i, part in enumerate(value):
        w = part.shape[1]
        if first:
            acc[rows, i * w : (i + 1) * w] = part
        else:
            acc[rows, i * w : (i + 1) * w] = acc[rows, i * w : (i + 1) * w] + part


def mm_kernel(k, first, parts, *refs):
    refs = list(refs)
    head, sibling = refs.pop(0), refs.pop(0)
    acc_in = None if first else refs.pop(0)
    acc = refs.pop()
    named = dict(zip(parts, refs))
    depth = refs[0].shape[1]
    m = 64 if "w" not in named else named["w"].shape[0] // 4
    n = acc.shape[0] // 2 - m
    core, near, far, mine, others, small_mine, small_others = offsets(k, n, m)

    def times(value, where):
        rows = pl.ds(pl.multiple_of(where * depth, depth), depth)
        return [jnp.dot(value, h[rows, :], preferred_element_type=F32) for h in (head, sibling)]

    def plus(x, y):
        return [i + j for i, j in zip(x, y)]

    if not first:
        acc[...] = acc_in[...]
    if "a" in named:

        @pl.when(core == 0)
        def _():
            add(acc, mine, plus(times(named["z"][...], near), times(named["a"][...], far)), first)
            value = times(named["b"][...], near)
            if "c" in named:
                value = plus(value, times(named["c"][...], far))
            add(acc, others, value, first)

        @pl.when(core == 1)
        def _():
            add(acc, mine, plus(times(named["z"][...], near), times(named["b"][...], far)), first)
            value = times(named["a"][...], near)
            if "c" in named:
                value = plus(value, times(named["c"][...], far))
            add(acc, others, value, first)

    if "w" in named:
        w = named["w"]
        value = plus(times(w[: 2 * m, :], near), times(w[2 * m :, :], far))
        add(acc, small_mine, [v[:m] for v in value], first)
        add(acc, small_others, [v[m:] for v in value], first)


def summarize(logits, squares, token_ids, bases, block, width, out):
    scale = lax.rsqrt(squares / width + 1e-05)
    logits = logits * scale
    top = jnp.max(logits, axis=1, keepdims=True)
    total = jnp.sum(jnp.exp(logits - top), axis=1, keepdims=True)
    lane = lax.broadcasted_iota(I32, (1, block), 1)
    target = jnp.zeros(top.shape, F32)
    for i, base in enumerate(bases):
        hit = (lane + base) == token_ids
        target += jnp.sum(
            jnp.where(hit, logits[:, i * block : (i + 1) * block], F32(0.0)), axis=1, keepdims=True
        )
    count, padded = logits.shape[0], out.shape[1]
    zeros = jnp.zeros((padded - count, 1), F32)
    out[...] = as_rows([jnp.concatenate([v, zeros]) for v in (top, total, target)], padded)


def last_kernel(k, n, width, head, sibling, acc_in, c, sums, token_ids, out, acc):
    count = acc_in.shape[0] // 2
    m = count - n
    block = head.shape[1]
    section, dp_index = lax.axis_index("section"), lax.axis_index("dp")
    groups = lax.axis_size("dp")
    bases = [(section * groups + dp_index) * block, ((section + 1 - 2 * lax.rem(section, 2)) * groups + dp_index) * block]
    acc[...] = acc_in[...]
    if c is not None:
        _, near, far, mine, others, _, _ = offsets(k, n, m)
        depth = c.shape[1]
        rows = pl.ds(pl.multiple_of(far * depth, depth), depth)
        for i, h in enumerate((head, sibling)):
            cols = slice(i * block, (i + 1) * block)
            acc[others, cols] = acc[others, cols] + jnp.dot(c[...], h[rows, :], preferred_element_type=F32)
    squares = [as_column(sums[p], 0) for p in range(2)]
    column = jnp.concatenate([squares[0][:n], squares[1][:n], squares[0][n:count], squares[1][n:count]])
    summarize(acc[...], column, token_ids[...], bases, block, width, out)


def final_kernel(count, n, width, lengths, sums, stats, out_ref, score_ref):
    section = lax.axis_index("section")
    m = count - n
    positions = out_ref.shape[1]
    where = lax.broadcasted_iota(I32, (1, positions), 1)
    logprob = jnp.zeros((1, positions), F32)
    score = jnp.zeros((1, 1), F32)
    index = lax.broadcasted_iota(I32, (count, 1), 0)
    for core in range(2):
        s = stats[core]
        lp = as_column(s, 0)
        for pair in range(2):
            value = jnp.concatenate([lp[pair * n : pair * n + n], lp[2 * n + pair * m : 2 * n + pair * m + m]])
            span, place = row_map(lengths, pair, core, index, count)
            hit = (place == where) & (span == section)
            logprob += jnp.sum(jnp.where(hit, value, F32(0.0)), axis=0, keepdims=True)
            columns = jnp.transpose(
                jnp.concatenate([sums[core, pair], jnp.zeros((LANES - 8, sums.shape[3]), F32)], axis=0)
            )[:count]
            reward = columns[:, 1:2] * lax.rsqrt(columns[:, 0:1] / width + 1e-05)
            score += jnp.sum(jnp.where(span == section, reward, F32(0.0)), axis=0, keepdims=True)
    out_ref[...] = logprob
    score_ref[...] = score / lengths[section].astype(F32)


def combine(parts):
    top = parts[0][0]
    for part in parts[1:]:
        top = jnp.maximum(top, part[0])
    total = sum(part[1] * jnp.exp(part[0] - top) for part in parts)
    target = sum(part[2] for part in parts)
    return jnp.concatenate([jnp.stack([top, total, target]), jnp.zeros((5,) + top.shape, F32)])


def call(body, outs, in_specs, args, flops=0, moved=0, alias=None, limit=32):
    many = isinstance(outs, (list, tuple))
    return pl.pallas_call(
        body,
        out_shape=outs,
        in_specs=in_specs,
        out_specs=[VMEM] * len(outs) if many else VMEM,
        input_output_aliases=alias or {},
        compiler_params=pltpu.CompilerParams(vmem_limit_bytes=limit << 20),
        cost_estimate=pl.CostEstimate(flops=flops, bytes_accessed=moved, transcendentals=0),
    )(*args)


def up(value):
    return -(-value // LANES) * LANES


def per_device(groups, hidden, norm_gain, head, reward_head, tokens, lengths):
    section = lax.axis_index("section")
    core, pair = section % 2, section // 2
    sections = lax.axis_size("section")
    spans, positions = tokens.shape
    block, width, part = head.shape[1], head.shape[0], hidden.shape[2]
    count = 3 * spans * positions // 4 // sections
    half = positions // 2
    big = (count * 7 // 9) // 16 * 16
    small = count - big
    rows = hidden[0]

    swap = [(s, s ^ 1) for s in range(sections)]
    over = [(s, s ^ 2) for s in range(sections)]
    sibling = lax.ppermute(rows, "section", swap)
    extra = lax.ppermute(rows[half:], "section", [(1, 3), (3, 1)])
    head_sibling = lax.ppermute(head, "section", swap)

    g, s0, partial = call(
        functools.partial(pick_kernel, count),
        [
            jax.ShapeDtypeStruct((big, part), BF16),
            jax.ShapeDtypeStruct((small, part), BF16),
            jax.ShapeDtypeStruct((8, up(count)), F32),
        ],
        [SMEM] + [VMEM] * 5,
        (lengths, rows, sibling, extra, norm_gain[None], reward_head[None]),
        flops=2 * count * 960 * part,
    )
    token_ids = call(
        functools.partial(token_kernel, count, big),
        jax.ShapeDtypeStruct((2 * count, 1), I32),
        [SMEM, VMEM],
        (lengths, tokens),
        flops=10**6,
    )

    def mesh_perm(move):
        pairs = []
        for s in range(sections):
            for d in range(groups):
                s2, d2 = move(s, d)
                pairs.append((s * groups + d, s2 * groups + d2))
        return pairs

    send = lambda value, perm: lax.ppermute(value, AXES, perm)
    acc_shape = jax.ShapeDtypeStruct((2 * count, 2 * block), F32)
    if groups == 8:
        perm_a = mesh_perm(lambda s, d: (s, d ^ 1) if s % 2 == 0 else (s ^ 2, d))
        perm_b = mesh_perm(lambda s, d: (s ^ 2, d) if s % 2 == 0 else (s, d ^ 1))
        perm_x = mesh_perm(lambda s, d: (s, d ^ 1))
        perm_z = {k: mesh_perm(lambda s, d, k=k: (s, d ^ (2 * k))) for k in (1, 2, 3)}
        zero = core == 0

        z = {0: g}
        a, b, c, w = {}, {}, {}, {}
        z[3] = send(g, perm_z[3])
        a3 = send(s0, perm_a)
        z[1] = send(g, perm_z[1])
        a[0] = send(g, perm_a)
        b3 = send(jnp.concatenate([s0, a3]), perm_b)
        b[0] = send(g, perm_b)
        c[0] = send(a[0], perm_b)
        w[0] = jnp.concatenate(
            [s0, jnp.where(zero, b3[:small], a3), jnp.where(zero, a3, b3[:small]), b3[small:]]
        )
        z[2] = send(z[3], perm_z[1])
        w[3] = send(w[0], perm_z[3])
        w[1] = send(w[0], perm_z[1])
        w[2] = send(w[3], perm_z[1])
        for k in (1, 3, 2):
            a[k] = send(z[k], perm_a)
            b[k] = send(z[k], perm_b)
            c[k] = send(a[k], perm_b)

        for perm in (perm_z[1], perm_z[2], perm_x):
            partial = partial + send(partial, perm)
        acc = None
        for k, parts in ((0, "zabcw"), (1, "zabcw"), (3, "zabcw"), (2, "zabw")):
            pieces = {"z": z, "a": a, "b": b, "c": c, "w": w}
            values = [pieces[p][k] for p in parts]
            first = acc is None
            acc = call(
                functools.partial(mm_kernel, k, first, parts),
                acc_shape,
                [VMEM] * (2 + (not first) + len(values)),
                (head, head_sibling) + (() if first else (acc,)) + tuple(values),
                flops=2 * 4 * count * part * 2 * block,
                alias={} if first else {2: 0},
            )
        last_c = c[2]
    else:
        partial = lax.psum(partial, "dp")
        mine = jnp.concatenate([g, s0])
        across = lax.ppermute(mine, "section", over)
        first_pair = jnp.where(pair == 0, mine, across)
        second_pair = jnp.where(pair == 0, across, mine)
        ordered = jnp.concatenate([first_pair[:big], second_pair[:big], first_pair[big:], second_pair[big:]])
        everything = lax.all_gather(ordered, "dp", axis=1, tiled=True)
        acc = jnp.concatenate(
            [jnp.dot(everything, h, preferred_element_type=F32) for h in (head, head_sibling)], axis=1
        )
        last_c = None

    other = lax.ppermute(partial, "section", over)
    sums = jnp.stack([jnp.where(pair == 0, partial, other), jnp.where(pair == 0, other, partial)])
    stats_shape = jax.ShapeDtypeStruct((8, up(2 * count)), F32)
    if last_c is not None:
        stats, _ = call(
            functools.partial(last_kernel, 2, big, width),
            [stats_shape, acc_shape],
            [VMEM] * 6,
            (head, head_sibling, acc, last_c, sums, token_ids),
            flops=2 * count * part * 2 * block,
            alias={2: 1},
        )
        stats = combine([stats] + [send(stats, perm_z[k]) for k in (1, 2, 3)])
        stats = combine(
            [stats]
            + [send(stats, mesh_perm(lambda s, d, v=v: (s ^ v[0], d ^ v[1]))) for v in ((0, 1), (2, 0), (2, 1))]
        )
    else:
        def body(head, sibling, acc_in, sums, token_ids, out, acc):
            last_kernel(2, big, width, head, sibling, acc_in, None, sums, token_ids, out, acc)

        stats, _ = call(
            body, [stats_shape, acc_shape], [VMEM] * 5, (head, head_sibling, acc, sums, token_ids), alias={2: 1}
        )
        gathered = lax.all_gather(stats, "dp")
        stats = combine([gathered[i] for i in range(groups)])
        stats = combine([stats, lax.ppermute(stats, "section", over)])
    lp = stats[2:3] - (stats[0:1] + jnp.log(stats[1:2]))
    lp = jnp.concatenate([lp, jnp.zeros((7, lp.shape[1]), F32)])
    both = lambda v, u: jnp.stack([jnp.where(core == 0, v, u), jnp.where(core == 0, u, v)])
    sums = both(sums, lax.ppermute(sums, "section", swap))
    stats = both(lp, lax.ppermute(lp, "section", swap))
    logprob, score = call(
        functools.partial(final_kernel, count, big, width),
        [jax.ShapeDtypeStruct((1, positions), F32), jax.ShapeDtypeStruct((1, 1), F32)],
        [SMEM, VMEM, VMEM],
        (lengths, sums, stats),
    )
    return (logprob, score[0])


def solution(mesh):
    groups = mesh.shape["dp"]
    return jax.shard_map(
        lambda *args: per_device(groups, *args),
        mesh=mesh,
        in_specs=(P("section", None, "dp"), P("dp"), P(None, ("section", "dp")), P("dp"), P(), P()),
        out_specs=(P("section", None), P("section")),
        check_vma=False,
    )
```

```python
import functools

import jax
import jax.numpy as jnp
from jax import lax
from jax.experimental import pallas as pl
from jax.experimental.pallas import tpu as pltpu
from jax.sharding import PartitionSpec as P

AXES = ("section", "dp")
F32 = jnp.float32
BF16 = jnp.bfloat16
I32 = jnp.int32
LANES = 128
VMEM = pl.BlockSpec(memory_space=pltpu.VMEM)
SMEM = pl.BlockSpec(memory_space=pltpu.SMEM)
ANY = pl.BlockSpec(memory_space=pl.ANY)


def row_map(lengths, pair, core, index, count):
    first, second = lengths[2 * pair], lengths[2 * pair + 1]
    other_first = lengths[2 - 2 * pair]
    j = core * count + index
    in_first = j < first
    in_second = j < first + second
    span = jnp.where(in_first, 2 * pair, jnp.where(in_second, 2 * pair + 1, 3 - 2 * pair))
    place = jnp.where(
        in_first, j, jnp.where(in_second, j - first, 2 * count - other_first + j - first - second)
    )
    return span, place


def as_rows(columns, count):
    lane = lax.broadcasted_iota(I32, (count, LANES), 1)
    wide = jnp.zeros((count, LANES), F32)
    for i, column in enumerate(columns):
        wide = jnp.where(lane == i, column, wide)
    return jnp.transpose(wide)[:8]


def as_column(rows, which):
    full = jnp.concatenate([rows, jnp.zeros((LANES - 8, rows.shape[1]), F32)], axis=0)
    return jnp.transpose(full)[:, which : which + 1]


def pick_kernel(count, lengths, rows, sibling, extra, gain, reward, head, big, small, partial, head_out, sem):
    copy = pltpu.make_async_copy(head, head_out, sem)
    copy.start()
    section = lax.axis_index("section")
    core, pair = lax.rem(section, 2), lax.div(section, 2)
    positions, half = rows.shape[0], extra.shape[0]
    index = lax.broadcasted_iota(I32, (count, 1), 0)
    span, place = row_map(lengths, pair, core, index, count)
    source = jnp.where(span == section, place, place + positions)
    source = jnp.where(span // 2 == pair, source, place + (2 * positions - (positions - half)))
    lane = lax.broadcasted_iota(I32, (count, 2 * positions + half), 1)
    pick = jnp.where(lane == source, F32(1.0), F32(0.0)).astype(BF16)
    picked = jnp.dot(pick[:, :positions], rows[...], preferred_element_type=F32)
    picked += jnp.dot(pick[:, positions : 2 * positions], sibling[...], preferred_element_type=F32)
    picked += jnp.dot(pick[:, 2 * positions :], extra[...], preferred_element_type=F32)
    scaled = (picked * gain[...].astype(F32)).astype(BF16)
    n = big.shape[0]
    big[...] = scaled[:n]
    small[...] = scaled[n:]
    squares = jnp.sum(picked * picked, axis=1, keepdims=True)
    rewards = jnp.sum(scaled.astype(F32) * reward[...].astype(F32), axis=1, keepdims=True)
    padded = partial.shape[1]
    zeros = jnp.zeros((padded - count, 1), F32)
    partial[...] = as_rows(
        [jnp.concatenate([squares, zeros]), jnp.concatenate([rewards, zeros])], padded
    )
    copy.wait()


def token_kernel(count, n, lengths, tokens, out):
    core = lax.rem(lax.axis_index("section"), 2)
    spans, positions = tokens.shape
    for pair in range(2):
        index = lax.broadcasted_iota(I32, (count, 1), 0)
        span, place = row_map(lengths, pair, core, index, count)
        lane = lax.broadcasted_iota(I32, (count, positions), 1)
        ids = jnp.zeros((count, 1), F32)
        for s in range(spans):
            hit = (lane == place) & (span == s)
            ids += jnp.sum(jnp.where(hit, tokens[s : s + 1, :].astype(F32), F32(0.0)), axis=1, keepdims=True)
        ids = ids.astype(I32)
        m = count - n
        out[pair * n : pair * n + n, :] = ids[:n]
        out[2 * n + pair * m : 2 * n + pair * m + m, :] = ids[n:]


def offsets(k, n, m):
    section, dp_index = lax.axis_index("section"), lax.axis_index("dp")
    core, pair = lax.rem(section, 2), lax.div(section, 2)
    near = jnp.bitwise_xor(dp_index, 2 * k)
    far = jnp.bitwise_xor(near, 1)
    mine = pl.ds(pl.multiple_of(pair * n, n), n)
    others = pl.ds(pl.multiple_of((1 - pair) * n, n), n)
    small_mine = pl.ds(pl.multiple_of(2 * n + pair * m, 16), m)
    small_others = pl.ds(pl.multiple_of(2 * n + (1 - pair) * m, 16), m)
    return core, near, far, mine, others, small_mine, small_others


def add(acc, rows, value, first):
    for i, part in enumerate(value):
        w = part.shape[1]
        if first:
            acc[rows, i * w : (i + 1) * w] = part
        else:
            acc[rows, i * w : (i + 1) * w] = acc[rows, i * w : (i + 1) * w] + part


def stage_kernel(stage, names, n, m, n_pass, *refs):
    refs = list(refs)
    head, sibling = refs[0], refs[1]
    first = stage == 0
    at = 2
    acc_in = None
    if not first:
        acc_in = refs[at]
        at += 1
    pieces = dict(zip(names, refs[at : at + len(names)]))
    at += len(names)
    sums = refs[at]
    at += 1
    if not first:
        received = refs[at]
        at += 1
    at += n_pass
    acc, sums_out = refs[at], refs[at + 1]
    depth = refs[2 if first else 3].shape[1]

    def times(name, k, far):
        _, near, other, _, _, _, _ = offsets(k, n, m)
        where = other if far else near
        rows = pl.ds(pl.multiple_of(where * depth, depth), depth)
        value = pieces[name][...]
        return [jnp.dot(value, h[rows, :], preferred_element_type=F32) for h in (head, sibling)]

    def plus(x, y):
        return [i + j for i, j in zip(x, y)]

    core, _, _, mine, others, small_mine, small_others = offsets(0, n, m)
    if first:
        sums_out[...] = sums[...]
        acc[2 * n :, :] = jnp.zeros((2 * m, acc.shape[1]), F32)
    else:
        sums_out[...] = sums[...] + received[...]
        acc[...] = acc_in[...]
    k = (0, 1, 3, 2)[stage]
    before = (0, 0, 1, 3)[stage]
    for c in range(2):

        @pl.when(core == c)
        def _():
            same, cross = ("a", "b") if c == 0 else ("b", "a")
            add(acc, mine, plus(times("z", k, False), times(same, k, True)), first)
            value = times(cross, k, False)
            if "c" in pieces:
                value = plus(value, times("c", before, True))
            add(acc, others, value, first)

    for name, w_k in (("w0", 0), ("w1", 1), ("w3", 3)):
        if name in pieces:
            small(acc, pieces[name], head, sibling, w_k, n, m)


def small(acc, w, head, sibling, k, n, m):
    _, near, far, _, _, mine, others = offsets(k, n, m)
    depth = w.shape[1]
    value = None
    for i, where in enumerate((near, far)):
        rows = pl.ds(pl.multiple_of(where * depth, depth), depth)
        part = [
            jnp.dot(w[2 * m * i : 2 * m * (i + 1), :], h[rows, :], preferred_element_type=F32)
            for h in (head, sibling)
        ]
        value = part if value is None else [x + y for x, y in zip(value, part)]
    add(acc, mine, [v[:m] for v in value], False)
    add(acc, others, [v[m:] for v in value], False)


def summarize(logits, squares, token_ids, bases, block, width, out):
    scale = lax.rsqrt(squares / width + 1e-05)
    logits = logits * scale
    top = jnp.max(logits, axis=1, keepdims=True)
    total = jnp.sum(jnp.exp(logits - top), axis=1, keepdims=True)
    lane = lax.broadcasted_iota(I32, (1, block), 1)
    target = jnp.zeros(top.shape, F32)
    for i, base in enumerate(bases):
        hit = (lane + base) == token_ids
        target += jnp.sum(
            jnp.where(hit, logits[:, i * block : (i + 1) * block], F32(0.0)), axis=1, keepdims=True
        )
    count, padded = logits.shape[0], out.shape[1]
    zeros = jnp.zeros((padded - count, 1), F32)
    out[...] = as_rows([jnp.concatenate([v, zeros]) for v in (top, total, target)], padded)


def last_kernel(k, n, width, head, sibling, acc_in, c, w, sums, across, token_ids, out, acc):
    count = acc_in.shape[0] // 2
    m = count - n
    block = head.shape[1]
    section, dp_index = lax.axis_index("section"), lax.axis_index("dp")
    groups = lax.axis_size("dp")
    bases = [(section * groups + dp_index) * block, ((section + 1 - 2 * lax.rem(section, 2)) * groups + dp_index) * block]
    acc[...] = acc_in[...]
    if c is not None:
        _, near, far, mine, others, _, _ = offsets(k, n, m)
        depth = c.shape[1]
        rows = pl.ds(pl.multiple_of(far * depth, depth), depth)
        for i, h in enumerate((head, sibling)):
            cols = slice(i * block, (i + 1) * block)
            acc[others, cols] = acc[others, cols] + jnp.dot(c[...], h[rows, :], preferred_element_type=F32)
        small(acc, w, head, sibling, k, n, m)
    swapped = lax.div(section, 2) == 1
    squares = [
        as_column(jnp.where(swapped, across[...], sums[...]), 0),
        as_column(jnp.where(swapped, sums[...], across[...]), 0),
    ]
    column = jnp.concatenate([squares[0][:n], squares[1][:n], squares[0][n:count], squares[1][n:count]])
    summarize(acc[...], column, token_ids[...], bases, block, width, out)


def final_kernel(count, n, width, lengths, sums, stats, out_ref, score_ref):
    section = lax.axis_index("section")
    m = count - n
    positions = out_ref.shape[1]
    where = lax.broadcasted_iota(I32, (1, positions), 1)
    logprob = jnp.zeros((1, positions), F32)
    score = jnp.zeros((1, 1), F32)
    index = lax.broadcasted_iota(I32, (count, 1), 0)
    for core in range(2):
        s = stats[core]
        lp = as_column(s, 0)
        for pair in range(2):
            value = jnp.concatenate([lp[pair * n : pair * n + n], lp[2 * n + pair * m : 2 * n + pair * m + m]])
            span, place = row_map(lengths, pair, core, index, count)
            hit = (place == where) & (span == section)
            logprob += jnp.sum(jnp.where(hit, value, F32(0.0)), axis=0, keepdims=True)
            columns = jnp.transpose(
                jnp.concatenate([sums[core, pair], jnp.zeros((LANES - 8, sums.shape[3]), F32)], axis=0)
            )[:count]
            reward = columns[:, 1:2] * lax.rsqrt(columns[:, 0:1] / width + 1e-05)
            score += jnp.sum(jnp.where(span == section, reward, F32(0.0)), axis=0, keepdims=True)
    out_ref[...] = logprob
    score_ref[...] = score / lengths[section].astype(F32)


def combine(parts):
    top = parts[0][0]
    for part in parts[1:]:
        top = jnp.maximum(top, part[0])
    total = sum(part[1] * jnp.exp(part[0] - top) for part in parts)
    target = sum(part[2] for part in parts)
    return jnp.concatenate([jnp.stack([top, total, target]), jnp.zeros((5,) + top.shape, F32)])


def call(body, outs, in_specs, args, flops=0, moved=0, alias=None, limit=32, out_specs=None, scratch=()):
    many = isinstance(outs, (list, tuple))
    return pl.pallas_call(
        body,
        out_shape=outs,
        in_specs=in_specs,
        out_specs=out_specs or ([VMEM] * len(outs) if many else VMEM),
        input_output_aliases=alias or {},
        scratch_shapes=scratch,
        compiler_params=pltpu.CompilerParams(vmem_limit_bytes=limit << 20),
        cost_estimate=pl.CostEstimate(flops=flops, bytes_accessed=moved, transcendentals=0),
    )(*args)


def up(value):
    return -(-value // LANES) * LANES


def per_device(groups, hidden, norm_gain, head, reward_head, tokens, lengths):
    section = lax.axis_index("section")
    core, pair = section % 2, section // 2
    sections = lax.axis_size("section")
    spans, positions = tokens.shape
    block, width, part = head.shape[1], head.shape[0], hidden.shape[2]
    count = 3 * spans * positions // 4 // sections
    half = positions // 2
    big = (count * 7 // 9) // 16 * 16
    small = count - big
    rows = hidden[0]

    swap = [(s, s ^ 1) for s in range(sections)]
    over = [(s, s ^ 2) for s in range(sections)]
    sibling = lax.ppermute(rows, "section", swap)
    extra = lax.ppermute(rows[half:], "section", [(1, 3), (3, 1)])

    g, s0, partial, head = call(
        functools.partial(pick_kernel, count),
        [
            jax.ShapeDtypeStruct((big, part), BF16),
            jax.ShapeDtypeStruct((small, part), BF16),
            jax.ShapeDtypeStruct((8, up(count)), F32),
            jax.ShapeDtypeStruct(head.shape, BF16),
        ],
        [SMEM] + [VMEM] * 5 + [ANY],
        (lengths, rows, sibling, extra, norm_gain[None], reward_head[None], head),
        flops=2 * count * 960 * part,
        scratch=[pltpu.SemaphoreType.DMA],
    )
    head_sibling = lax.ppermute(head, "section", swap)
    token_ids = call(
        functools.partial(token_kernel, count, big),
        jax.ShapeDtypeStruct((2 * count, 1), I32),
        [SMEM, VMEM],
        (lengths, tokens),
        flops=10**6,
    )

    def mesh_perm(move):
        pairs = []
        for s in range(sections):
            for d in range(groups):
                s2, d2 = move(s, d)
                pairs.append((s * groups + d, s2 * groups + d2))
        return pairs

    send = lambda value, perm: lax.ppermute(value, AXES, perm)
    acc_shape = jax.ShapeDtypeStruct((2 * count, 2 * block), F32)
    if groups == 8:
        perm_a = mesh_perm(lambda s, d: (s, d ^ 1) if s % 2 == 0 else (s ^ 2, d))
        perm_b = mesh_perm(lambda s, d: (s ^ 2, d) if s % 2 == 0 else (s, d ^ 1))
        perm_x = mesh_perm(lambda s, d: (s, d ^ 1))
        perm_z = {k: mesh_perm(lambda s, d, k=k: (s, d ^ (2 * k))) for k in (1, 2, 3)}
        zero = core == 0

        z1 = send(g, perm_z[1])
        z3 = send(g, perm_z[3])
        a3 = send(s0, perm_a)
        a0 = send(g, perm_a)
        b0 = send(g, perm_b)
        b3 = send(jnp.concatenate([s0, a3]), perm_b)
        c0 = send(a0, perm_b)
        w0 = jnp.concatenate(
            [s0, jnp.where(zero, b3[:small], a3), jnp.where(zero, a3, b3[:small]), b3[small:]]
        )
        z2 = send(z3, perm_z[1])

        def run(stage, acc, pieces, sums, received, passed):
            first = acc is None
            args = (head, head_sibling) + (() if first else (acc,)) + tuple(pieces.values())
            args = args + (sums,) + (() if first else (received,))
            alias = {len(args) + i: 2 + i for i in range(len(passed))}
            if not first:
                alias[2] = 0
            return call(
                functools.partial(stage_kernel, stage, tuple(pieces), big, small, len(passed)),
                [acc_shape, jax.ShapeDtypeStruct(partial.shape, F32)]
                + [jax.ShapeDtypeStruct(p.shape, p.dtype) for p in passed],
                [VMEM] * len(args) + [ANY] * len(passed),
                args + tuple(passed),
                flops=2 * len(pieces) * big * part * 2 * block,
                alias=alias,
                out_specs=[VMEM] * 2 + [ANY] * len(passed),
            )

        acc, sums, z1, w0 = run(0, None, {"z": g, "a": a0, "b": b0}, partial, None, (z1, w0))
        received = send(sums, perm_z[1])
        w1 = send(w0, perm_z[1])
        a1 = send(z1, perm_a)
        b1 = send(z1, perm_b)
        c1 = send(a1, perm_b)
        acc, sums, z3, w0 = run(1, acc, {"z": z1, "a": a1, "b": b1, "c": c0}, sums, received, (z3, w0))
        received = send(sums, perm_z[2])
        w3 = send(w0, perm_z[3])
        a_3 = send(z3, perm_a)
        b_3 = send(z3, perm_b)
        c_3 = send(a_3, perm_b)
        acc, sums, z2 = run(
            2, acc, {"z": z3, "a": a_3, "b": b_3, "c": c1, "w0": w0, "w1": w1}, sums, received, (z2,)
        )
        received = send(sums, perm_x)
        a_2 = send(z2, perm_a)
        b_2 = send(z2, perm_b)
        c_2 = send(a_2, perm_b)
        w2 = send(w3, perm_z[1])
        acc, partial = run(
            3, acc, {"z": z2, "a": a_2, "b": b_2, "c": c_3, "w3": w3}, sums, received, ()
        )
        last_c = c_2
    else:
        partial = lax.psum(partial, "dp")
        mine = jnp.concatenate([g, s0])
        across = lax.ppermute(mine, "section", over)
        first_pair = jnp.where(pair == 0, mine, across)
        second_pair = jnp.where(pair == 0, across, mine)
        ordered = jnp.concatenate([first_pair[:big], second_pair[:big], first_pair[big:], second_pair[big:]])
        everything = lax.all_gather(ordered, "dp", axis=1, tiled=True)
        acc = jnp.concatenate(
            [jnp.dot(everything, h, preferred_element_type=F32) for h in (head, head_sibling)], axis=1
        )
        last_c = None

    other = lax.ppermute(partial, "section", over)
    sums = jnp.stack([jnp.where(pair == 0, partial, other), jnp.where(pair == 0, other, partial)])
    stats_shape = jax.ShapeDtypeStruct((8, up(2 * count)), F32)
    if last_c is not None:
        stats, _ = call(
            functools.partial(last_kernel, 2, big, width),
            [stats_shape, acc_shape],
            [VMEM] * 8,
            (head, head_sibling, acc, last_c, w2, partial, other, token_ids),
            flops=2 * count * part * 2 * block,
            alias={2: 1},
        )
        stats = combine([stats] + [send(stats, perm_z[k]) for k in (1, 2, 3)])
        stats = combine(
            [stats]
            + [send(stats, mesh_perm(lambda s, d, v=v: (s ^ v[0], d ^ v[1]))) for v in ((0, 1), (2, 0), (2, 1))]
        )
    else:
        def body(head, sibling, acc_in, sums, across, token_ids, out, acc):
            last_kernel(2, big, width, head, sibling, acc_in, None, None, sums, across, token_ids, out, acc)

        stats, _ = call(
            body,
            [stats_shape, acc_shape],
            [VMEM] * 6,
            (head, head_sibling, acc, partial, other, token_ids),
            alias={2: 1},
        )
        gathered = lax.all_gather(stats, "dp")
        stats = combine([gathered[i] for i in range(groups)])
        stats = combine([stats, lax.ppermute(stats, "section", over)])
    lp = stats[2:3] - (stats[0:1] + jnp.log(stats[1:2]))
    lp = jnp.concatenate([lp, jnp.zeros((7, lp.shape[1]), F32)])
    both = lambda v, u: jnp.stack([jnp.where(core == 0, v, u), jnp.where(core == 0, u, v)])
    sums = both(sums, lax.ppermute(sums, "section", swap))
    stats = both(lp, lax.ppermute(lp, "section", swap))
    logprob, score = call(
        functools.partial(final_kernel, count, big, width),
        [jax.ShapeDtypeStruct((1, positions), F32), jax.ShapeDtypeStruct((1, 1), F32)],
        [SMEM, VMEM, VMEM],
        (lengths, sums, stats),
    )
    return (logprob, score[0])


def solution(mesh):
    groups = mesh.shape["dp"]
    return jax.shard_map(
        lambda *args: per_device(groups, *args),
        mesh=mesh,
        in_specs=(P("section", None, "dp"), P("dp"), P(None, ("section", "dp")), P("dp"), P(), P()),
        out_specs=(P("section", None), P("section")),
        check_vma=False,
    )
```

```python
import functools

import jax
import jax.numpy as jnp
from jax import lax
from jax.experimental import pallas as pl
from jax.experimental.pallas import tpu as pltpu
from jax.sharding import PartitionSpec as P

AXES = ("section", "dp")
F32 = jnp.float32
BF16 = jnp.bfloat16
I32 = jnp.int32
LANES = 128
VMEM = pl.BlockSpec(memory_space=pltpu.VMEM)
SMEM = pl.BlockSpec(memory_space=pltpu.SMEM)
ANY = pl.BlockSpec(memory_space=pl.ANY)
HBM = pl.BlockSpec(memory_space=pltpu.HBM)


def row_map(lengths, pair, core, index, count):
    first, second = lengths[2 * pair], lengths[2 * pair + 1]
    other_first = lengths[2 - 2 * pair]
    j = core * count + index
    in_first = j < first
    in_second = j < first + second
    span = jnp.where(in_first, 2 * pair, jnp.where(in_second, 2 * pair + 1, 3 - 2 * pair))
    place = jnp.where(
        in_first, j, jnp.where(in_second, j - first, 2 * count - other_first + j - first - second)
    )
    return span, place


def as_rows(columns, count):
    lane = lax.broadcasted_iota(I32, (count, LANES), 1)
    wide = jnp.zeros((count, LANES), F32)
    for i, column in enumerate(columns):
        wide = jnp.where(lane == i, column, wide)
    return jnp.transpose(wide)[:8]


def as_column(rows, which):
    full = jnp.concatenate([rows, jnp.zeros((LANES - 8, rows.shape[1]), F32)], axis=0)
    return jnp.transpose(full)[:, which : which + 1]


def pick_kernel(count, lengths, rows, sibling, extra, gain, reward, head, full, big, partial, head_out, sem):
    copy = pltpu.make_async_copy(head, head_out, sem)
    copy.start()
    section = lax.axis_index("section")
    core, pair = lax.rem(section, 2), lax.div(section, 2)
    positions, half = rows.shape[0], extra.shape[0]
    index = lax.broadcasted_iota(I32, (count, 1), 0)
    span, place = row_map(lengths, pair, core, index, count)
    source = jnp.where(span == section, place, place + positions)
    source = jnp.where(span // 2 == pair, source, place + (2 * positions - (positions - half)))
    lane = lax.broadcasted_iota(I32, (count, 2 * positions + half), 1)
    pick = jnp.where(lane == source, F32(1.0), F32(0.0)).astype(BF16)
    picked = jnp.dot(pick[:, :positions], rows[...], preferred_element_type=F32)
    picked += jnp.dot(pick[:, positions : 2 * positions], sibling[...], preferred_element_type=F32)
    picked += jnp.dot(pick[:, 2 * positions :], extra[...], preferred_element_type=F32)
    scaled = (picked * gain[...].astype(F32)).astype(BF16)
    full[...] = scaled
    big[...] = scaled[: big.shape[0]]
    squares = jnp.sum(picked * picked, axis=1, keepdims=True)
    rewards = jnp.sum(scaled.astype(F32) * reward[...].astype(F32), axis=1, keepdims=True)
    padded = partial.shape[1]
    zeros = jnp.zeros((padded - count, 1), F32)
    partial[...] = as_rows(
        [jnp.concatenate([squares, zeros]), jnp.concatenate([rewards, zeros])], padded
    )
    copy.wait()


def token_kernel(count, lengths, tokens, out):
    core = lax.rem(lax.axis_index("section"), 2)
    spans, positions = tokens.shape
    for pair in range(2):
        index = lax.broadcasted_iota(I32, (count, 1), 0)
        span, place = row_map(lengths, pair, core, index, count)
        lane = lax.broadcasted_iota(I32, (count, positions), 1)
        ids = jnp.zeros((count, 1), F32)
        for s in range(spans):
            hit = (lane == place) & (span == s)
            ids += jnp.sum(jnp.where(hit, tokens[s : s + 1, :].astype(F32), F32(0.0)), axis=1, keepdims=True)
        out[pair * count : pair * count + count, :] = ids.astype(I32)


def here():
    section = lax.axis_index("section")
    return section, lax.rem(section, 2), lax.div(section, 2)


def blocks(count):
    _, _, pair = here()
    return pl.multiple_of(pair * count, 16), pl.multiple_of((1 - pair) * count, 16)


def weights(head, sibling, depth, k, far):
    dp_index = lax.axis_index("dp")
    where = jnp.bitwise_xor(dp_index, 2 * k + (1 if far else 0))
    rows = pl.ds(pl.multiple_of(where * depth, depth), depth)
    return head[rows, :], sibling[rows, :]


def products(terms):
    value = jnp.concatenate([t[0] for t in terms], axis=1) if len(terms) > 1 else terms[0][0]
    out = []
    for side in range(2):
        w = [t[1][side] for t in terms]
        w = jnp.concatenate(w, axis=0) if len(w) > 1 else w[0]
        out.append(jnp.dot(value, w, preferred_element_type=F32))
    return jnp.concatenate(out, axis=1)


def small_terms(w, head, sibling, k):
    m2 = w.shape[0] // 2
    depth = w.shape[1]
    return products(
        [(w[:m2, :], weights(head, sibling, depth, k, False)), (w[m2:, :], weights(head, sibling, depth, k, True))]
    )


def first_kernel(n, head, sibling, z, a, b, c, sums, z1, z3, acc, sums_out, w0, z1_out, z3_out):
    count, depth = z.shape
    m = count - n
    _, core, _ = here()
    mine, others = blocks(count)
    near = weights(head, sibling, depth, 0, False)
    far = weights(head, sibling, depth, 0, True)
    w0[:m, :] = z[n:, :]
    w0[3 * m :, :] = c[n:, :]
    for which, same, cross in ((0, a, b), (1, b, a)):

        @pl.when(core == which)
        def _():
            acc[pl.ds(mine, count), :] = products([(z[...], near), (same[...], far)])
            acc[pl.ds(others, count), :] = products([(cross[...], near), (c[...], far)])
            w0[m : 2 * m, :] = cross[n:, :]
            w0[2 * m : 3 * m, :] = same[n:, :]

    sums_out[...] = sums[...]
    z1_out[...] = z1[...]
    z3_out[...] = z3[...]


def stage_kernel(k, n_small, n_pass, *refs):
    refs = list(refs)
    head, sibling, acc_in, z, a, b, c, sums, received = refs[:9]
    smalls = refs[9 : 9 + n_small]
    passed = refs[9 + n_small : 9 + n_small + n_pass]
    acc, sums_out = refs[9 + n_small + n_pass : 11 + n_small + n_pass]
    outs = refs[11 + n_small + n_pass :]
    n, depth = z.shape
    count = acc.shape[0] // 2
    m = count - n
    _, core, _ = here()
    mine, others = blocks(count)
    near = weights(head, sibling, depth, k, False)
    far = weights(head, sibling, depth, k, True)
    for which, same, cross in ((0, a, b), (1, b, a)):

        @pl.when(core == which)
        def _():
            rows = pl.ds(mine, n)
            acc[rows, :] = acc_in[rows, :] + products([(z[...], near), (same[...], far)])
            rows = pl.ds(others, n)
            acc[rows, :] = acc_in[rows, :] + products([(cross[...], near), (c[...], far)])

    for i, base in enumerate((mine, others)):
        rows = pl.ds(pl.multiple_of(base + n, 16), m)
        value = acc_in[rows, :]
        acc[rows, :] = value
    for w, w_k in zip(smalls, (1, 3)):
        value = small_terms(w, head, sibling, w_k)
        for i, base in enumerate((mine, others)):
            rows = pl.ds(pl.multiple_of(base + n, 16), m)
            acc[rows, :] = acc[rows, :] + value[i * m : (i + 1) * m]
    sums_out[...] = sums[...] + received[...]
    for out, value in zip(outs, passed):
        out[...] = value[...]


def gate_kernel(value, after, out):
    out[...] = value[...]


def column_ids(block):
    section, core, _ = here()
    dp_index, groups = lax.axis_index("dp"), lax.axis_size("dp")
    lane = lax.broadcasted_iota(I32, (1, block), 1)
    own = (section * groups + dp_index) * block
    other = ((section + 1 - 2 * core) * groups + dp_index) * block
    return jnp.concatenate([lane + own, lane + other], axis=1)


def summary(logits, squares, token_ids, ids, width):
    logits = logits * lax.rsqrt(squares / width + 1e-05)
    top = jnp.max(logits, axis=1, keepdims=True)
    total = jnp.sum(jnp.exp(logits - top), axis=1, keepdims=True)
    target = jnp.sum(jnp.where(ids == token_ids, logits, F32(0.0)), axis=1, keepdims=True)
    lane = lax.broadcasted_iota(I32, (logits.shape[0], LANES), 1)
    return jnp.where(lane == 0, top, jnp.where(lane == 1, total, jnp.where(lane == 2, target, F32(0.0))))


def own_kernel(k, width, head, sibling, acc_in, z, a, b, w, sums, received, token_ids, acc, sums_out, own):
    n, depth = z.shape
    count = acc_in.shape[0] // 2
    m = count - n
    _, core, _ = here()
    mine, others = blocks(count)
    near = weights(head, sibling, depth, k, False)
    far = weights(head, sibling, depth, k, True)
    total = sums[...] + received[...]
    sums_out[...] = total
    scale = as_column(total, 0)
    ids = column_ids(head.shape[1])
    for which, same, cross in ((0, a, b), (1, b, a)):

        @pl.when(core == which)
        def _():
            rows = pl.ds(mine, n)
            logits = acc_in[rows, :] + products([(z[...], near), (same[...], far)])
            own[...] = summary(logits, scale[:n], token_ids[rows, :], ids, width)
            acc[:n, :] = acc_in[pl.ds(others, n), :] + products([(cross[...], near)])

    value = small_terms(w, head, sibling, 3)
    for i, base in enumerate((mine, others)):
        rows = pl.ds(pl.multiple_of(base + n, 16), m)
        acc[n + i * m : n + (i + 1) * m, :] = acc_in[rows, :] + value[i * m : (i + 1) * m]


def last_kernel(k, width, head, sibling, acc, c, w, own, sums, across, token_ids, out, wide):
    n, depth = c.shape
    count = token_ids.shape[0] // 2
    m = count - n
    mine, others = blocks(count)
    ids = column_ids(head.shape[1])
    scale, scale_across = as_column(sums[...], 0), as_column(across[...], 0)
    wide[2 * count :, :] = jnp.zeros((wide.shape[0] - 2 * count, LANES), F32)
    wide[pl.ds(mine, n), :] = own[...]
    logits = acc[:n, :] + products([(c[...], weights(head, sibling, depth, k, True))])
    rows = pl.ds(others, n)
    wide[rows, :] = summary(logits, scale_across[:n], token_ids[rows, :], ids, width)
    value = acc[n:, :] + small_terms(w, head, sibling, k)
    for i, (base, squares) in enumerate(((mine, scale), (others, scale_across))):
        rows = pl.ds(pl.multiple_of(base + n, 16), m)
        wide[rows, :] = summary(value[i * m : (i + 1) * m], squares[n:count], token_ids[rows, :], ids, width)
    out[...] = jnp.transpose(wide[...])[:8]


def whole_kernel(width, acc, sums, token_ids, out):
    count = acc.shape[0] // 2
    ids = column_ids(acc.shape[1] // 2)
    squares = jnp.concatenate([as_column(sums[0], 0)[:count], as_column(sums[1], 0)[:count]])
    wide = summary(acc[...], squares, token_ids[...], ids, width)
    wide = jnp.concatenate([wide, jnp.zeros((out.shape[1] - 2 * count, LANES), F32)])
    out[...] = jnp.transpose(wide)[:8]


def final_kernel(count, width, lengths, sums, stats, out_ref, score_ref):
    section = lax.axis_index("section")
    positions = out_ref.shape[1]
    where = lax.broadcasted_iota(I32, (1, positions), 1)
    logprob = jnp.zeros((1, positions), F32)
    score = jnp.zeros((1, 1), F32)
    index = lax.broadcasted_iota(I32, (count, 1), 0)
    for core in range(2):
        s = stats[core]
        lp = as_column(s, 0)
        for pair in range(2):
            value = lp[pair * count : pair * count + count]
            span, place = row_map(lengths, pair, core, index, count)
            hit = (place == where) & (span == section)
            logprob += jnp.sum(jnp.where(hit, value, F32(0.0)), axis=0, keepdims=True)
            columns = jnp.transpose(
                jnp.concatenate([sums[core, pair], jnp.zeros((LANES - 8, sums.shape[3]), F32)], axis=0)
            )[:count]
            reward = columns[:, 1:2] * lax.rsqrt(columns[:, 0:1] / width + 1e-05)
            score += jnp.sum(jnp.where(span == section, reward, F32(0.0)), axis=0, keepdims=True)
    out_ref[...] = logprob
    score_ref[...] = score / lengths[section].astype(F32)


def combine(parts):
    top = parts[0][0]
    for part in parts[1:]:
        top = jnp.maximum(top, part[0])
    total = sum(part[1] * jnp.exp(part[0] - top) for part in parts)
    target = sum(part[2] for part in parts)
    return jnp.concatenate([jnp.stack([top, total, target]), jnp.zeros((5,) + top.shape, F32)])


def call(body, outs, in_specs, args, limit=16, scratch=()):
    many = isinstance(outs, (list, tuple))
    return pl.pallas_call(
        body,
        out_shape=outs,
        in_specs=in_specs,
        out_specs=[VMEM] * len(outs) if many else VMEM,
        scratch_shapes=scratch,
        compiler_params=pltpu.CompilerParams(vmem_limit_bytes=limit << 20),
    )(*args)


def up(value):
    return -(-value // LANES) * LANES


def per_device(groups, hidden, norm_gain, head, reward_head, tokens, lengths):
    section = lax.axis_index("section")
    core, pair = section % 2, section // 2
    sections = lax.axis_size("section")
    spans, positions = tokens.shape
    block, width, part = head.shape[1], head.shape[0], hidden.shape[2]
    count = 3 * spans * positions // 4 // sections
    half = positions // 2
    big = (count * 7 // 9) // 16 * 16
    small = count - big
    rows = hidden[0]

    swap = [(s, s ^ 1) for s in range(sections)]
    over = [(s, s ^ 2) for s in range(sections)]
    sibling = lax.ppermute(rows, "section", swap)
    extra = lax.ppermute(rows[half:], "section", [(1, 3), (3, 1)])

    full, g, partial, head = call(
        functools.partial(pick_kernel, count),
        [
            jax.ShapeDtypeStruct((count, part), BF16),
            jax.ShapeDtypeStruct((big, part), BF16),
            jax.ShapeDtypeStruct((8, up(count)), F32),
            jax.ShapeDtypeStruct(head.shape, BF16),
        ],
        [SMEM] + [VMEM] * 5 + [HBM],
        (lengths, rows, sibling, extra, norm_gain[None], reward_head[None], head),
        scratch=[pltpu.SemaphoreType.DMA],
    )
    head_sibling = lax.ppermute(head, "section", swap)
    token_ids = call(
        functools.partial(token_kernel, count), jax.ShapeDtypeStruct((2 * count, 1), I32), [SMEM, VMEM], (lengths, tokens)
    )

    def mesh_perm(move):
        pairs = []
        for s in range(sections):
            for d in range(groups):
                s2, d2 = move(s, d)
                pairs.append((s * groups + d, s2 * groups + d2))
        return pairs

    send = lambda value, perm: lax.ppermute(value, AXES, perm)
    like = lambda v: jax.ShapeDtypeStruct(v.shape, v.dtype)
    acc_shape = jax.ShapeDtypeStruct((2 * count, 2 * block), F32)
    stats_shape = jax.ShapeDtypeStruct((8, up(2 * count)), F32)
    if groups == 8:
        perm_a = mesh_perm(lambda s, d: (s, d ^ 1) if s % 2 == 0 else (s ^ 2, d))
        perm_b = mesh_perm(lambda s, d: (s ^ 2, d) if s % 2 == 0 else (s, d ^ 1))
        perm_x = mesh_perm(lambda s, d: (s, d ^ 1))
        perm_z = {k: mesh_perm(lambda s, d, k=k: (s, d ^ (2 * k))) for k in (1, 2, 3)}

        def gate(value, after):
            return call(gate_kernel, like(value), [VMEM, ANY], (value, after))

        def stage(k, acc, pieces, sums, received, smalls, passed):
            args = (head, head_sibling, acc) + pieces + (sums, received) + smalls + passed
            return call(
                functools.partial(stage_kernel, k, len(smalls), len(passed)),
                [acc_shape, like(sums)] + [like(p) for p in passed],
                [VMEM] * len(args),
                args,
            )

        z1 = send(g, perm_z[1])
        z3 = send(g, perm_z[3])
        a0 = send(full, perm_a)
        b0 = send(full, perm_b)
        c0 = send(a0, perm_b)
        z1 = gate(z1, b0)
        a1 = send(z1, perm_a)
        acc, sums, w0, z1, z3 = call(
            functools.partial(first_kernel, big),
            [acc_shape, like(partial), jax.ShapeDtypeStruct((4 * small, part), BF16), like(z1), like(z3)],
            [VMEM] * 9,
            (head, head_sibling, full, a0, b0, c0, partial, z1, z3),
        )
        received = send(sums, perm_z[1])
        b1 = send(z1, perm_b)
        z2 = send(z3, perm_z[1])
        w3 = send(w0, perm_z[3])
        c1 = send(a1, perm_b)
        z3 = gate(z3, b1)
        a3 = send(z3, perm_a)
        acc, sums, z3, w0 = stage(1, acc, (z1, a1, b1, c1), sums, received, (), (z3, w0))
        received = send(sums, perm_z[2])
        b3 = send(z3, perm_b)
        w1 = send(w0, perm_z[1])
        c3 = send(a3, perm_b)
        z2 = gate(z2, b3)
        a2 = send(z2, perm_a)
        acc, sums, z2, w3 = stage(3, acc, (z3, a3, b3, c3), sums, received, (w1,), (z2, w3))
        received = send(sums, perm_x)
        b2 = send(z2, perm_b)
        w2 = send(w3, perm_z[1])
        c2 = send(a2, perm_b)
        acc, sums, own = call(
            functools.partial(own_kernel, 2, width),
            [jax.ShapeDtypeStruct((big + 2 * small, 2 * block), F32), like(sums), jax.ShapeDtypeStruct((big, LANES), F32)],
            [VMEM] * 10,
            (head, head_sibling, acc, z2, a2, b2, w3, sums, received, token_ids),
        )
        across = lax.ppermute(sums, "section", over)
        stats = call(
            functools.partial(last_kernel, 2, width),
            stats_shape,
            [VMEM] * 9,
            (head, head_sibling, acc, c2, w2, own, sums, across, token_ids),
            scratch=[pltpu.VMEM((up(2 * count), LANES), F32)],
        )
        stats = combine([stats] + [send(stats, perm_z[k]) for k in (1, 2, 3)])
        stats = combine(
            [stats]
            + [send(stats, mesh_perm(lambda s, d, v=v: (s ^ v[0], d ^ v[1]))) for v in ((0, 1), (2, 0), (2, 1))]
        )
    else:
        sums = lax.psum(partial, "dp")
        across = lax.ppermute(sums, "section", over)
    all_sums = jnp.stack([jnp.where(pair == 0, sums, across), jnp.where(pair == 0, across, sums)])
    if groups != 8:
        other = lax.ppermute(full, "section", over)
        ordered = jnp.concatenate([jnp.where(pair == 0, full, other), jnp.where(pair == 0, other, full)])
        everything = lax.all_gather(ordered, "dp", axis=1, tiled=True)
        acc = jnp.concatenate(
            [jnp.dot(everything, h, preferred_element_type=F32) for h in (head, head_sibling)], axis=1
        )
        stats = call(functools.partial(whole_kernel, width), stats_shape, [VMEM] * 3, (acc, all_sums, token_ids))
        gathered = lax.all_gather(stats, "dp")
        stats = combine([gathered[i] for i in range(groups)])
        stats = combine([stats, lax.ppermute(stats, "section", over)])
    lp = stats[2:3] - (stats[0:1] + jnp.log(stats[1:2]))
    lp = jnp.concatenate([lp, jnp.zeros((7, lp.shape[1]), F32)])
    both = lambda v, u: jnp.stack([jnp.where(core == 0, v, u), jnp.where(core == 0, u, v)])
    all_sums = both(all_sums, lax.ppermute(all_sums, "section", swap))
    stats = both(lp, lax.ppermute(lp, "section", swap))
    logprob, score = call(
        functools.partial(final_kernel, count, width),
        [jax.ShapeDtypeStruct((1, positions), F32), jax.ShapeDtypeStruct((1, 1), F32)],
        [SMEM, VMEM, VMEM],
        (lengths, all_sums, stats),
    )
    return (logprob, score[0])


def solution(mesh):
    groups = mesh.shape["dp"]
    return jax.shard_map(
        lambda *args: per_device(groups, *args),
        mesh=mesh,
        in_specs=(P("section", None, "dp"), P("dp"), P(None, ("section", "dp")), P("dp"), P(), P()),
        out_specs=(P("section", None), P("section")),
        check_vma=False,
    )
```

```python
import functools

import jax
import jax.numpy as jnp
from jax import lax
from jax.experimental import pallas as pl
from jax.experimental.pallas import tpu as pltpu
from jax.sharding import PartitionSpec as P

AXES = ("section", "dp")
F32 = jnp.float32
BF16 = jnp.bfloat16
I32 = jnp.int32
LANES = 128
VMEM = pl.BlockSpec(memory_space=pltpu.VMEM)
SMEM = pl.BlockSpec(memory_space=pltpu.SMEM)
ANY = pl.BlockSpec(memory_space=pl.ANY)
HBM = pl.BlockSpec(memory_space=pltpu.HBM)


def row_map(lengths, pair, core, index, count):
    first, second = lengths[2 * pair], lengths[2 * pair + 1]
    other_first = lengths[2 - 2 * pair]
    j = core * count + index
    in_first = j < first
    in_second = j < first + second
    span = jnp.where(in_first, 2 * pair, jnp.where(in_second, 2 * pair + 1, 3 - 2 * pair))
    place = jnp.where(
        in_first, j, jnp.where(in_second, j - first, 2 * count - other_first + j - first - second)
    )
    return span, place


def as_rows(columns, count):
    lane = lax.broadcasted_iota(I32, (count, LANES), 1)
    wide = jnp.zeros((count, LANES), F32)
    for i, column in enumerate(columns):
        wide = jnp.where(lane == i, column, wide)
    return jnp.transpose(wide)[:8]


def as_column(rows, which):
    full = jnp.concatenate([rows, jnp.zeros((LANES - 8, rows.shape[1]), F32)], axis=0)
    return jnp.transpose(full)[:, which : which + 1]


def sum_kernel(rows, gain, reward, lengths, out):
    value = rows[...].astype(F32)
    scaled = (value * gain[...].astype(F32)).astype(BF16).astype(F32)
    squares = jnp.sum(value * value, axis=1, keepdims=True)
    rewards = jnp.sum(scaled * reward[...].astype(F32), axis=1, keepdims=True)
    out[...] = as_rows([squares, rewards], rows.shape[0])


def pick_kernel(count, lengths, rows, sibling, extra, gain, sums, received, full, big, sums_out):
    section = lax.axis_index("section")
    core, pair = lax.rem(section, 2), lax.div(section, 2)
    positions, half = rows.shape[0], extra.shape[0]
    index = lax.broadcasted_iota(I32, (count, 1), 0)
    span, place = row_map(lengths, pair, core, index, count)
    source = jnp.where(span == section, place, place + positions)
    source = jnp.where(span // 2 == pair, source, place + (2 * positions - (positions - half)))
    lane = lax.broadcasted_iota(I32, (count, 2 * positions + half), 1)
    pick = jnp.where(lane == source, F32(1.0), F32(0.0)).astype(BF16)
    picked = jnp.dot(pick[:, :positions], rows[...], preferred_element_type=F32)
    picked += jnp.dot(pick[:, positions : 2 * positions], sibling[...], preferred_element_type=F32)
    picked += jnp.dot(pick[:, 2 * positions :], extra[...], preferred_element_type=F32)
    scaled = (picked * gain[...].astype(F32)).astype(BF16)
    full[...] = scaled
    big[...] = scaled[: big.shape[0]]
    sums_out[...] = sums[...] + received[...]


def row_kernel(count, width, lengths, tokens, s0, s1, s2, s3, ids, scales):
    section, core, _ = here()
    spans, positions = tokens.shape
    by_move = (s0, s1, s2, s3)
    for pair in range(2):
        index = lax.broadcasted_iota(I32, (count, 1), 0)
        span, place = row_map(lengths, pair, core, index, count)
        lane = lax.broadcasted_iota(I32, (count, positions), 1)
        found = jnp.zeros((count, positions), F32)
        squares = jnp.zeros((count, positions), F32)
        for s in range(spans):
            found = jnp.where(span == s, tokens[s : s + 1, :].astype(F32), found)
        for move in range(spans):
            squares = jnp.where(span == jnp.bitwise_xor(section, move), by_move[move][0:1, :], squares)
        hit = lane == place
        found = jnp.sum(jnp.where(hit, found, F32(0.0)), axis=1, keepdims=True)
        squares = jnp.sum(jnp.where(hit, squares, F32(0.0)), axis=1, keepdims=True)
        ids[pair * count : pair * count + count, :] = found.astype(I32)
        scales[pair * count : pair * count + count, :] = lax.rsqrt(squares / width + 1e-05)


def here():
    section = lax.axis_index("section")
    return section, lax.rem(section, 2), lax.div(section, 2)


def blocks(count):
    _, _, pair = here()
    return pl.multiple_of(pair * count, 16), pl.multiple_of((1 - pair) * count, 16)


def weights(head, sibling, depth, k, far):
    dp_index = lax.axis_index("dp")
    where = jnp.bitwise_xor(dp_index, 2 * k + (1 if far else 0))
    rows = pl.ds(pl.multiple_of(where * depth, depth), depth)
    return head[rows, :], sibling[rows, :]


def products(terms):
    value = jnp.concatenate([t[0] for t in terms], axis=1) if len(terms) > 1 else terms[0][0]
    out = []
    for side in range(2):
        w = [t[1][side] for t in terms]
        w = jnp.concatenate(w, axis=0) if len(w) > 1 else w[0]
        out.append(jnp.dot(value, w, preferred_element_type=F32))
    return jnp.concatenate(out, axis=1)


def small_terms(w, head, sibling, k):
    m2 = w.shape[0] // 2
    depth = w.shape[1]
    return products(
        [(w[:m2, :], weights(head, sibling, depth, k, False)), (w[m2:, :], weights(head, sibling, depth, k, True))]
    )


def first_kernel(n, head, sibling, z, a, b, c, ids, scales, z1, z3, acc, ids_out, scales_out, w0, z1_out, z3_out):
    count, depth = z.shape
    m = count - n
    _, core, _ = here()
    mine, others = blocks(count)
    near = weights(head, sibling, depth, 0, False)
    far = weights(head, sibling, depth, 0, True)
    w0[:m, :] = z[n:, :]
    w0[3 * m :, :] = c[n:, :]
    for which, same, cross in ((0, a, b), (1, b, a)):

        @pl.when(core == which)
        def _():
            acc[pl.ds(mine, count), :] = products([(z[...], near), (same[...], far)])
            acc[pl.ds(others, count), :] = products([(cross[...], near), (c[...], far)])
            w0[m : 2 * m, :] = cross[n:, :]
            w0[2 * m : 3 * m, :] = same[n:, :]

    ids_out[...] = ids[...]
    scales_out[...] = scales[...]
    z1_out[...] = z1[...]
    z3_out[...] = z3[...]


def stage_kernel(k, small_k, n_pass, *refs):
    refs = list(refs)
    n_small = len(small_k)
    head, sibling, acc_in, z, a, b, c = refs[:7]
    smalls = refs[7 : 7 + n_small]
    passed = refs[7 + n_small : 7 + n_small + n_pass]
    acc = refs[7 + n_small + n_pass]
    outs = refs[8 + n_small + n_pass :]
    n, depth = z.shape
    count = acc.shape[0] // 2
    m = count - n
    _, core, _ = here()
    mine, others = blocks(count)
    near = weights(head, sibling, depth, k, False)
    far = weights(head, sibling, depth, k, True)
    for which, same, cross in ((0, a, b), (1, b, a)):

        @pl.when(core == which)
        def _():
            rows = pl.ds(mine, n)
            acc[rows, :] = acc_in[rows, :] + products([(z[...], near), (same[...], far)])
            rows = pl.ds(others, n)
            acc[rows, :] = acc_in[rows, :] + products([(cross[...], near), (c[...], far)])

    values = [small_terms(w, head, sibling, w_k) for w, w_k in zip(smalls, small_k)]
    for i, base in enumerate((mine, others)):
        rows = pl.ds(pl.multiple_of(base + n, 16), m)
        value = acc_in[rows, :]
        for v in values:
            value = value + v[i * m : (i + 1) * m]
        acc[rows, :] = value
    for out, value in zip(outs, passed):
        out[...] = value[...]


def gate_kernel(value, *refs):
    refs[-1][...] = value[...]


def column_ids(block):
    section, core, _ = here()
    dp_index, groups = lax.axis_index("dp"), lax.axis_size("dp")
    lane = lax.broadcasted_iota(I32, (1, block), 1)
    own = (section * groups + dp_index) * block
    other = ((section + 1 - 2 * core) * groups + dp_index) * block
    return jnp.concatenate([lane + own, lane + other], axis=1)


def summary(logits, scale, token_ids, ids):
    logits = logits * scale
    top = jnp.max(logits, axis=1, keepdims=True)
    total = jnp.sum(jnp.exp(logits - top), axis=1, keepdims=True)
    target = jnp.sum(jnp.where(ids == token_ids, logits, F32(0.0)), axis=1, keepdims=True)
    lane = lax.broadcasted_iota(I32, (logits.shape[0], LANES), 1)
    return jnp.where(lane == 0, top, jnp.where(lane == 1, total, jnp.where(lane == 2, target, F32(0.0))))


def own_kernel(k, head, sibling, acc_in, z, a, b, w, token_ids, scales, left, far_out, wide):
    n, depth = z.shape
    count = acc_in.shape[0] // 2
    m = count - n
    _, core, _ = here()
    mine, others = blocks(count)
    near = weights(head, sibling, depth, k, False)
    far = weights(head, sibling, depth, k, True)
    block = head.shape[1]
    far_out[:, :block] = far[0]
    far_out[:, block:] = far[1]
    ids = column_ids(block)
    wide[...] = jnp.zeros(wide.shape, F32)
    for which, same, cross in ((0, a, b), (1, b, a)):

        @pl.when(core == which)
        def _():
            rows = pl.ds(mine, n)
            logits = acc_in[rows, :] + products([(z[...], near), (same[...], far)])
            wide[rows, :] = summary(logits, scales[rows, :], token_ids[rows, :], ids)
            left[...] = acc_in[pl.ds(others, n), :] + products([(cross[...], near)])

    value = small_terms(w, head, sibling, k)
    for i, base in enumerate((mine, others)):
        rows = pl.ds(pl.multiple_of(base + n, 16), m)
        logits = acc_in[rows, :] + value[i * m : (i + 1) * m]
        wide[rows, :] = summary(logits, scales[rows, :], token_ids[rows, :], ids)


def last_kernel(far, left, c, wide_in, token_ids, scales, out, wide):
    n = c.shape[0]
    count = token_ids.shape[0] // 2
    _, others = blocks(count)
    ids = column_ids(far.shape[1] // 2)
    wide[...] = wide_in[...]
    logits = left[...] + jnp.dot(c[...], far[...], preferred_element_type=F32)
    rows = pl.ds(others, n)
    wide[rows, :] = summary(logits, scales[rows, :], token_ids[rows, :], ids)
    out[...] = jnp.transpose(wide[...])[:8]


def whole_kernel(acc, token_ids, scales, out):
    count = acc.shape[0] // 2
    ids = column_ids(acc.shape[1] // 2)
    wide = summary(acc[...], scales[...], token_ids[...], ids)
    wide = jnp.concatenate([wide, jnp.zeros((out.shape[1] - 2 * count, LANES), F32)])
    out[...] = jnp.transpose(wide)[:8]


def final_kernel(count, width, lengths, sums, stats, out_ref, score_ref):
    section = lax.axis_index("section")
    positions = out_ref.shape[1]
    where = lax.broadcasted_iota(I32, (1, positions), 1)
    logprob = jnp.zeros((1, positions), F32)
    index = lax.broadcasted_iota(I32, (count, 1), 0)
    for core in range(2):
        lp = as_column(stats[core], 0)
        for pair in range(2):
            value = lp[pair * count : pair * count + count]
            span, place = row_map(lengths, pair, core, index, count)
            hit = (place == where) & (span == section)
            logprob += jnp.sum(jnp.where(hit, value, F32(0.0)), axis=0, keepdims=True)
    out_ref[...] = logprob
    length = lengths[section]
    reward = sums[1:2, :] * lax.rsqrt(sums[0:1, :] / width + 1e-05)
    score = jnp.sum(jnp.where(where < length, reward, F32(0.0)), axis=1, keepdims=True)
    score_ref[...] = score / length.astype(F32)


def combine(parts):
    top = parts[0][0]
    for part in parts[1:]:
        top = jnp.maximum(top, part[0])
    total = sum(part[1] * jnp.exp(part[0] - top) for part in parts)
    target = sum(part[2] for part in parts)
    return jnp.concatenate([jnp.stack([top, total, target]), jnp.zeros((5,) + top.shape, F32)])


def call(body, outs, in_specs, args, limit=16, scratch=()):
    many = isinstance(outs, (list, tuple))
    return pl.pallas_call(
        body,
        out_shape=outs,
        in_specs=in_specs,
        out_specs=[VMEM] * len(outs) if many else VMEM,
        scratch_shapes=scratch,
        compiler_params=pltpu.CompilerParams(vmem_limit_bytes=limit << 20),
    )(*args)


def up(value):
    return -(-value // LANES) * LANES


def per_device(groups, hidden, norm_gain, head, reward_head, tokens, lengths):
    section = lax.axis_index("section")
    core, pair = section % 2, section // 2
    sections = lax.axis_size("section")
    spans, positions = tokens.shape
    block, width, part = head.shape[1], head.shape[0], hidden.shape[2]
    count = 3 * spans * positions // 4 // sections
    half = positions // 2
    big = (count * 8 // 9) // 16 * 16
    small = count - big
    rows = hidden[0]
    gain = norm_gain[None]

    def mesh_perm(move):
        pairs = []
        for s in range(sections):
            for d in range(groups):
                s2, d2 = move(s, d)
                pairs.append((s * groups + d, s2 * groups + d2))
        return pairs

    send = lambda value, perm: lax.ppermute(value, AXES, perm)
    like = lambda v: jax.ShapeDtypeStruct(v.shape, v.dtype)
    acc_shape = jax.ShapeDtypeStruct((2 * count, 2 * block), F32)
    stats_shape = jax.ShapeDtypeStruct((8, up(2 * count)), F32)
    ids_shape = jax.ShapeDtypeStruct((2 * count, 1), I32)
    scales_shape = jax.ShapeDtypeStruct((2 * count, 1), F32)
    perm_z = {k: mesh_perm(lambda s, d, k=k: (s, d ^ (2 * k))) for k in (1, 2, 3)}
    perm_x = mesh_perm(lambda s, d: (s, d ^ 1))

    swap = [(s, s ^ 1) for s in range(sections)]
    over = [(s, s ^ 2) for s in range(sections)]
    across = [(s, s ^ 3) for s in range(sections)]
    extra = lax.ppermute(rows[half:], "section", [(1, 3), (3, 1)])
    sibling = lax.ppermute(rows, "section", swap)
    head_sibling = lax.ppermute(head, "section", swap)

    sums = call(
        sum_kernel,
        jax.ShapeDtypeStruct((8, positions), F32),
        [VMEM] * 3 + [SMEM],
        (rows, gain, reward_head[None], lengths),
    )
    if groups == 8:
        sums = sums + send(sums, perm_z[1])
        received = send(sums, perm_z[2])
    else:
        sums = lax.psum(sums, "dp")
        received = jnp.zeros_like(sums)
    full, g, sums = call(
        functools.partial(pick_kernel, count),
        [
            jax.ShapeDtypeStruct((count, part), BF16),
            jax.ShapeDtypeStruct((big, part), BF16),
            like(sums),
        ],
        [SMEM] + [VMEM] * 6,
        (lengths, rows, sibling, extra, gain, sums, received),
    )
    if groups == 8:
        sums = sums + send(sums, perm_x)
    token_ids, scales = call(
        functools.partial(row_kernel, count, width),
        [ids_shape, scales_shape],
        [SMEM] + [VMEM] * 5,
        (lengths, tokens, sums) + tuple(lax.ppermute(sums, "section", p) for p in (swap, over, across)),
    )

    if groups == 8:
        perm_a = mesh_perm(lambda s, d: (s, d ^ 1) if s % 2 == 0 else (s ^ 2, d))
        perm_b = mesh_perm(lambda s, d: (s ^ 2, d) if s % 2 == 0 else (s, d ^ 1))

        def gate(value, *after):
            return call(gate_kernel, like(value), [VMEM] + [ANY] * len(after), (value,) + after)

        def stage(k, acc, pieces, smalls, passed):
            args = (head, head_sibling, acc) + pieces + tuple(smalls.values()) + passed
            return call(
                functools.partial(stage_kernel, k, tuple(smalls), len(passed)),
                [acc_shape] + [like(p) for p in passed],
                [VMEM] * len(args),
                args,
            )

        z1 = send(g, perm_z[1])
        z3 = send(full, perm_z[3])[:big]
        a0 = send(full, perm_a)
        b0 = send(full, perm_b)
        c0 = send(a0, perm_b)
        z1 = gate(z1, b0)
        a1 = send(z1, perm_a)
        acc, token_ids, scales, w0, z1, z3 = call(
            functools.partial(first_kernel, big),
            [acc_shape, ids_shape, scales_shape, jax.ShapeDtypeStruct((4 * small, part), BF16), like(z1), like(z3)],
            [VMEM] * 10,
            (head, head_sibling, full, a0, b0, c0, token_ids, scales, z1, z3),
        )
        b1 = send(z1, perm_b)
        z2 = send(z3, perm_z[1])
        c1 = send(a1, perm_b)
        z3 = gate(z3, b1, z2)
        a3 = send(z3, perm_a)
        acc, z3, w0 = stage(1, acc, (z1, a1, b1, c1), {}, (z3, w0))
        b3 = send(z3, perm_b)
        w3 = send(w0, perm_z[3])
        w1 = send(w0, perm_z[1])
        c3 = send(a3, perm_b)
        z2 = gate(z2, b3)
        a2 = send(z2, perm_a)
        acc, z2, w3 = stage(3, acc, (z3, a3, b3, c3), {1: w1, 3: w3}, (z2, w3))
        b2 = send(z2, perm_b)
        w2 = send(w3, perm_z[1])
        c2 = send(a2, perm_b)
        left, far, wide = call(
            functools.partial(own_kernel, 2),
            [
                jax.ShapeDtypeStruct((big, 2 * block), F32),
                jax.ShapeDtypeStruct((part, 2 * block), BF16),
                jax.ShapeDtypeStruct((up(2 * count), LANES), F32),
            ],
            [VMEM] * 9,
            (head, head_sibling, acc, z2, a2, b2, w2, token_ids, scales),
        )
        stats = call(
            last_kernel,
            stats_shape,
            [VMEM] * 6,
            (far, left, c2, wide, token_ids, scales),
            scratch=[pltpu.VMEM((up(2 * count), LANES), F32)],
        )
        stats = combine([stats] + [send(stats, perm_z[k]) for k in (1, 2, 3)])
        stats = combine(
            [stats]
            + [send(stats, mesh_perm(lambda s, d, v=v: (s ^ v[0], d ^ v[1]))) for v in ((0, 1), (2, 0), (2, 1))]
        )
    else:
        other = lax.ppermute(full, "section", over)
        ordered = jnp.concatenate([jnp.where(pair == 0, full, other), jnp.where(pair == 0, other, full)])
        everything = lax.all_gather(ordered, "dp", axis=1, tiled=True)
        acc = jnp.concatenate(
            [jnp.dot(everything, h, preferred_element_type=F32) for h in (head, head_sibling)], axis=1
        )
        stats = call(whole_kernel, stats_shape, [VMEM] * 3, (acc, token_ids, scales))
        gathered = lax.all_gather(stats, "dp")
        stats = combine([gathered[i] for i in range(groups)])
        stats = combine([stats, lax.ppermute(stats, "section", over)])
    lp = stats[2:3] - (stats[0:1] + jnp.log(stats[1:2]))
    lp = jnp.concatenate([lp, jnp.zeros((7, lp.shape[1]), F32)])
    both = lambda v, u: jnp.stack([jnp.where(core == 0, v, u), jnp.where(core == 0, u, v)])
    stats = both(lp, lax.ppermute(lp, "section", swap))
    logprob, score = call(
        functools.partial(final_kernel, count, width),
        [jax.ShapeDtypeStruct((1, positions), F32), jax.ShapeDtypeStruct((1, 1), F32)],
        [SMEM, VMEM, VMEM],
        (lengths, sums, stats),
    )
    return (logprob, score[0])


def solution(mesh):
    groups = mesh.shape["dp"]
    return jax.shard_map(
        lambda *args: per_device(groups, *args),
        mesh=mesh,
        in_specs=(P("section", None, "dp"), P("dp"), P(None, ("section", "dp")), P("dp"), P(), P()),
        out_specs=(P("section", None), P("section")),
        check_vma=False,
    )
```

```python
import functools

import jax
import jax.numpy as jnp
from jax import lax
from jax.experimental import pallas as pl
from jax.experimental.pallas import tpu as pltpu
from jax.sharding import PartitionSpec as P

AXES = ("section", "dp")
F32 = jnp.float32
BF16 = jnp.bfloat16
I32 = jnp.int32
LANES = 128
VMEM = pl.BlockSpec(memory_space=pltpu.VMEM)
SMEM = pl.BlockSpec(memory_space=pltpu.SMEM)
ANY = pl.BlockSpec(memory_space=pl.ANY)


def row_map(lengths, pair, core, index, count):
    first, second = lengths[2 * pair], lengths[2 * pair + 1]
    other_first = lengths[2 - 2 * pair]
    j = core * count + index
    in_first = j < first
    in_second = j < first + second
    span = jnp.where(in_first, 2 * pair, jnp.where(in_second, 2 * pair + 1, 3 - 2 * pair))
    place = jnp.where(
        in_first, j, jnp.where(in_second, j - first, 2 * count - other_first + j - first - second)
    )
    return span, place


def as_rows(columns, count):
    lane = lax.broadcasted_iota(I32, (count, LANES), 1)
    wide = jnp.zeros((count, LANES), F32)
    for i, column in enumerate(columns):
        wide = jnp.where(lane == i, column, wide)
    return jnp.transpose(wide)[:8]


def as_column(rows, which):
    full = jnp.concatenate([rows, jnp.zeros((LANES - 8, rows.shape[1]), F32)], axis=0)
    return jnp.transpose(full)[:, which : which + 1]


def sum_kernel(rows, gain, reward, lengths, out):
    _, core, _ = here()
    value = rows[...].astype(F32)
    scaled = (value * gain[...].astype(F32)).astype(BF16).astype(F32)
    squares = jnp.sum(value * value, axis=1, keepdims=True)
    rewards = jnp.sum(scaled * reward[...].astype(F32), axis=1, keepdims=True)
    zero = jnp.zeros(squares.shape, F32)
    first = core == 0
    columns = [
        jnp.where(first, squares, zero),
        jnp.where(first, zero, squares),
        jnp.where(first, rewards, zero),
        jnp.where(first, zero, rewards),
    ]
    out[...] = as_rows(columns, rows.shape[0])


def pick_kernel(count, lengths, rows, sibling, extra, gain, s0, s1, s2, s3, full, sums_out):
    section = lax.axis_index("section")
    core, pair = lax.rem(section, 2), lax.div(section, 2)
    positions, half = rows.shape[0], extra.shape[0]
    index = lax.broadcasted_iota(I32, (count, 1), 0)
    span, place = row_map(lengths, pair, core, index, count)
    source = jnp.where(span == section, place, place + positions)
    source = jnp.where(span // 2 == pair, source, place + (2 * positions - (positions - half)))
    lane = lax.broadcasted_iota(I32, (count, 2 * positions + half), 1)
    pick = jnp.where(lane == source, F32(1.0), F32(0.0)).astype(BF16)
    picked = jnp.dot(pick[:, :positions], rows[...], preferred_element_type=F32)
    picked += jnp.dot(pick[:, positions : 2 * positions], sibling[...], preferred_element_type=F32)
    picked += jnp.dot(pick[:, 2 * positions :], extra[...], preferred_element_type=F32)
    scaled = (picked * gain[...].astype(F32)).astype(BF16)
    full[...] = scaled
    sums_out[...] = s0[...] + s1[...] + s2[...] + s3[...]


def row_kernel(count, width, lengths, tokens, near, across, ids, scales):
    _, core, own_pair = here()
    spans, positions = tokens.shape
    for pair in range(2):
        index = lax.broadcasted_iota(I32, (count, 1), 0)
        span, place = row_map(lengths, pair, core, index, count)
        lane = lax.broadcasted_iota(I32, (count, positions), 1)
        found = jnp.zeros((count, positions), F32)
        squares = jnp.zeros((count, positions), F32)
        for s in range(spans):
            found = jnp.where(span == s, tokens[s : s + 1, :].astype(F32), found)
            row = s % 2
            value = jnp.where(own_pair == s // 2, near[row : row + 1, :], across[row : row + 1, :])
            squares = jnp.where(span == s, value, squares)
        hit = lane == place
        found = jnp.sum(jnp.where(hit, found, F32(0.0)), axis=1, keepdims=True)
        squares = jnp.sum(jnp.where(hit, squares, F32(0.0)), axis=1, keepdims=True)
        ids[pair * count : pair * count + count, :] = found.astype(I32)
        scales[pair * count : pair * count + count, :] = lax.rsqrt(squares / width + 1e-05)


def here():
    section = lax.axis_index("section")
    return section, lax.rem(section, 2), lax.div(section, 2)


def blocks(count):
    _, _, pair = here()
    return pl.multiple_of(pair * count, 16), pl.multiple_of((1 - pair) * count, 16)


def weights(head, sibling, depth, k, far):
    dp_index = lax.axis_index("dp")
    where = jnp.bitwise_xor(dp_index, 2 * k + (1 if far else 0))
    rows = pl.ds(pl.multiple_of(where * depth, depth), depth)
    return head[rows, :], sibling[rows, :]


def products(terms):
    value = jnp.concatenate([t[0] for t in terms], axis=1) if len(terms) > 1 else terms[0][0]
    out = []
    for side in range(2):
        w = [t[1][side] for t in terms]
        w = jnp.concatenate(w, axis=0) if len(w) > 1 else w[0]
        out.append(jnp.dot(value, w, preferred_element_type=F32))
    return jnp.concatenate(out, axis=1)


def first_kernel(head, sibling, z, a, b, c, ids, scales, z1, z3, after, acc, ids_out, scales_out, z1_out, z3_out):
    count, depth = z.shape
    _, core, _ = here()
    mine, others = blocks(count)
    near = weights(head, sibling, depth, 0, False)
    far = weights(head, sibling, depth, 0, True)
    for which, same, cross in ((0, a, b), (1, b, a)):

        @pl.when(core == which)
        def _():
            acc[pl.ds(mine, count), :] = products([(z[...], near), (same[...], far)])
            acc[pl.ds(others, count), :] = products([(cross[...], near), (c[...], far)])

    ids_out[...] = ids[...]
    scales_out[...] = scales[...]
    z1_out[...] = z1[...]
    z3_out[...] = z3[...]


def stage_kernel(k, head, sibling, acc_in, z, a, b, passed, acc, out):
    count, depth = z.shape
    _, core, _ = here()
    mine, others = blocks(count)
    near = weights(head, sibling, depth, k, False)
    far = weights(head, sibling, depth, k, True)
    for which, same, cross in ((0, a, b), (1, b, a)):

        @pl.when(core == which)
        def _():
            rows = pl.ds(mine, count)
            acc[rows, :] = acc_in[rows, :] + products([(z[...], near), (same[...], far)])
            rows = pl.ds(others, count)
            acc[rows, :] = acc_in[rows, :] + products([(cross[...], near)])

    out[...] = passed[...]


def gate_kernel(value, *refs):
    refs[-1][...] = value[...]


def column_ids(block):
    section, core, _ = here()
    dp_index, groups = lax.axis_index("dp"), lax.axis_size("dp")
    lane = lax.broadcasted_iota(I32, (1, block), 1)
    own = (section * groups + dp_index) * block
    other = ((section + 1 - 2 * core) * groups + dp_index) * block
    return jnp.concatenate([lane + own, lane + other], axis=1)


def summary(logits, scale, token_ids, ids):
    logits = logits * scale
    top = jnp.max(logits, axis=1, keepdims=True)
    total = jnp.sum(jnp.exp(logits - top), axis=1, keepdims=True)
    target = jnp.sum(jnp.where(ids == token_ids, logits, F32(0.0)), axis=1, keepdims=True)
    lane = lax.broadcasted_iota(I32, (logits.shape[0], LANES), 1)
    return jnp.where(lane == 0, top, jnp.where(lane == 1, total, jnp.where(lane == 2, target, F32(0.0))))


def own_kernel(head, sibling, acc_in, z, a, b, c1, c3, token_ids, scales, left, far_out, wide):
    count, depth = z.shape
    _, core, _ = here()
    mine, others = blocks(count)
    near = weights(head, sibling, depth, 2, False)
    far = weights(head, sibling, depth, 2, True)
    block = head.shape[1]
    far_out[:, :block] = far[0]
    far_out[:, block:] = far[1]
    ids = column_ids(block)
    far1 = weights(head, sibling, depth, 1, True)
    far3 = weights(head, sibling, depth, 3, True)
    wide[...] = jnp.zeros(wide.shape, F32)
    for which, same, cross in ((0, a, b), (1, b, a)):

        @pl.when(core == which)
        def _():
            rows = pl.ds(mine, count)
            logits = acc_in[rows, :] + products([(z[...], near), (same[...], far)])
            wide[rows, :] = summary(logits, scales[rows, :], token_ids[rows, :], ids)
            left[...] = acc_in[pl.ds(others, count), :] + products(
                [(cross[...], near), (c1[...], far1), (c3[...], far3)]
            )


def last_kernel(far, left, c, wide_in, token_ids, scales, out, wide):
    count = c.shape[0]
    _, others = blocks(count)
    ids = column_ids(far.shape[1] // 2)
    wide[...] = wide_in[...]
    logits = left[...] + jnp.dot(c[...], far[...], preferred_element_type=F32)
    rows = pl.ds(others, count)
    wide[rows, :] = summary(logits, scales[rows, :], token_ids[rows, :], ids)
    out[...] = jnp.transpose(wide[...])[:8]


def whole_kernel(acc, token_ids, scales, out):
    count = acc.shape[0] // 2
    ids = column_ids(acc.shape[1] // 2)
    wide = summary(acc[...], scales[...], token_ids[...], ids)
    wide = jnp.concatenate([wide, jnp.zeros((out.shape[1] - 2 * count, LANES), F32)])
    out[...] = jnp.transpose(wide)[:8]


def final_kernel(count, width, lengths, sums, stats, out_ref, score_ref):
    section = lax.axis_index("section")
    positions = out_ref.shape[1]
    where = lax.broadcasted_iota(I32, (1, positions), 1)
    logprob = jnp.zeros((1, positions), F32)
    index = lax.broadcasted_iota(I32, (count, 1), 0)
    for core in range(2):
        lp = as_column(stats[core], 0)
        for pair in range(2):
            value = lp[pair * count : pair * count + count]
            span, place = row_map(lengths, pair, core, index, count)
            hit = (place == where) & (span == section)
            logprob += jnp.sum(jnp.where(hit, value, F32(0.0)), axis=0, keepdims=True)
    out_ref[...] = logprob
    length = lengths[section]
    first = lax.rem(section, 2) == 0
    squares = jnp.where(first, sums[0:1, :], sums[1:2, :])
    reward = jnp.where(first, sums[2:3, :], sums[3:4, :]) * lax.rsqrt(squares / width + 1e-05)
    score = jnp.sum(jnp.where(where < length, reward, F32(0.0)), axis=1, keepdims=True)
    score_ref[...] = score / length.astype(F32)


def combine(parts):
    top = parts[0][0]
    for part in parts[1:]:
        top = jnp.maximum(top, part[0])
    total = sum(part[1] * jnp.exp(part[0] - top) for part in parts)
    target = sum(part[2] for part in parts)
    return jnp.concatenate([jnp.stack([top, total, target]), jnp.zeros((5,) + top.shape, F32)])


def call(body, outs, in_specs, args, limit=16, scratch=()):
    many = isinstance(outs, (list, tuple))
    return pl.pallas_call(
        body,
        out_shape=outs,
        in_specs=in_specs,
        out_specs=[VMEM] * len(outs) if many else VMEM,
        scratch_shapes=scratch,
        compiler_params=pltpu.CompilerParams(vmem_limit_bytes=limit << 20),
    )(*args)


def up(value):
    return -(-value // LANES) * LANES


def per_device(groups, hidden, norm_gain, head, reward_head, tokens, lengths):
    section = lax.axis_index("section")
    core, pair = section % 2, section // 2
    sections = lax.axis_size("section")
    spans, positions = tokens.shape
    block, width, part = head.shape[1], head.shape[0], hidden.shape[2]
    count = 3 * spans * positions // 4 // sections
    half = positions // 2
    rows = hidden[0]
    gain = norm_gain[None]

    def mesh_perm(move):
        pairs = []
        for s in range(sections):
            for d in range(groups):
                s2, d2 = move(s, d)
                pairs.append((s * groups + d, s2 * groups + d2))
        return pairs

    send = lambda value, perm: lax.ppermute(value, AXES, perm)
    like = lambda v: jax.ShapeDtypeStruct(v.shape, v.dtype)
    acc_shape = jax.ShapeDtypeStruct((2 * count, 2 * block), F32)
    stats_shape = jax.ShapeDtypeStruct((8, up(2 * count)), F32)
    ids_shape = jax.ShapeDtypeStruct((2 * count, 1), I32)
    scales_shape = jax.ShapeDtypeStruct((2 * count, 1), F32)
    perm_z = {k: mesh_perm(lambda s, d, k=k: (s, d ^ (2 * k))) for k in (1, 2, 3)}
    perm_x = mesh_perm(lambda s, d: (s, d ^ 1))

    swap = [(s, s ^ 1) for s in range(sections)]
    over = [(s, s ^ 2) for s in range(sections)]
    extra = lax.ppermute(rows[half:], "section", [(1, 3), (3, 1)])
    sibling = lax.ppermute(rows, "section", swap)
    head_sibling = lax.ppermute(head, "section", swap)

    sums = call(
        sum_kernel,
        jax.ShapeDtypeStruct((8, positions), F32),
        [VMEM] * 3 + [SMEM],
        (rows, gain, reward_head[None], lengths),
    )
    sums = sums + lax.ppermute(sums, "section", swap)
    if groups == 8:
        parts = (sums,) + tuple(send(sums, perm_z[k]) for k in (1, 2, 3))
    else:
        sums = lax.psum(sums, "dp")
        parts = (sums,) + (jnp.zeros_like(sums),) * 3
    full, sums = call(
        functools.partial(pick_kernel, count),
        [jax.ShapeDtypeStruct((count, part), BF16), like(sums)],
        [SMEM] + [VMEM] * 8,
        (lengths, rows, sibling, extra, gain) + parts,
    )
    if groups == 8:
        sums = sums + send(sums, perm_x)
    token_ids, scales = call(
        functools.partial(row_kernel, count, width),
        [ids_shape, scales_shape],
        [SMEM] + [VMEM] * 3,
        (lengths, tokens, sums, lax.ppermute(sums, "section", over)),
    )

    if groups == 8:
        perm_a = mesh_perm(lambda s, d: (s, d ^ 1) if s % 2 == 0 else (s ^ 2, d))
        perm_b = mesh_perm(lambda s, d: (s ^ 2, d) if s % 2 == 0 else (s, d ^ 1))

        def gate(value, *after):
            return call(gate_kernel, like(value), [VMEM] + [ANY] * len(after), (value,) + after)

        def stage(k, acc, pieces, passed):
            args = (head, head_sibling, acc) + pieces + (passed,)
            return call(functools.partial(stage_kernel, k), [acc_shape, like(passed)], [VMEM] * len(args), args)

        z1 = send(full, perm_z[1])
        z3 = send(full, perm_z[3])
        a0 = send(full, perm_a)
        b0 = send(full, perm_b)
        c0 = send(a0, perm_b)
        z1 = gate(z1, b0)
        a1 = send(z1, perm_a)
        acc, token_ids, scales, z1, z3 = call(
            first_kernel,
            [acc_shape, ids_shape, scales_shape, like(z1), like(z3)],
            [VMEM] * 10 + [ANY],
            (head, head_sibling, full, a0, b0, c0, token_ids, scales, z1, z3, a1),
        )
        b1 = send(z1, perm_b)
        a3 = send(z3, perm_a)
        z2 = send(z3, perm_z[1])
        acc, z3 = stage(1, acc, (z1, a1, b1), z3)
        b3 = send(z3, perm_b)
        z2 = gate(z2, a3)
        a2 = send(z2, perm_a)
        acc, a3 = stage(3, acc, (z3, a3, b3), a3)
        c3 = send(a3, perm_b)
        c1 = send(c0, perm_z[1])
        z2 = gate(z2, a2)
        b2 = send(z2, perm_b)
        c2 = send(a2, perm_b)
        left, far, wide = call(
            own_kernel,
            [
                jax.ShapeDtypeStruct((count, 2 * block), F32),
                jax.ShapeDtypeStruct((part, 2 * block), BF16),
                jax.ShapeDtypeStruct((up(2 * count), LANES), F32),
            ],
            [VMEM] * 10,
            (head, head_sibling, acc, z2, a2, b2, c1, c3, token_ids, scales),
        )
        stats = call(
            last_kernel,
            stats_shape,
            [VMEM] * 6,
            (far, left, c2, wide, token_ids, scales),
            scratch=[pltpu.VMEM((up(2 * count), LANES), F32)],
        )
        stats = combine([stats] + [send(stats, perm_z[k]) for k in (1, 2, 3)])
        stats = combine(
            [stats]
            + [send(stats, mesh_perm(lambda s, d, v=v: (s ^ v[0], d ^ v[1]))) for v in ((0, 1), (2, 0), (2, 1))]
        )
    else:
        other = lax.ppermute(full, "section", over)
        ordered = jnp.concatenate([jnp.where(pair == 0, full, other), jnp.where(pair == 0, other, full)])
        everything = lax.all_gather(ordered, "dp", axis=1, tiled=True)
        acc = jnp.concatenate(
            [jnp.dot(everything, h, preferred_element_type=F32) for h in (head, head_sibling)], axis=1
        )
        stats = call(whole_kernel, stats_shape, [VMEM] * 3, (acc, token_ids, scales))
        gathered = lax.all_gather(stats, "dp")
        stats = combine([gathered[i] for i in range(groups)])
        stats = combine([stats, lax.ppermute(stats, "section", over)])
    lp = stats[2:3] - (stats[0:1] + jnp.log(stats[1:2]))
    lp = jnp.concatenate([lp, jnp.zeros((7, lp.shape[1]), F32)])
    both = lambda v, u: jnp.stack([jnp.where(core == 0, v, u), jnp.where(core == 0, u, v)])
    stats = both(lp, lax.ppermute(lp, "section", swap))
    logprob, score = call(
        functools.partial(final_kernel, count, width),
        [jax.ShapeDtypeStruct((1, positions), F32), jax.ShapeDtypeStruct((1, 1), F32)],
        [SMEM, VMEM, VMEM],
        (lengths, sums, stats),
    )
    return (logprob, score[0])


def solution(mesh):
    groups = mesh.shape["dp"]
    return jax.shard_map(
        lambda *args: per_device(groups, *args),
        mesh=mesh,
        in_specs=(P("section", None, "dp"), P("dp"), P(None, ("section", "dp")), P("dp"), P(), P()),
        out_specs=(P("section", None), P("section")),
        check_vma=False,
    )
```

```python
import functools

import jax
import jax.numpy as jnp
from jax import lax
from jax.experimental import pallas as pl
from jax.experimental.pallas import tpu as pltpu
from jax.sharding import PartitionSpec as P

AXES = ("section", "dp")
F32 = jnp.float32
BF16 = jnp.bfloat16
I32 = jnp.int32
LANES = 128
VMEM = pl.BlockSpec(memory_space=pltpu.VMEM)
SMEM = pl.BlockSpec(memory_space=pltpu.SMEM)
ANY = pl.BlockSpec(memory_space=pl.ANY)


def row_map(lengths, pair, core, index, count):
    first, second = lengths[2 * pair], lengths[2 * pair + 1]
    other_first = lengths[2 - 2 * pair]
    j = core * count + index
    in_first = j < first
    in_second = j < first + second
    span = jnp.where(in_first, 2 * pair, jnp.where(in_second, 2 * pair + 1, 3 - 2 * pair))
    place = jnp.where(
        in_first, j, jnp.where(in_second, j - first, 2 * count - other_first + j - first - second)
    )
    return span, place


def as_rows(columns, count):
    lane = lax.broadcasted_iota(I32, (count, LANES), 1)
    wide = jnp.zeros((count, LANES), F32)
    for i, column in enumerate(columns):
        wide = jnp.where(lane == i, column, wide)
    return jnp.transpose(wide)[:8]


def as_column(rows, which):
    full = jnp.concatenate([rows, jnp.zeros((LANES - 8, rows.shape[1]), F32)], axis=0)
    return jnp.transpose(full)[:, which : which + 1]


def pick_kernel(count, lengths, rows, sibling, extra, near, far, full, near_out, far_out):
    section = lax.axis_index("section")
    core, pair = lax.rem(section, 2), lax.div(section, 2)
    positions, half = rows.shape[0], extra.shape[0]
    index = lax.broadcasted_iota(I32, (count, 1), 0)
    span, place = row_map(lengths, pair, core, index, count)
    source = jnp.where(span == section, place, place + positions)
    source = jnp.where(span // 2 == pair, source, place + (2 * positions - (positions - half)))
    lane = lax.broadcasted_iota(I32, (count, 2 * positions + half), 1)
    pick = jnp.where(lane == source, F32(1.0), F32(0.0)).astype(BF16)
    picked = jnp.dot(pick[:, :positions], rows[...], preferred_element_type=F32)
    picked += jnp.dot(pick[:, positions : 2 * positions], sibling[...], preferred_element_type=F32)
    picked += jnp.dot(pick[:, 2 * positions :], extra[...], preferred_element_type=F32)
    full[...] = (picked * near[0:1, :]).astype(BF16)
    near_out[...] = near[...]
    far_out[...] = far[...]


def token_kernel(count, lengths, tokens, out):
    core = lax.rem(lax.axis_index("section"), 2)
    spans, positions = tokens.shape
    for pair in range(2):
        index = lax.broadcasted_iota(I32, (count, 1), 0)
        span, place = row_map(lengths, pair, core, index, count)
        lane = lax.broadcasted_iota(I32, (count, positions), 1)
        found = jnp.zeros((count, positions), F32)
        for s in range(spans):
            found = jnp.where(span == s, tokens[s : s + 1, :].astype(F32), found)
        found = jnp.sum(jnp.where(lane == place, found, F32(0.0)), axis=1, keepdims=True)
        out[pair * count : pair * count + count, :] = found.astype(I32)


def here():
    section = lax.axis_index("section")
    return section, lax.rem(section, 2), lax.div(section, 2)


def blocks(count):
    _, _, pair = here()
    return pl.multiple_of(pair * count, 16), pl.multiple_of((1 - pair) * count, 16)


def weights(head, sibling, depth, k, far):
    dp_index = lax.axis_index("dp")
    where = jnp.bitwise_xor(dp_index, 2 * k + (1 if far else 0))
    rows = pl.ds(pl.multiple_of(where * depth, depth), depth)
    return head[rows, :], sibling[rows, :]


def products(terms):
    value = jnp.concatenate([t[0] for t in terms], axis=1) if len(terms) > 1 else terms[0][0]
    out = []
    for side in range(2):
        w = [t[1][side] for t in terms]
        w = jnp.concatenate(w, axis=0) if len(w) > 1 else w[0]
        out.append(jnp.dot(value, w, preferred_element_type=F32))
    return jnp.concatenate(out, axis=1)


def sides(terms):
    square, reward = None, None
    for value, table, k in terms:
        value = value.astype(F32)
        gain, weight = table[k : k + 1, :], table[k + 4 : k + 5, :]
        s = value * value * (1.0 / (gain * gain))
        r = value * weight
        for i in range(value.shape[1] // LANES):
            cols = slice(i * LANES, (i + 1) * LANES)
            square = s[:, cols] if square is None else square + s[:, cols]
            reward = r[:, cols] if reward is None else reward + r[:, cols]
    return jnp.concatenate([square, reward], axis=1)


def begin_kernel(head, sibling, near, far, z, a, b, c, z1, a1, b1, ids, z2, acc, side, ids_out, z2_out):
    count, depth = z.shape
    _, core, _ = here()
    mine, others = blocks(count)
    near0, far0 = weights(head, sibling, depth, 0, False), weights(head, sibling, depth, 0, True)
    near1, far1 = weights(head, sibling, depth, 1, False), weights(head, sibling, depth, 1, True)
    for which, same, cross, same1, cross1 in ((0, a, b, a1, b1), (1, b, a, b1, a1)):

        @pl.when(core == which)
        def _():
            rows = pl.ds(mine, count)
            acc[rows, :] = products([(z[...], near0), (same[...], far0), (z1[...], near1), (same1[...], far1)])
            side[rows, :] = sides([(z[...], near, 0), (same[...], far, 0), (z1[...], near, 1), (same1[...], far, 1)])
            rows = pl.ds(others, count)
            acc[rows, :] = products([(cross[...], near0), (c[...], far0), (cross1[...], near1)])
            side[rows, :] = sides([(cross[...], near, 0), (c[...], far, 0), (cross1[...], near, 1)])

    ids_out[...] = ids[...]
    z2_out[...] = z2[...]


def middle_kernel(head, sibling, near, far, acc_in, side_in, z, a, b, c, a2, acc, side, a2_out):
    count, depth = z.shape
    _, core, _ = here()
    mine, others = blocks(count)
    near3, far3 = weights(head, sibling, depth, 3, False), weights(head, sibling, depth, 3, True)
    for which, same, cross in ((0, a, b), (1, b, a)):

        @pl.when(core == which)
        def _():
            rows = pl.ds(mine, count)
            acc[rows, :] = acc_in[rows, :] + products([(z[...], near3), (same[...], far3)])
            side[rows, :] = side_in[rows, :] + sides([(z[...], near, 3), (same[...], far, 3)])
            rows = pl.ds(others, count)
            acc[rows, :] = acc_in[rows, :] + products([(cross[...], near3), (c[...], far3)])
            side[rows, :] = side_in[rows, :] + sides([(cross[...], near, 3), (c[...], far, 3)])

    a2_out[...] = a2[...]


def gate_kernel(value, *refs):
    refs[-1][...] = value[...]


def column_ids(block):
    section, core, _ = here()
    dp_index, groups = lax.axis_index("dp"), lax.axis_size("dp")
    lane = lax.broadcasted_iota(I32, (1, block), 1)
    own = (section * groups + dp_index) * block
    other = ((section + 1 - 2 * core) * groups + dp_index) * block
    return jnp.concatenate([lane + own, lane + other], axis=1)


def summary(logits, square, reward, token_ids, ids, width):
    scale = lax.rsqrt(square / width + 1e-05)
    logits = logits * scale
    top = jnp.max(logits, axis=1, keepdims=True)
    total = jnp.sum(jnp.exp(logits - top), axis=1, keepdims=True)
    target = jnp.sum(jnp.where(ids == token_ids, logits, F32(0.0)), axis=1, keepdims=True)
    lane = lax.broadcasted_iota(I32, (logits.shape[0], LANES), 1)
    wide = jnp.where(lane == 2, target, jnp.where(lane == 3, reward * scale, F32(0.0)))
    return jnp.where(lane == 0, top, jnp.where(lane == 1, total, wide))


def added(side):
    return jnp.sum(side[:, :LANES], axis=1, keepdims=True), jnp.sum(side[:, LANES:], axis=1, keepdims=True)


def own_kernel(width, head, sibling, near, far, acc_in, side_in, z, a, b, c1, token_ids, left, left_side, far_out, wide):
    count, depth = z.shape
    _, core, _ = here()
    mine, others = blocks(count)
    near2, far2 = weights(head, sibling, depth, 2, False), weights(head, sibling, depth, 2, True)
    far1 = weights(head, sibling, depth, 1, True)
    block = head.shape[1]
    far_out[:, :block] = far2[0]
    far_out[:, block:] = far2[1]
    ids = column_ids(block)
    wide[...] = jnp.zeros(wide.shape, F32)
    for which, same, cross in ((0, a, b), (1, b, a)):

        @pl.when(core == which)
        def _():
            rows = pl.ds(mine, count)
            logits = acc_in[rows, :] + products([(z[...], near2), (same[...], far2)])
            square, reward = added(side_in[rows, :] + sides([(z[...], near, 2), (same[...], far, 2)]))
            wide[rows, :] = summary(logits, square, reward, token_ids[rows, :], ids, width)
            rows = pl.ds(others, count)
            left[...] = acc_in[rows, :] + products([(cross[...], near2), (c1[...], far1)])
            left_side[...] = side_in[rows, :] + sides([(cross[...], near, 2), (c1[...], far, 1)])


def last_kernel(width, far_weights, far, left, left_side, c, wide_in, token_ids, out, wide):
    count = c.shape[0]
    _, others = blocks(count)
    ids = column_ids(far_weights.shape[1] // 2)
    wide[...] = wide_in[...]
    logits = left[...] + jnp.dot(c[...], far_weights[...], preferred_element_type=F32)
    square, reward = added(left_side[...] + sides([(c[...], far, 2)]))
    rows = pl.ds(others, count)
    wide[rows, :] = summary(logits, square, reward, token_ids[rows, :], ids, width)
    out[...] = jnp.transpose(wide[...])[:8]


def whole_kernel(width, acc, square, reward, token_ids, out):
    count = acc.shape[0] // 2
    ids = column_ids(acc.shape[1] // 2)
    wide = summary(acc[...], square[...], reward[...], token_ids[...], ids, width)
    wide = jnp.concatenate([wide, jnp.zeros((out.shape[1] - 2 * count, LANES), F32)])
    out[...] = jnp.transpose(wide)[:8]


def final_kernel(count, lengths, stats, out_ref, score_ref):
    section = lax.axis_index("section")
    positions = out_ref.shape[1]
    where = lax.broadcasted_iota(I32, (1, positions), 1)
    logprob = jnp.zeros((1, positions), F32)
    score = jnp.zeros((1, 1), F32)
    index = lax.broadcasted_iota(I32, (count, 1), 0)
    for core in range(2):
        columns = jnp.transpose(
            jnp.concatenate([stats[core], jnp.zeros((LANES - 8, stats.shape[2]), F32)], axis=0)
        )
        for pair in range(2):
            value = columns[pair * count : pair * count + count]
            span, place = row_map(lengths, pair, core, index, count)
            own = span == section
            logprob += jnp.sum(jnp.where((place == where) & own, value[:, 0:1], F32(0.0)), axis=0, keepdims=True)
            score += jnp.sum(jnp.where(own, value[:, 1:2], F32(0.0)), axis=0, keepdims=True)
    out_ref[...] = logprob
    score_ref[...] = score / lengths[section].astype(F32)


def combine(parts):
    top = parts[0][0]
    for part in parts[1:]:
        top = jnp.maximum(top, part[0])
    total = sum(part[1] * jnp.exp(part[0] - top) for part in parts)
    target = sum(part[2] for part in parts)
    return jnp.concatenate([jnp.stack([top, total, target, parts[0][3]]), jnp.zeros((4,) + top.shape, F32)])


def call(body, outs, in_specs, args, limit=16, scratch=()):
    many = isinstance(outs, (list, tuple))
    return pl.pallas_call(
        body,
        out_shape=outs,
        in_specs=in_specs,
        out_specs=[VMEM] * len(outs) if many else VMEM,
        scratch_shapes=scratch,
        compiler_params=pltpu.CompilerParams(vmem_limit_bytes=limit << 20),
    )(*args)


def up(value):
    return -(-value // LANES) * LANES


def per_device(groups, hidden, norm_gain, head, reward_head, tokens, lengths):
    section = lax.axis_index("section")
    core, pair = section % 2, section // 2
    sections = lax.axis_size("section")
    spans, positions = tokens.shape
    block, width, part = head.shape[1], head.shape[0], hidden.shape[2]
    count = 3 * spans * positions // 4 // sections
    half = positions // 2
    rows = hidden[0]

    def mesh_perm(move):
        pairs = []
        for s in range(sections):
            for d in range(groups):
                s2, d2 = move(s, d)
                pairs.append((s * groups + d, s2 * groups + d2))
        return pairs

    send = lambda value, perm: lax.ppermute(value, AXES, perm)
    like = lambda v: jax.ShapeDtypeStruct(v.shape, v.dtype)
    acc_shape = jax.ShapeDtypeStruct((2 * count, 2 * block), F32)
    stats_shape = jax.ShapeDtypeStruct((8, up(2 * count)), F32)
    ids_shape = jax.ShapeDtypeStruct((2 * count, 1), I32)
    perm_z = {k: mesh_perm(lambda s, d, k=k: (s, d ^ (2 * k))) for k in (1, 2, 3)}
    perm_x = mesh_perm(lambda s, d: (s, d ^ 1))
    table = jnp.stack([norm_gain, reward_head]).astype(F32)

    swap = [(s, s ^ 1) for s in range(sections)]
    over = [(s, s ^ 2) for s in range(sections)]
    extra = lax.ppermute(rows[half:], "section", [(1, 3), (3, 1)])
    sibling = lax.ppermute(rows, "section", swap)
    head_sibling = lax.ppermute(head, "section", swap)

    if groups == 8:
        tables = [table] + [send(table, perm_z[k]) for k in (1, 2, 3)]
        near = jnp.concatenate([t[i : i + 1] for i in range(2) for t in tables])
        far = send(near, perm_x)
    else:
        near = jnp.concatenate([jnp.broadcast_to(table[i : i + 1], (4, part)) for i in range(2)])
        far = near
    full, near, far = call(
        functools.partial(pick_kernel, count),
        [jax.ShapeDtypeStruct((count, part), BF16), like(near), like(far)],
        [SMEM] + [VMEM] * 5,
        (lengths, rows, sibling, extra, near, far),
    )
    token_ids = call(functools.partial(token_kernel, count), ids_shape, [SMEM, VMEM], (lengths, tokens))

    if groups == 8:
        perm_a = mesh_perm(lambda s, d: (s, d ^ 1) if s % 2 == 0 else (s ^ 2, d))
        perm_b = mesh_perm(lambda s, d: (s ^ 2, d) if s % 2 == 0 else (s, d ^ 1))

        def gate(value, *after):
            return call(gate_kernel, like(value), [VMEM] + [ANY] * len(after), (value,) + after)

        side_shape = jax.ShapeDtypeStruct((2 * count, 2 * LANES), F32)
        z1 = send(full, perm_z[1])
        z3 = send(full, perm_z[3])
        a0 = send(full, perm_a)
        b0 = send(full, perm_b)
        c0 = send(a0, perm_b)
        z1 = gate(z1, b0)
        a1 = send(z1, perm_a)
        b1 = send(z1, perm_b)
        z3 = gate(z3, a1, b1, c0)
        a3 = send(z3, perm_a)
        b3 = send(z3, perm_b)
        z2 = send(z3, perm_z[1])
        c3 = send(a3, perm_b)
        acc, side, token_ids, z2 = call(
            begin_kernel,
            [acc_shape, side_shape, ids_shape, like(z2)],
            [VMEM] * 13,
            (head, head_sibling, near, far, full, a0, b0, c0, z1, a1, b1, token_ids, z2),
        )
        a2 = send(z2, perm_a)
        b2 = send(z2, perm_b)
        c1 = send(c0, perm_z[1])
        acc, side, a2 = call(
            middle_kernel,
            [acc_shape, side_shape, like(a2)],
            [VMEM] * 11,
            (head, head_sibling, near, far, acc, side, z3, a3, b3, c3, a2),
        )
        c2 = send(a2, perm_b)
        left, left_side, far_weights, wide = call(
            functools.partial(own_kernel, width),
            [
                jax.ShapeDtypeStruct((count, 2 * block), F32),
                jax.ShapeDtypeStruct((count, 2 * LANES), F32),
                jax.ShapeDtypeStruct((part, 2 * block), BF16),
                jax.ShapeDtypeStruct((up(2 * count), LANES), F32),
            ],
            [VMEM] * 11,
            (head, head_sibling, near, far, acc, side, z2, a2, b2, c1, token_ids),
        )
        stats = call(
            functools.partial(last_kernel, width),
            stats_shape,
            [VMEM] * 7,
            (far_weights, far, left, left_side, c2, wide, token_ids),
            scratch=[pltpu.VMEM((up(2 * count), LANES), F32)],
        )
        stats = combine([stats] + [send(stats, perm_z[k]) for k in (1, 2, 3)])
        stats = combine(
            [stats]
            + [send(stats, mesh_perm(lambda s, d, v=v: (s ^ v[0], d ^ v[1]))) for v in ((0, 1), (2, 0), (2, 1))]
        )
    else:
        other = lax.ppermute(full, "section", over)
        ordered = jnp.concatenate([jnp.where(pair == 0, full, other), jnp.where(pair == 0, other, full)])
        everything = lax.all_gather(ordered, "dp", axis=1, tiled=True)
        acc = jnp.concatenate(
            [jnp.dot(everything, h, preferred_element_type=F32) for h in (head, head_sibling)], axis=1
        )
        gains, weights_all = (lax.all_gather(t, "dp", axis=0, tiled=True) for t in table)
        wide = everything.astype(F32)
        square = jnp.sum((wide / gains) ** 2, axis=1, keepdims=True)
        reward = jnp.sum(wide * weights_all, axis=1, keepdims=True)
        stats = call(
            functools.partial(whole_kernel, width), stats_shape, [VMEM] * 4, (acc, square, reward, token_ids)
        )
        gathered = lax.all_gather(stats, "dp")
        stats = combine([gathered[i] for i in range(groups)])
        stats = combine([stats, lax.ppermute(stats, "section", over)])
    lp = stats[2:3] - (stats[0:1] + jnp.log(stats[1:2]))
    lp = jnp.concatenate([lp, stats[3:4], jnp.zeros((6, lp.shape[1]), F32)])
    both = lambda v, u: jnp.stack([jnp.where(core == 0, v, u), jnp.where(core == 0, u, v)])
    stats = both(lp, lax.ppermute(lp, "section", swap))
    logprob, score = call(
        functools.partial(final_kernel, count),
        [jax.ShapeDtypeStruct((1, positions), F32), jax.ShapeDtypeStruct((1, 1), F32)],
        [SMEM, VMEM],
        (lengths, stats),
    )
    return (logprob, score[0])


def solution(mesh):
    groups = mesh.shape["dp"]
    return jax.shard_map(
        lambda *args: per_device(groups, *args),
        mesh=mesh,
        in_specs=(P("section", None, "dp"), P("dp"), P(None, ("section", "dp")), P("dp"), P(), P()),
        out_specs=(P("section", None), P("section")),
        check_vma=False,
    )
```

```python
import functools

import jax
import jax.numpy as jnp
from jax import lax
from jax.experimental import pallas as pl
from jax.experimental.pallas import tpu as pltpu
from jax.sharding import PartitionSpec as P

AXES = ("section", "dp")
F32 = jnp.float32
BF16 = jnp.bfloat16
I32 = jnp.int32
LANES = 128
VMEM = pl.BlockSpec(memory_space=pltpu.VMEM)
SMEM = pl.BlockSpec(memory_space=pltpu.SMEM)
ANY = pl.BlockSpec(memory_space=pl.ANY)


def row_map(lengths, pair, core, index, count):
    first, second = lengths[2 * pair], lengths[2 * pair + 1]
    other_first = lengths[2 - 2 * pair]
    j = core * count + index
    in_first = j < first
    in_second = j < first + second
    span = jnp.where(in_first, 2 * pair, jnp.where(in_second, 2 * pair + 1, 3 - 2 * pair))
    place = jnp.where(
        in_first, j, jnp.where(in_second, j - first, 2 * count - other_first + j - first - second)
    )
    return span, place


def as_rows(columns, count):
    lane = lax.broadcasted_iota(I32, (count, LANES), 1)
    wide = jnp.zeros((count, LANES), F32)
    for i, column in enumerate(columns):
        wide = jnp.where(lane == i, column, wide)
    return jnp.transpose(wide)[:8]


def as_column(rows, which):
    full = jnp.concatenate([rows, jnp.zeros((LANES - 8, rows.shape[1]), F32)], axis=0)
    return jnp.transpose(full)[:, which : which + 1]


def table_kernel(gain, reward, rows, lengths, table):
    value = gain[...].astype(F32)
    table[0:1, :] = 1.0 / (value * value)
    table[1:2, :] = reward[...].astype(F32)


def pick_kernel(count, lengths, rows, sibling, extra, gain, near, after, full, near_out):
    section = lax.axis_index("section")
    core, pair = lax.rem(section, 2), lax.div(section, 2)
    positions, half = rows.shape[0], extra.shape[0]
    index = lax.broadcasted_iota(I32, (count, 1), 0)
    span, place = row_map(lengths, pair, core, index, count)
    source = jnp.where(span == section, place, place + positions)
    source = jnp.where(span // 2 == pair, source, place + (2 * positions - (positions - half)))
    lane = lax.broadcasted_iota(I32, (count, 2 * positions + half), 1)
    pick = jnp.where(lane == source, F32(1.0), F32(0.0)).astype(BF16)
    picked = jnp.dot(pick[:, :positions], rows[...], preferred_element_type=F32)
    picked += jnp.dot(pick[:, positions : 2 * positions], sibling[...], preferred_element_type=F32)
    picked += jnp.dot(pick[:, 2 * positions :], extra[...], preferred_element_type=F32)
    full[...] = (picked * gain[...].astype(F32)).astype(BF16)
    near_out[...] = near[...]


def token_kernel(count, lengths, tokens, out):
    core = lax.rem(lax.axis_index("section"), 2)
    spans, positions = tokens.shape
    for pair in range(2):
        index = lax.broadcasted_iota(I32, (count, 1), 0)
        span, place = row_map(lengths, pair, core, index, count)
        lane = lax.broadcasted_iota(I32, (count, positions), 1)
        found = jnp.zeros((count, positions), F32)
        for s in range(spans):
            found = jnp.where(span == s, tokens[s : s + 1, :].astype(F32), found)
        found = jnp.sum(jnp.where(lane == place, found, F32(0.0)), axis=1, keepdims=True)
        out[pair * count : pair * count + count, :] = found.astype(I32)


def here():
    section = lax.axis_index("section")
    return section, lax.rem(section, 2), lax.div(section, 2)


def blocks(count):
    _, _, pair = here()
    return pl.multiple_of(pair * count, 16), pl.multiple_of((1 - pair) * count, 16)


def weights(head, sibling, depth, k, far):
    dp_index = lax.axis_index("dp")
    where = jnp.bitwise_xor(dp_index, 2 * k + (1 if far else 0))
    rows = pl.ds(pl.multiple_of(where * depth, depth), depth)
    return head[rows, :], sibling[rows, :]


def products(terms):
    value = jnp.concatenate([t[0] for t in terms], axis=1) if len(terms) > 1 else terms[0][0]
    out = []
    for side in range(2):
        w = [t[1][side] for t in terms]
        w = jnp.concatenate(w, axis=0) if len(w) > 1 else w[0]
        out.append(jnp.dot(value, w, preferred_element_type=F32))
    return jnp.concatenate(out, axis=1)


def add_sides(terms, base, side_in, side):
    step = 32
    count, depth = terms[0][0].shape

    def body(i, _):
        rows = pl.ds(pl.multiple_of(i * step, step), step)
        at = pl.ds(pl.multiple_of(base + i * step, step), step)
        square, reward = jnp.zeros((step, LANES), F32), jnp.zeros((step, LANES), F32)
        if side_in is not None:
            square, reward = side_in[at, :LANES], side_in[at, LANES:]
        for piece, table, k in terms:
            for c in range(depth // LANES):
                cols = slice(c * LANES, (c + 1) * LANES)
                value = piece[rows, cols].astype(F32)
                square += value * value * table[k : k + 1, cols]
                reward += value * table[k + 4 : k + 5, cols]
        side[at, :LANES] = square
        side[at, LANES:] = reward
        return 0

    lax.fori_loop(0, count // step, body, 0)


def begin_kernel(head, sibling, near, far, z, a, b, c, z1, a1, b1, ids, acc, side, ids_out):
    count, depth = z.shape
    _, core, _ = here()
    mine, others = blocks(count)
    near0, far0 = weights(head, sibling, depth, 0, False), weights(head, sibling, depth, 0, True)
    near1, far1 = weights(head, sibling, depth, 1, False), weights(head, sibling, depth, 1, True)
    for which, same, cross, same1, cross1 in ((0, a, b, a1, b1), (1, b, a, b1, a1)):

        @pl.when(core == which)
        def _():
            rows = pl.ds(mine, count)
            acc[rows, :] = products([(z[...], near0), (same[...], far0), (z1[...], near1), (same1[...], far1)])
            add_sides([(z, near, 0), (same, far, 0), (z1, near, 1), (same1, far, 1)], mine, None, side)
            rows = pl.ds(others, count)
            acc[rows, :] = products([(cross[...], near0), (c[...], far0), (cross1[...], near1)])
            add_sides([(cross, near, 0), (c, far, 0), (cross1, near, 1)], others, None, side)

    ids_out[...] = ids[...]


def middle_kernel(head, sibling, near, far, acc_in, side_in, z, a, b, c, a2, acc, side, a2_out):
    count, depth = z.shape
    _, core, _ = here()
    mine, others = blocks(count)
    near3, far3 = weights(head, sibling, depth, 3, False), weights(head, sibling, depth, 3, True)
    for which, same, cross in ((0, a, b), (1, b, a)):

        @pl.when(core == which)
        def _():
            rows = pl.ds(mine, count)
            acc[rows, :] = acc_in[rows, :] + products([(z[...], near3), (same[...], far3)])
            add_sides([(z, near, 3), (same, far, 3)], mine, side_in, side)
            rows = pl.ds(others, count)
            acc[rows, :] = acc_in[rows, :] + products([(cross[...], near3), (c[...], far3)])
            add_sides([(cross, near, 3), (c, far, 3)], others, side_in, side)

    a2_out[...] = a2[...]


def gate_kernel(value, *refs):
    refs[-1][...] = value[...]


def column_ids(block):
    section, core, _ = here()
    dp_index, groups = lax.axis_index("dp"), lax.axis_size("dp")
    lane = lax.broadcasted_iota(I32, (1, block), 1)
    own = (section * groups + dp_index) * block
    other = ((section + 1 - 2 * core) * groups + dp_index) * block
    return jnp.concatenate([lane + own, lane + other], axis=1)


def summary(logits, square, reward, token_ids, ids, width):
    scale = lax.rsqrt(square / width + 1e-05)
    logits = logits * scale
    top = jnp.max(logits, axis=1, keepdims=True)
    total = jnp.sum(jnp.exp(logits - top), axis=1, keepdims=True)
    target = jnp.sum(jnp.where(ids == token_ids, logits, F32(0.0)), axis=1, keepdims=True)
    lane = lax.broadcasted_iota(I32, (logits.shape[0], LANES), 1)
    wide = jnp.where(lane == 2, target, jnp.where(lane == 3, reward * scale, F32(0.0)))
    return jnp.where(lane == 0, top, jnp.where(lane == 1, total, wide))


def added(side):
    return jnp.sum(side[:, :LANES], axis=1, keepdims=True), jnp.sum(side[:, LANES:], axis=1, keepdims=True)


def own_kernel(width, head, sibling, near, far, acc_in, side_in, z, a, b, c1, token_ids, left, left_side, far_out, wide, side):
    count, depth = z.shape
    _, core, _ = here()
    mine, others = blocks(count)
    near2, far2 = weights(head, sibling, depth, 2, False), weights(head, sibling, depth, 2, True)
    far1 = weights(head, sibling, depth, 1, True)
    block = head.shape[1]
    far_out[:, :block] = far2[0]
    far_out[:, block:] = far2[1]
    ids = column_ids(block)
    wide[...] = jnp.zeros(wide.shape, F32)
    for which, same, cross in ((0, a, b), (1, b, a)):

        @pl.when(core == which)
        def _():
            rows = pl.ds(mine, count)
            logits = acc_in[rows, :] + products([(z[...], near2), (same[...], far2)])
            add_sides([(z, near, 2), (same, far, 2)], mine, side_in, side)
            square, reward = added(side[rows, :])
            wide[rows, :] = summary(logits, square, reward, token_ids[rows, :], ids, width)
            rows = pl.ds(others, count)
            left[...] = acc_in[rows, :] + products([(cross[...], near2), (c1[...], far1)])
            add_sides([(cross, near, 2), (c1, far, 1)], others, side_in, side)
            left_side[...] = side[rows, :]


def last_kernel(width, far_weights, far, left, left_side, c, wide_in, token_ids, out, wide, side):
    count = c.shape[0]
    _, others = blocks(count)
    ids = column_ids(far_weights.shape[1] // 2)
    wide[...] = wide_in[...]
    logits = left[...] + jnp.dot(c[...], far_weights[...], preferred_element_type=F32)
    add_sides([(c, far, 2)], 0, left_side, side)
    square, reward = added(side[...])
    rows = pl.ds(others, count)
    wide[rows, :] = summary(logits, square, reward, token_ids[rows, :], ids, width)
    out[...] = jnp.transpose(wide[...])[:8]


def whole_kernel(width, acc, square, reward, token_ids, out):
    count = acc.shape[0] // 2
    ids = column_ids(acc.shape[1] // 2)
    wide = summary(acc[...], square[...], reward[...], token_ids[...], ids, width)
    wide = jnp.concatenate([wide, jnp.zeros((out.shape[1] - 2 * count, LANES), F32)])
    out[...] = jnp.transpose(wide)[:8]


def final_kernel(count, lengths, stats, out_ref, score_ref):
    section = lax.axis_index("section")
    positions = out_ref.shape[1]
    where = lax.broadcasted_iota(I32, (1, positions), 1)
    logprob = jnp.zeros((1, positions), F32)
    score = jnp.zeros((1, 1), F32)
    index = lax.broadcasted_iota(I32, (count, 1), 0)
    for core in range(2):
        columns = jnp.transpose(
            jnp.concatenate([stats[core], jnp.zeros((LANES - 8, stats.shape[2]), F32)], axis=0)
        )
        for pair in range(2):
            value = columns[pair * count : pair * count + count]
            span, place = row_map(lengths, pair, core, index, count)
            own = span == section
            logprob += jnp.sum(jnp.where((place == where) & own, value[:, 0:1], F32(0.0)), axis=0, keepdims=True)
            score += jnp.sum(jnp.where(own, value[:, 1:2], F32(0.0)), axis=0, keepdims=True)
    out_ref[...] = logprob
    score_ref[...] = score / lengths[section].astype(F32)


def combine(parts):
    top = parts[0][0]
    for part in parts[1:]:
        top = jnp.maximum(top, part[0])
    total = sum(part[1] * jnp.exp(part[0] - top) for part in parts)
    target = sum(part[2] for part in parts)
    return jnp.concatenate([jnp.stack([top, total, target, parts[0][3]]), jnp.zeros((4,) + top.shape, F32)])


def call(body, outs, in_specs, args, limit=16, scratch=()):
    many = isinstance(outs, (list, tuple))
    return pl.pallas_call(
        body,
        out_shape=outs,
        in_specs=in_specs,
        out_specs=[VMEM] * len(outs) if many else VMEM,
        scratch_shapes=scratch,
        compiler_params=pltpu.CompilerParams(vmem_limit_bytes=limit << 20),
    )(*args)


def up(value):
    return -(-value // LANES) * LANES


def per_device(groups, hidden, norm_gain, head, reward_head, tokens, lengths):
    section = lax.axis_index("section")
    core, pair = section % 2, section // 2
    sections = lax.axis_size("section")
    spans, positions = tokens.shape
    block, width, part = head.shape[1], head.shape[0], hidden.shape[2]
    count = 3 * spans * positions // 4 // sections
    half = positions // 2
    rows = hidden[0]

    def mesh_perm(move):
        pairs = []
        for s in range(sections):
            for d in range(groups):
                s2, d2 = move(s, d)
                pairs.append((s * groups + d, s2 * groups + d2))
        return pairs

    send = lambda value, perm: lax.ppermute(value, AXES, perm)
    like = lambda v: jax.ShapeDtypeStruct(v.shape, v.dtype)
    acc_shape = jax.ShapeDtypeStruct((2 * count, 2 * block), F32)
    stats_shape = jax.ShapeDtypeStruct((8, up(2 * count)), F32)
    ids_shape = jax.ShapeDtypeStruct((2 * count, 1), I32)
    perm_z = {k: mesh_perm(lambda s, d, k=k: (s, d ^ (2 * k))) for k in (1, 2, 3)}
    perm_x = mesh_perm(lambda s, d: (s, d ^ 1))
    gain = norm_gain[None]
    table = call(
        table_kernel, jax.ShapeDtypeStruct((2, part), F32), [VMEM] * 3 + [SMEM], (gain, reward_head[None], rows, lengths)
    )

    swap = [(s, s ^ 1) for s in range(sections)]
    over = [(s, s ^ 2) for s in range(sections)]
    extra = lax.ppermute(rows[half:], "section", [(1, 3), (3, 1)])
    sibling = lax.ppermute(rows, "section", swap)
    head_sibling = lax.ppermute(head, "section", swap)

    if groups == 8:
        tables = [table] + [send(table, perm_z[k]) for k in (1, 2, 3)]
        near = jnp.concatenate([t[i : i + 1] for i in range(2) for t in tables])
    else:
        near = jnp.concatenate([jnp.broadcast_to(table[i : i + 1], (4, part)) for i in range(2)])
    full, near = call(
        functools.partial(pick_kernel, count),
        [jax.ShapeDtypeStruct((count, part), BF16), like(near)],
        [SMEM] + [VMEM] * 5 + [ANY],
        (lengths, rows, sibling, extra, gain, near, head_sibling),
    )
    token_ids = call(functools.partial(token_kernel, count), ids_shape, [SMEM, VMEM], (lengths, tokens))

    if groups == 8:
        perm_a = mesh_perm(lambda s, d: (s, d ^ 1) if s % 2 == 0 else (s ^ 2, d))
        perm_b = mesh_perm(lambda s, d: (s ^ 2, d) if s % 2 == 0 else (s, d ^ 1))

        def gate(value, *after):
            return call(gate_kernel, like(value), [VMEM] + [ANY] * len(after), (value,) + after)

        side_shape = jax.ShapeDtypeStruct((2 * count, 2 * LANES), F32)
        z1 = send(full, perm_z[1])
        z3 = send(full, perm_z[3])
        a0 = send(full, perm_a)
        b0 = send(full, perm_b)
        far = send(near, perm_x)
        z1 = gate(z1, b0)
        a1 = send(z1, perm_a)
        b1 = send(z1, perm_b)
        c0 = send(a0, perm_b)
        z3 = gate(z3, a1, b1, c0, far)
        a3 = send(z3, perm_a)
        b3 = send(z3, perm_b)
        z2 = send(z3, perm_z[1])
        acc, side, token_ids = call(
            begin_kernel,
            [acc_shape, side_shape, ids_shape],
            [VMEM] * 12,
            (head, head_sibling, near, far, full, a0, b0, c0, z1, a1, b1, token_ids),
        )
        a3 = gate(a3, token_ids)
        c3 = send(a3, perm_b)
        a2 = send(z2, perm_a)
        b2 = send(z2, perm_b)
        c1 = send(c0, perm_z[1])
        acc, side, a2 = call(
            middle_kernel,
            [acc_shape, side_shape, like(a2)],
            [VMEM] * 11,
            (head, head_sibling, near, far, acc, side, z3, a3, b3, c3, a2),
        )
        c2 = send(a2, perm_b)
        left, left_side, far_weights, wide = call(
            functools.partial(own_kernel, width),
            [
                jax.ShapeDtypeStruct((count, 2 * block), F32),
                jax.ShapeDtypeStruct((count, 2 * LANES), F32),
                jax.ShapeDtypeStruct((part, 2 * block), BF16),
                jax.ShapeDtypeStruct((up(2 * count), LANES), F32),
            ],
            [VMEM] * 11,
            (head, head_sibling, near, far, acc, side, z2, a2, b2, c1, token_ids),
            scratch=[pltpu.VMEM((2 * count, 2 * LANES), F32)],
        )
        stats = call(
            functools.partial(last_kernel, width),
            stats_shape,
            [VMEM] * 7,
            (far_weights, far, left, left_side, c2, wide, token_ids),
            scratch=[pltpu.VMEM((up(2 * count), LANES), F32), pltpu.VMEM((count, 2 * LANES), F32)],
        )
        stats = combine([stats] + [send(stats, perm_z[k]) for k in (1, 2, 3)])
        stats = combine(
            [stats]
            + [send(stats, mesh_perm(lambda s, d, v=v: (s ^ v[0], d ^ v[1]))) for v in ((0, 1), (2, 0), (2, 1))]
        )
    else:
        other = lax.ppermute(full, "section", over)
        ordered = jnp.concatenate([jnp.where(pair == 0, full, other), jnp.where(pair == 0, other, full)])
        everything = lax.all_gather(ordered, "dp", axis=1, tiled=True)
        acc = jnp.concatenate(
            [jnp.dot(everything, h, preferred_element_type=F32) for h in (head, head_sibling)], axis=1
        )
        gains, weights_all = (lax.all_gather(t, "dp", axis=0, tiled=True) for t in table)
        wide = everything.astype(F32)
        square = jnp.sum(wide * wide * gains, axis=1, keepdims=True)
        reward = jnp.sum(wide * weights_all, axis=1, keepdims=True)
        stats = call(
            functools.partial(whole_kernel, width), stats_shape, [VMEM] * 4, (acc, square, reward, token_ids)
        )
        gathered = lax.all_gather(stats, "dp")
        stats = combine([gathered[i] for i in range(groups)])
        stats = combine([stats, lax.ppermute(stats, "section", over)])
    lp = stats[2:3] - (stats[0:1] + jnp.log(stats[1:2]))
    lp = jnp.concatenate([lp, stats[3:4], jnp.zeros((6, lp.shape[1]), F32)])
    both = lambda v, u: jnp.stack([jnp.where(core == 0, v, u), jnp.where(core == 0, u, v)])
    stats = both(lp, lax.ppermute(lp, "section", swap))
    logprob, score = call(
        functools.partial(final_kernel, count),
        [jax.ShapeDtypeStruct((1, positions), F32), jax.ShapeDtypeStruct((1, 1), F32)],
        [SMEM, VMEM],
        (lengths, stats),
    )
    return (logprob, score[0])


def solution(mesh):
    groups = mesh.shape["dp"]
    return jax.shard_map(
        lambda *args: per_device(groups, *args),
        mesh=mesh,
        in_specs=(P("section", None, "dp"), P("dp"), P(None, ("section", "dp")), P("dp"), P(), P()),
        out_specs=(P("section", None), P("section")),
        check_vma=False,
    )
```

```python
import functools

import jax
import jax.numpy as jnp
from jax import lax
from jax.experimental import pallas as pl
from jax.experimental.pallas import tpu as pltpu
from jax.sharding import PartitionSpec as P

AXES = ("section", "dp")
F32 = jnp.float32
BF16 = jnp.bfloat16
I32 = jnp.int32
LANES = 128
VMEM = pl.BlockSpec(memory_space=pltpu.VMEM)
SMEM = pl.BlockSpec(memory_space=pltpu.SMEM)
ANY = pl.BlockSpec(memory_space=pl.ANY)


def row_map(lengths, pair, core, index, count):
    first, second = lengths[2 * pair], lengths[2 * pair + 1]
    other_first = lengths[2 - 2 * pair]
    j = core * count + index
    in_first = j < first
    in_second = j < first + second
    span = jnp.where(in_first, 2 * pair, jnp.where(in_second, 2 * pair + 1, 3 - 2 * pair))
    place = jnp.where(
        in_first, j, jnp.where(in_second, j - first, 2 * count - other_first + j - first - second)
    )
    return span, place


def as_rows(columns, count):
    lane = lax.broadcasted_iota(I32, (count, LANES), 1)
    wide = jnp.zeros((count, LANES), F32)
    for i, column in enumerate(columns):
        wide = jnp.where(lane == i, column, wide)
    return jnp.transpose(wide)[:8]


def as_column(rows, which):
    full = jnp.concatenate([rows, jnp.zeros((LANES - 8, rows.shape[1]), F32)], axis=0)
    return jnp.transpose(full)[:, which : which + 1]


def table_kernel(gain, reward, rows, table, rows_out):
    rows_out[...] = rows[...]
    value = gain[...].astype(F32)
    table[0:1, :] = 1.0 / (value * value)
    table[1:2, :] = reward[...].astype(F32)


def pick_kernel(count, lengths, rows, sibling, extra, gain, near, after, full, near_out):
    section = lax.axis_index("section")
    core, pair = lax.rem(section, 2), lax.div(section, 2)
    positions, half = rows.shape[0], extra.shape[0]
    index = lax.broadcasted_iota(I32, (count, 1), 0)
    span, place = row_map(lengths, pair, core, index, count)
    source = jnp.where(span == section, place, place + positions)
    source = jnp.where(span // 2 == pair, source, place + (2 * positions - (positions - half)))
    lane = lax.broadcasted_iota(I32, (count, 2 * positions + half), 1)
    pick = jnp.where(lane == source, F32(1.0), F32(0.0)).astype(BF16)
    picked = jnp.dot(pick[:, :positions], rows[...], preferred_element_type=F32)
    picked += jnp.dot(pick[:, positions : 2 * positions], sibling[...], preferred_element_type=F32)
    picked += jnp.dot(pick[:, 2 * positions :], extra[...], preferred_element_type=F32)
    full[...] = (picked * gain[...].astype(F32)).astype(BF16)
    near_out[...] = near[...]


def token_kernel(count, lengths, tokens, out):
    core = lax.rem(lax.axis_index("section"), 2)
    spans, positions = tokens.shape
    for pair in range(2):
        index = lax.broadcasted_iota(I32, (count, 1), 0)
        span, place = row_map(lengths, pair, core, index, count)
        lane = lax.broadcasted_iota(I32, (count, positions), 1)
        found = jnp.zeros((count, positions), F32)
        for s in range(spans):
            found = jnp.where(span == s, tokens[s : s + 1, :].astype(F32), found)
        found = jnp.sum(jnp.where(lane == place, found, F32(0.0)), axis=1, keepdims=True)
        out[pair * count : pair * count + count, :] = found.astype(I32)


def here():
    section = lax.axis_index("section")
    return section, lax.rem(section, 2), lax.div(section, 2)


def blocks(count):
    _, _, pair = here()
    return pl.multiple_of(pair * count, 16), pl.multiple_of((1 - pair) * count, 16)


def weights(head, sibling, depth, k, far):
    dp_index = lax.axis_index("dp")
    where = jnp.bitwise_xor(dp_index, 2 * k + (1 if far else 0))
    rows = pl.ds(pl.multiple_of(where * depth, depth), depth)
    return head[rows, :], sibling[rows, :]


def products(terms):
    value = jnp.concatenate([t[0] for t in terms], axis=1) if len(terms) > 1 else terms[0][0]
    out = []
    for side in range(2):
        w = [t[1][side] for t in terms]
        w = jnp.concatenate(w, axis=0) if len(w) > 1 else w[0]
        out.append(jnp.dot(value, w, preferred_element_type=F32))
    return jnp.concatenate(out, axis=1)


def add_sides(terms, base, side_in, side):
    step = 32
    count, depth = terms[0][0].shape

    def body(i, _):
        rows = pl.ds(pl.multiple_of(i * step, step), step)
        at = pl.ds(pl.multiple_of(base + i * step, step), step)
        square, reward = jnp.zeros((step, LANES), F32), jnp.zeros((step, LANES), F32)
        if side_in is not None:
            square, reward = side_in[at, :LANES], side_in[at, LANES:]
        for piece, table, k in terms:
            for c in range(depth // LANES):
                cols = slice(c * LANES, (c + 1) * LANES)
                value = piece[rows, cols].astype(F32)
                square += value * value * table[2 * k : 2 * k + 1, cols]
                reward += value * table[2 * k + 1 : 2 * k + 2, cols]
        side[at, :LANES] = square
        side[at, LANES:] = reward
        return 0

    lax.fori_loop(0, count // step, body, 0)


def begin_kernel(head, sibling, near, far, z, a, b, c, z1, a1, b1, ids, acc, side, ids_out):
    count, depth = z.shape
    _, core, _ = here()
    mine, others = blocks(count)
    near0, far0 = weights(head, sibling, depth, 0, False), weights(head, sibling, depth, 0, True)
    near1, far1 = weights(head, sibling, depth, 1, False), weights(head, sibling, depth, 1, True)
    for which, same, cross, same1, cross1 in ((0, a, b, a1, b1), (1, b, a, b1, a1)):

        @pl.when(core == which)
        def _():
            rows = pl.ds(mine, count)
            acc[rows, :] = products([(z[...], near0), (same[...], far0), (z1[...], near1), (same1[...], far1)])
            add_sides([(z, near, 0), (same, far, 0), (z1, near, 1), (same1, far, 1)], mine, None, side)
            rows = pl.ds(others, count)
            acc[rows, :] = products([(cross[...], near0), (c[...], far0), (cross1[...], near1)])
            add_sides([(cross, near, 0), (c, far, 0), (cross1, near, 1)], others, None, side)

    ids_out[...] = ids[...]


def middle_kernel(head, sibling, near, far, acc_in, side_in, z, a, b, c, acc, side):
    count, depth = z.shape
    _, core, _ = here()
    mine, others = blocks(count)
    near3, far3 = weights(head, sibling, depth, 3, False), weights(head, sibling, depth, 3, True)
    for which, same, cross in ((0, a, b), (1, b, a)):

        @pl.when(core == which)
        def _():
            rows = pl.ds(mine, count)
            acc[rows, :] = acc_in[rows, :] + products([(z[...], near3), (same[...], far3)])
            add_sides([(z, near, 3), (same, far, 3)], mine, side_in, side)
            rows = pl.ds(others, count)
            acc[rows, :] = acc_in[rows, :] + products([(cross[...], near3), (c[...], far3)])
            add_sides([(cross, near, 3), (c, far, 3)], others, side_in, side)


def gate_kernel(value, *refs):
    refs[-1][...] = value[...]


def column_ids(block):
    section, core, _ = here()
    dp_index, groups = lax.axis_index("dp"), lax.axis_size("dp")
    lane = lax.broadcasted_iota(I32, (1, block), 1)
    own = (section * groups + dp_index) * block
    other = ((section + 1 - 2 * core) * groups + dp_index) * block
    return jnp.concatenate([lane + own, lane + other], axis=1)


def summary(logits, square, reward, token_ids, ids, width):
    scale = lax.rsqrt(square / width + 1e-05)
    logits = logits * scale
    top = jnp.max(logits, axis=1, keepdims=True)
    total = jnp.sum(jnp.exp(logits - top), axis=1, keepdims=True)
    target = jnp.sum(jnp.where(ids == token_ids, logits, F32(0.0)), axis=1, keepdims=True)
    lane = lax.broadcasted_iota(I32, (logits.shape[0], LANES), 1)
    wide = jnp.where(lane == 2, target, jnp.where(lane == 3, reward * scale, F32(0.0)))
    return jnp.where(lane == 0, top, jnp.where(lane == 1, total, wide))


def added(side):
    return jnp.sum(side[:, :LANES], axis=1, keepdims=True), jnp.sum(side[:, LANES:], axis=1, keepdims=True)


def own_kernel(width, head, sibling, near, far, acc_in, side_in, z, a, b, c1, token_ids, left, left_side, far_out, wide, side):
    count, depth = z.shape
    _, core, _ = here()
    mine, others = blocks(count)
    near2, far2 = weights(head, sibling, depth, 2, False), weights(head, sibling, depth, 2, True)
    far1 = weights(head, sibling, depth, 1, True)
    block = head.shape[1]
    far_out[:, :block] = far2[0]
    far_out[:, block:] = far2[1]
    ids = column_ids(block)
    wide[...] = jnp.zeros(wide.shape, F32)
    for which, same, cross in ((0, a, b), (1, b, a)):

        @pl.when(core == which)
        def _():
            rows = pl.ds(mine, count)
            logits = acc_in[rows, :] + products([(z[...], near2), (same[...], far2)])
            add_sides([(z, near, 2), (same, far, 2)], mine, side_in, side)
            square, reward = added(side[rows, :])
            wide[rows, :] = summary(logits, square, reward, token_ids[rows, :], ids, width)
            rows = pl.ds(others, count)
            left[...] = acc_in[rows, :] + products([(cross[...], near2), (c1[...], far1)])
            add_sides([(cross, near, 2), (c1, far, 1)], others, side_in, side)
            left_side[...] = side[rows, :]


def last_kernel(width, far_weights, far, left, left_side, c, wide_in, token_ids, out, wide, side):
    count = c.shape[0]
    _, others = blocks(count)
    ids = column_ids(far_weights.shape[1] // 2)
    wide[...] = wide_in[...]
    logits = left[...] + jnp.dot(c[...], far_weights[...], preferred_element_type=F32)
    add_sides([(c, far, 2)], 0, left_side, side)
    square, reward = added(side[...])
    rows = pl.ds(others, count)
    wide[rows, :] = summary(logits, square, reward, token_ids[rows, :], ids, width)
    out[...] = jnp.transpose(wide[...])[:8]


def whole_kernel(width, acc, square, reward, token_ids, out):
    count = acc.shape[0] // 2
    ids = column_ids(acc.shape[1] // 2)
    wide = summary(acc[...], square[...], reward[...], token_ids[...], ids, width)
    wide = jnp.concatenate([wide, jnp.zeros((out.shape[1] - 2 * count, LANES), F32)])
    out[...] = jnp.transpose(wide)[:8]


def final_kernel(count, lengths, stats, out_ref, score_ref):
    section = lax.axis_index("section")
    positions = out_ref.shape[1]
    where = lax.broadcasted_iota(I32, (1, positions), 1)
    logprob = jnp.zeros((1, positions), F32)
    score = jnp.zeros((1, 1), F32)
    index = lax.broadcasted_iota(I32, (count, 1), 0)
    for core in range(2):
        columns = jnp.transpose(
            jnp.concatenate([stats[core], jnp.zeros((LANES - 8, stats.shape[2]), F32)], axis=0)
        )
        for pair in range(2):
            value = columns[pair * count : pair * count + count]
            span, place = row_map(lengths, pair, core, index, count)
            own = span == section
            logprob += jnp.sum(jnp.where((place == where) & own, value[:, 0:1], F32(0.0)), axis=0, keepdims=True)
            score += jnp.sum(jnp.where(own, value[:, 1:2], F32(0.0)), axis=0, keepdims=True)
    out_ref[...] = logprob
    score_ref[...] = score / lengths[section].astype(F32)


def combine(parts):
    top = parts[0][0]
    for part in parts[1:]:
        top = jnp.maximum(top, part[0])
    total = sum(part[1] * jnp.exp(part[0] - top) for part in parts)
    target = sum(part[2] for part in parts)
    return jnp.concatenate([jnp.stack([top, total, target, parts[0][3]]), jnp.zeros((4,) + top.shape, F32)])


def call(body, outs, in_specs, args, limit=16, scratch=()):
    many = isinstance(outs, (list, tuple))
    return pl.pallas_call(
        body,
        out_shape=outs,
        in_specs=in_specs,
        out_specs=[VMEM] * len(outs) if many else VMEM,
        scratch_shapes=scratch,
        compiler_params=pltpu.CompilerParams(vmem_limit_bytes=limit << 20),
    )(*args)


def up(value):
    return -(-value // LANES) * LANES


def per_device(groups, hidden, norm_gain, head, reward_head, tokens, lengths):
    section = lax.axis_index("section")
    core, pair = section % 2, section // 2
    sections = lax.axis_size("section")
    spans, positions = tokens.shape
    block, width, part = head.shape[1], head.shape[0], hidden.shape[2]
    count = 3 * spans * positions // 4 // sections
    half = positions // 2
    rows = hidden[0]

    def mesh_perm(move):
        pairs = []
        for s in range(sections):
            for d in range(groups):
                s2, d2 = move(s, d)
                pairs.append((s * groups + d, s2 * groups + d2))
        return pairs

    send = lambda value, perm: lax.ppermute(value, AXES, perm)
    like = lambda v: jax.ShapeDtypeStruct(v.shape, v.dtype)
    acc_shape = jax.ShapeDtypeStruct((2 * count, 2 * block), F32)
    stats_shape = jax.ShapeDtypeStruct((8, up(2 * count)), F32)
    ids_shape = jax.ShapeDtypeStruct((2 * count, 1), I32)
    perm_z = {k: mesh_perm(lambda s, d, k=k: (s, d ^ (2 * k))) for k in (1, 2, 3)}
    perm_x = mesh_perm(lambda s, d: (s, d ^ 1))
    gain = norm_gain[None]

    swap = [(s, s ^ 1) for s in range(sections)]
    over = [(s, s ^ 2) for s in range(sections)]
    extra = lax.ppermute(rows[half:], "section", [(1, 3), (3, 1)])
    sibling = lax.ppermute(rows, "section", swap)
    head_sibling = lax.ppermute(head, "section", swap)
    table, rows = call(
        table_kernel, [jax.ShapeDtypeStruct((2, part), F32), like(rows)], [VMEM] * 3, (gain, reward_head[None], rows)
    )

    if groups == 8:
        near = jnp.concatenate([table, send(table, perm_z[1])])
        near = jnp.concatenate([near, send(near, perm_z[2])])
    else:
        near = jnp.concatenate([table] * 4)
    full, near = call(
        functools.partial(pick_kernel, count),
        [jax.ShapeDtypeStruct((count, part), BF16), like(near)],
        [SMEM] + [VMEM] * 5 + [ANY],
        (lengths, rows, sibling, extra, gain, near, head_sibling),
    )
    token_ids = call(functools.partial(token_kernel, count), ids_shape, [SMEM, VMEM], (lengths, tokens))

    if groups == 8:
        perm_a = mesh_perm(lambda s, d: (s, d ^ 1) if s % 2 == 0 else (s ^ 2, d))
        perm_b = mesh_perm(lambda s, d: (s ^ 2, d) if s % 2 == 0 else (s, d ^ 1))

        def gate(value, *after):
            return call(gate_kernel, like(value), [VMEM] + [ANY] * len(after), (value,) + after)

        side_shape = jax.ShapeDtypeStruct((2 * count, 2 * LANES), F32)
        z1 = send(full, perm_z[1])
        z3 = send(full, perm_z[3])
        a0 = send(full, perm_a)
        b0 = send(full, perm_b)
        far = send(near, perm_x)
        z1 = gate(z1, b0)
        a1 = send(z1, perm_a)
        b1 = send(z1, perm_b)
        c0 = send(a0, perm_b)
        z3 = gate(z3, a1, b1, c0, far)
        a3 = send(z3, perm_a)
        b3 = send(z3, perm_b)
        z2 = send(z3, perm_z[1])
        acc, side, token_ids = call(
            begin_kernel,
            [acc_shape, side_shape, ids_shape],
            [VMEM] * 12,
            (head, head_sibling, near, far, full, a0, b0, c0, z1, a1, b1, token_ids),
        )
        a3 = gate(a3, token_ids)
        c3 = send(a3, perm_b)
        a2 = send(z2, perm_a)
        b2 = send(z2, perm_b)
        c1 = send(c0, perm_z[1])
        acc, side = call(
            middle_kernel,
            [acc_shape, side_shape],
            [VMEM] * 10,
            (head, head_sibling, near, far, acc, side, z3, a3, b3, c3),
        )
        a2 = gate(a2, side)
        c2 = send(a2, perm_b)
        left, left_side, far_weights, wide = call(
            functools.partial(own_kernel, width),
            [
                jax.ShapeDtypeStruct((count, 2 * block), F32),
                jax.ShapeDtypeStruct((count, 2 * LANES), F32),
                jax.ShapeDtypeStruct((part, 2 * block), BF16),
                jax.ShapeDtypeStruct((up(2 * count), LANES), F32),
            ],
            [VMEM] * 11,
            (head, head_sibling, near, far, acc, side, z2, a2, b2, c1, token_ids),
            scratch=[pltpu.VMEM((2 * count, 2 * LANES), F32)],
        )
        stats = call(
            functools.partial(last_kernel, width),
            stats_shape,
            [VMEM] * 7,
            (far_weights, far, left, left_side, c2, wide, token_ids),
            scratch=[pltpu.VMEM((up(2 * count), LANES), F32), pltpu.VMEM((count, 2 * LANES), F32)],
        )
        stats = combine([stats] + [send(stats, perm_z[k]) for k in (1, 2, 3)])
        stats = combine(
            [stats]
            + [send(stats, mesh_perm(lambda s, d, v=v: (s ^ v[0], d ^ v[1]))) for v in ((0, 1), (2, 0), (2, 1))]
        )
    else:
        other = lax.ppermute(full, "section", over)
        ordered = jnp.concatenate([jnp.where(pair == 0, full, other), jnp.where(pair == 0, other, full)])
        everything = lax.all_gather(ordered, "dp", axis=1, tiled=True)
        acc = jnp.concatenate(
            [jnp.dot(everything, h, preferred_element_type=F32) for h in (head, head_sibling)], axis=1
        )
        gains, weights_all = (lax.all_gather(t, "dp", axis=0, tiled=True) for t in table)
        wide = everything.astype(F32)
        square = jnp.sum(wide * wide * gains, axis=1, keepdims=True)
        reward = jnp.sum(wide * weights_all, axis=1, keepdims=True)
        stats = call(
            functools.partial(whole_kernel, width), stats_shape, [VMEM] * 4, (acc, square, reward, token_ids)
        )
        gathered = lax.all_gather(stats, "dp")
        stats = combine([gathered[i] for i in range(groups)])
        stats = combine([stats, lax.ppermute(stats, "section", over)])
    lp = stats[2:3] - (stats[0:1] + jnp.log(stats[1:2]))
    lp = jnp.concatenate([lp, stats[3:4], jnp.zeros((6, lp.shape[1]), F32)])
    both = lambda v, u: jnp.stack([jnp.where(core == 0, v, u), jnp.where(core == 0, u, v)])
    stats = both(lp, lax.ppermute(lp, "section", swap))
    logprob, score = call(
        functools.partial(final_kernel, count),
        [jax.ShapeDtypeStruct((1, positions), F32), jax.ShapeDtypeStruct((1, 1), F32)],
        [SMEM, VMEM],
        (lengths, stats),
    )
    return (logprob, score[0])


def solution(mesh):
    groups = mesh.shape["dp"]
    return jax.shard_map(
        lambda *args: per_device(groups, *args),
        mesh=mesh,
        in_specs=(P("section", None, "dp"), P("dp"), P(None, ("section", "dp")), P("dp"), P(), P()),
        out_specs=(P("section", None), P("section")),
        check_vma=False,
    )
```

```python
import functools

import jax
import jax.numpy as jnp
from jax import lax
from jax.experimental import pallas as pl
from jax.experimental.pallas import tpu as pltpu
from jax.sharding import PartitionSpec as P

AXES = ("section", "dp")
F32 = jnp.float32
BF16 = jnp.bfloat16
I32 = jnp.int32
LANES = 128
VMEM = pl.BlockSpec(memory_space=pltpu.VMEM)
SMEM = pl.BlockSpec(memory_space=pltpu.SMEM)
ANY = pl.BlockSpec(memory_space=pl.ANY)


def row_map(lengths, pair, core, index, count):
    first, second = lengths[2 * pair], lengths[2 * pair + 1]
    other_first = lengths[2 - 2 * pair]
    j = core * count + index
    in_first = j < first
    in_second = j < first + second
    span = jnp.where(in_first, 2 * pair, jnp.where(in_second, 2 * pair + 1, 3 - 2 * pair))
    place = jnp.where(
        in_first, j, jnp.where(in_second, j - first, 2 * count - other_first + j - first - second)
    )
    return span, place


def as_rows(columns, count):
    lane = lax.broadcasted_iota(I32, (count, LANES), 1)
    wide = jnp.zeros((count, LANES), F32)
    for i, column in enumerate(columns):
        wide = jnp.where(lane == i, column, wide)
    return jnp.transpose(wide)[:8]


def as_column(rows, which):
    full = jnp.concatenate([rows, jnp.zeros((LANES - 8, rows.shape[1]), F32)], axis=0)
    return jnp.transpose(full)[:, which : which + 1]


def table_kernel(gain, reward, rows, table, rows_out):
    rows_out[...] = rows[...]
    value = gain[...].astype(F32)
    table[0:1, :] = 1.0 / (value * value)
    table[1:2, :] = reward[...].astype(F32)


def pick_kernel(count, lengths, rows, sibling, extra, gain, near, after, full, near_out):
    section = lax.axis_index("section")
    core, pair = lax.rem(section, 2), lax.div(section, 2)
    positions, half = rows.shape[0], extra.shape[0]
    index = lax.broadcasted_iota(I32, (count, 1), 0)
    span, place = row_map(lengths, pair, core, index, count)
    source = jnp.where(span == section, place, place + positions)
    source = jnp.where(span // 2 == pair, source, place + (2 * positions - (positions - half)))
    lane = lax.broadcasted_iota(I32, (count, 2 * positions + half), 1)
    pick = jnp.where(lane == source, F32(1.0), F32(0.0)).astype(BF16)
    picked = jnp.dot(pick[:, :positions], rows[...], preferred_element_type=F32)
    picked += jnp.dot(pick[:, positions : 2 * positions], sibling[...], preferred_element_type=F32)
    picked += jnp.dot(pick[:, 2 * positions :], extra[...], preferred_element_type=F32)
    full[...] = (picked * gain[...].astype(F32)).astype(BF16)
    near_out[...] = near[...]


def token_kernel(count, lengths, tokens, out):
    core = lax.rem(lax.axis_index("section"), 2)
    spans, positions = tokens.shape
    for pair in range(2):
        index = lax.broadcasted_iota(I32, (count, 1), 0)
        span, place = row_map(lengths, pair, core, index, count)
        lane = lax.broadcasted_iota(I32, (count, positions), 1)
        found = jnp.zeros((count, positions), F32)
        for s in range(spans):
            found = jnp.where(span == s, tokens[s : s + 1, :].astype(F32), found)
        found = jnp.sum(jnp.where(lane == place, found, F32(0.0)), axis=1, keepdims=True)
        out[pair * count : pair * count + count, :] = found.astype(I32)


def here():
    section = lax.axis_index("section")
    return section, lax.rem(section, 2), lax.div(section, 2)


def blocks(count):
    _, _, pair = here()
    return pl.multiple_of(pair * count, 16), pl.multiple_of((1 - pair) * count, 16)


def weights(head, sibling, depth, k, far):
    dp_index = lax.axis_index("dp")
    where = jnp.bitwise_xor(dp_index, 2 * k + (1 if far else 0))
    rows = pl.ds(pl.multiple_of(where * depth, depth), depth)
    return head[rows, :], sibling[rows, :]


def products(terms):
    value = jnp.concatenate([t[0] for t in terms], axis=1) if len(terms) > 1 else terms[0][0]
    out = []
    for side in range(2):
        w = [t[1][side] for t in terms]
        w = jnp.concatenate(w, axis=0) if len(w) > 1 else w[0]
        out.append(jnp.dot(value, w, preferred_element_type=F32))
    return jnp.concatenate(out, axis=1)


def add_sides(terms, base, side_in, side):
    step = 32
    count, depth = terms[0][0].shape

    def body(i, _):
        rows = pl.ds(pl.multiple_of(i * step, step), step)
        at = pl.ds(pl.multiple_of(base + i * step, step), step)
        square, reward = jnp.zeros((step, LANES), F32), jnp.zeros((step, LANES), F32)
        if side_in is not None:
            square, reward = side_in[at, :LANES], side_in[at, LANES:]
        for piece, table, k in terms:
            for c in range(depth // LANES):
                cols = slice(c * LANES, (c + 1) * LANES)
                value = piece[rows, cols].astype(F32)
                square += value * value * table[2 * k : 2 * k + 1, cols]
                reward += value * table[2 * k + 1 : 2 * k + 2, cols]
        side[at, :LANES] = square
        side[at, LANES:] = reward
        return 0

    lax.fori_loop(0, count // step, body, 0)


def both_weights(head, sibling, depth, k):
    return weights(head, sibling, depth, k, False), weights(head, sibling, depth, k, True)


def begin_kernel(head, sibling, near, far, z, a, b, c, z1, a1, b1, ids, acc, side, ids_out):
    count, depth = z.shape
    _, core, _ = here()
    mine, others = blocks(count)
    near0, far0 = both_weights(head, sibling, depth, 0)
    for which, k, same, cross, same1, cross1 in ((0, 1, a, b, a1, b1), (1, 3, b, a, b1, a1)):

        @pl.when(core == which)
        def _():
            near1, far1 = both_weights(head, sibling, depth, k)
            rows = pl.ds(mine, count)
            acc[rows, :] = products([(z[...], near0), (same[...], far0), (z1[...], near1), (same1[...], far1)])
            add_sides([(z, near, 0), (same, far, 0), (z1, near, k), (same1, far, k)], mine, None, side)
            rows = pl.ds(others, count)
            acc[rows, :] = products([(cross[...], near0), (c[...], far0), (cross1[...], near1)])
            add_sides([(cross, near, 0), (c, far, 0), (cross1, near, k)], others, None, side)

    ids_out[...] = ids[...]


def middle_kernel(head, sibling, near, far, acc_in, side_in, z, a, b, c, acc, side):
    count, depth = z.shape
    _, core, _ = here()
    mine, others = blocks(count)
    for which, k, same, cross in ((0, 3, a, b), (1, 1, b, a)):

        @pl.when(core == which)
        def _():
            near3, far3 = both_weights(head, sibling, depth, k)
            rows = pl.ds(mine, count)
            acc[rows, :] = acc_in[rows, :] + products([(z[...], near3), (same[...], far3)])
            add_sides([(z, near, k), (same, far, k)], mine, side_in, side)
            rows = pl.ds(others, count)
            acc[rows, :] = acc_in[rows, :] + products([(cross[...], near3), (c[...], far3)])
            add_sides([(cross, near, k), (c, far, k)], others, side_in, side)


def gate_kernel(value, *refs):
    refs[-1][...] = value[...]


def column_ids(block):
    section, core, _ = here()
    dp_index, groups = lax.axis_index("dp"), lax.axis_size("dp")
    lane = lax.broadcasted_iota(I32, (1, block), 1)
    own = (section * groups + dp_index) * block
    other = ((section + 1 - 2 * core) * groups + dp_index) * block
    return jnp.concatenate([lane + own, lane + other], axis=1)


def summary(logits, square, reward, token_ids, ids, width):
    scale = lax.rsqrt(square / width + 1e-05)
    logits = logits * scale
    top = jnp.max(logits, axis=1, keepdims=True)
    total = jnp.sum(jnp.exp(logits - top), axis=1, keepdims=True)
    target = jnp.sum(jnp.where(ids == token_ids, logits, F32(0.0)), axis=1, keepdims=True)
    lane = lax.broadcasted_iota(I32, (logits.shape[0], LANES), 1)
    wide = jnp.where(lane == 2, target, jnp.where(lane == 3, reward * scale, F32(0.0)))
    return jnp.where(lane == 0, top, jnp.where(lane == 1, total, wide))


def added(side):
    return jnp.sum(side[:, :LANES], axis=1, keepdims=True), jnp.sum(side[:, LANES:], axis=1, keepdims=True)


def own_kernel(width, head, sibling, near, far, acc_in, side_in, z, a, b, c1, token_ids, left, left_side, far_out, wide, side):
    count, depth = z.shape
    _, core, _ = here()
    mine, others = blocks(count)
    near2, far2 = weights(head, sibling, depth, 2, False), weights(head, sibling, depth, 2, True)
    block = head.shape[1]
    far_out[:, :block] = far2[0]
    far_out[:, block:] = far2[1]
    ids = column_ids(block)
    wide[...] = jnp.zeros(wide.shape, F32)
    for which, k, same, cross in ((0, 1, a, b), (1, 3, b, a)):

        @pl.when(core == which)
        def _():
            far1 = weights(head, sibling, depth, k, True)
            rows = pl.ds(mine, count)
            logits = acc_in[rows, :] + products([(z[...], near2), (same[...], far2)])
            add_sides([(z, near, 2), (same, far, 2)], mine, side_in, side)
            square, reward = added(side[rows, :])
            wide[rows, :] = summary(logits, square, reward, token_ids[rows, :], ids, width)
            rows = pl.ds(others, count)
            left[...] = acc_in[rows, :] + products([(cross[...], near2), (c1[...], far1)])
            add_sides([(cross, near, 2), (c1, far, k)], others, side_in, side)
            left_side[...] = side[rows, :]


def last_kernel(width, far_weights, far, left, left_side, c, wide_in, token_ids, out, wide, side):
    count = c.shape[0]
    _, others = blocks(count)
    ids = column_ids(far_weights.shape[1] // 2)
    wide[...] = wide_in[...]
    logits = left[...] + jnp.dot(c[...], far_weights[...], preferred_element_type=F32)
    add_sides([(c, far, 2)], 0, left_side, side)
    square, reward = added(side[...])
    rows = pl.ds(others, count)
    wide[rows, :] = summary(logits, square, reward, token_ids[rows, :], ids, width)
    out[...] = jnp.transpose(wide[...])[:8]


def whole_kernel(width, acc, square, reward, token_ids, out):
    count = acc.shape[0] // 2
    ids = column_ids(acc.shape[1] // 2)
    wide = summary(acc[...], square[...], reward[...], token_ids[...], ids, width)
    wide = jnp.concatenate([wide, jnp.zeros((out.shape[1] - 2 * count, LANES), F32)])
    out[...] = jnp.transpose(wide)[:8]


def final_kernel(count, lengths, stats, out_ref, score_ref):
    section = lax.axis_index("section")
    positions = out_ref.shape[1]
    where = lax.broadcasted_iota(I32, (1, positions), 1)
    logprob = jnp.zeros((1, positions), F32)
    score = jnp.zeros((1, 1), F32)
    index = lax.broadcasted_iota(I32, (count, 1), 0)
    for core in range(2):
        columns = jnp.transpose(
            jnp.concatenate([stats[core], jnp.zeros((LANES - 8, stats.shape[2]), F32)], axis=0)
        )
        for pair in range(2):
            value = columns[pair * count : pair * count + count]
            span, place = row_map(lengths, pair, core, index, count)
            own = span == section
            logprob += jnp.sum(jnp.where((place == where) & own, value[:, 0:1], F32(0.0)), axis=0, keepdims=True)
            score += jnp.sum(jnp.where(own, value[:, 1:2], F32(0.0)), axis=0, keepdims=True)
    out_ref[...] = logprob
    score_ref[...] = score / lengths[section].astype(F32)


def combine(parts):
    top = parts[0][0]
    for part in parts[1:]:
        top = jnp.maximum(top, part[0])
    total = sum(part[1] * jnp.exp(part[0] - top) for part in parts)
    target = sum(part[2] for part in parts)
    return jnp.concatenate([jnp.stack([top, total, target, parts[0][3]]), jnp.zeros((4,) + top.shape, F32)])


def call(body, outs, in_specs, args, limit=16, scratch=()):
    many = isinstance(outs, (list, tuple))
    return pl.pallas_call(
        body,
        out_shape=outs,
        in_specs=in_specs,
        out_specs=[VMEM] * len(outs) if many else VMEM,
        scratch_shapes=scratch,
        compiler_params=pltpu.CompilerParams(vmem_limit_bytes=limit << 20),
    )(*args)


def up(value):
    return -(-value // LANES) * LANES


def per_device(groups, hidden, norm_gain, head, reward_head, tokens, lengths):
    section = lax.axis_index("section")
    core, pair = section % 2, section // 2
    sections = lax.axis_size("section")
    spans, positions = tokens.shape
    block, width, part = head.shape[1], head.shape[0], hidden.shape[2]
    count = 3 * spans * positions // 4 // sections
    half = positions // 2
    rows = hidden[0]

    def mesh_perm(move):
        pairs = []
        for s in range(sections):
            for d in range(groups):
                s2, d2 = move(s, d)
                pairs.append((s * groups + d, s2 * groups + d2))
        return pairs

    send = lambda value, perm: lax.ppermute(value, AXES, perm)
    like = lambda v: jax.ShapeDtypeStruct(v.shape, v.dtype)
    acc_shape = jax.ShapeDtypeStruct((2 * count, 2 * block), F32)
    stats_shape = jax.ShapeDtypeStruct((8, up(2 * count)), F32)
    ids_shape = jax.ShapeDtypeStruct((2 * count, 1), I32)
    perm_z = {k: mesh_perm(lambda s, d, k=k: (s, d ^ (2 * k))) for k in (1, 2, 3)}
    perm_x = mesh_perm(lambda s, d: (s, d ^ 1))
    gain = norm_gain[None]

    swap = [(s, s ^ 1) for s in range(sections)]
    over = [(s, s ^ 2) for s in range(sections)]
    extra = lax.ppermute(rows[half:], "section", [(1, 3), (3, 1)])
    sibling = lax.ppermute(rows, "section", swap)
    head_sibling = lax.ppermute(head, "section", swap)
    table, rows = call(
        table_kernel, [jax.ShapeDtypeStruct((2, part), F32), like(rows)], [VMEM] * 3, (gain, reward_head[None], rows)
    )

    if groups == 8:
        near = jnp.concatenate([table, send(table, perm_z[1])])
        near = jnp.concatenate([near, send(near, perm_z[2])])
    else:
        near = jnp.concatenate([table] * 4)
    full, near = call(
        functools.partial(pick_kernel, count),
        [jax.ShapeDtypeStruct((count, part), BF16), like(near)],
        [SMEM] + [VMEM] * 5 + [ANY],
        (lengths, rows, sibling, extra, gain, near, head_sibling),
    )
    token_ids = call(functools.partial(token_kernel, count), ids_shape, [SMEM, VMEM], (lengths, tokens))

    if groups == 8:
        perm_a = mesh_perm(lambda s, d: (s, d ^ 1) if s % 2 == 0 else (s ^ 2, d))
        perm_b = mesh_perm(lambda s, d: (s ^ 2, d) if s % 2 == 0 else (s, d ^ 1))

        def gate(value, *after):
            return call(gate_kernel, like(value), [VMEM] + [ANY] * len(after), (value,) + after)

        side_shape = jax.ShapeDtypeStruct((2 * count, 2 * LANES), F32)
        perm_e = mesh_perm(lambda s, d: (s, d ^ (2 if s % 2 == 0 else 6)))
        perm_f = mesh_perm(lambda s, d: (s, d ^ (6 if s % 2 == 0 else 2)))
        z1 = send(full, perm_e)
        a0 = send(full, perm_a)
        b0 = send(full, perm_b)
        far = send(near, perm_x)
        z3 = send(gate(full, z1), perm_f)
        z1 = gate(z1, b0)
        a1 = send(z1, perm_a)
        b1 = send(z1, perm_b)
        c0 = send(a0, perm_b)
        z3 = gate(z3, a1, b1, c0, far)
        a3 = send(z3, perm_a)
        b3 = send(z3, perm_b)
        z2 = send(z1, perm_f)
        acc, side, token_ids = call(
            begin_kernel,
            [acc_shape, side_shape, ids_shape],
            [VMEM] * 12,
            (head, head_sibling, near, far, full, a0, b0, c0, z1, a1, b1, token_ids),
        )
        a3 = gate(a3, token_ids)
        c3 = send(a3, perm_b)
        a2 = send(z2, perm_a)
        b2 = send(z2, perm_b)
        c1 = send(c0, perm_e)
        acc, side = call(
            middle_kernel,
            [acc_shape, side_shape],
            [VMEM] * 10,
            (head, head_sibling, near, far, acc, side, z3, a3, b3, c3),
        )
        a2 = gate(a2, side)
        c2 = send(a2, perm_b)
        left, left_side, far_weights, wide = call(
            functools.partial(own_kernel, width),
            [
                jax.ShapeDtypeStruct((count, 2 * block), F32),
                jax.ShapeDtypeStruct((count, 2 * LANES), F32),
                jax.ShapeDtypeStruct((part, 2 * block), BF16),
                jax.ShapeDtypeStruct((up(2 * count), LANES), F32),
            ],
            [VMEM] * 11,
            (head, head_sibling, near, far, acc, side, z2, a2, b2, c1, token_ids),
            scratch=[pltpu.VMEM((2 * count, 2 * LANES), F32)],
        )
        stats = call(
            functools.partial(last_kernel, width),
            stats_shape,
            [VMEM] * 7,
            (far_weights, far, left, left_side, c2, wide, token_ids),
            scratch=[pltpu.VMEM((up(2 * count), LANES), F32), pltpu.VMEM((count, 2 * LANES), F32)],
        )
        stats = combine([stats] + [send(stats, perm_z[k]) for k in (1, 2, 3)])
        stats = combine(
            [stats]
            + [send(stats, mesh_perm(lambda s, d, v=v: (s ^ v[0], d ^ v[1]))) for v in ((0, 1), (2, 0), (2, 1))]
        )
    else:
        other = lax.ppermute(full, "section", over)
        ordered = jnp.concatenate([jnp.where(pair == 0, full, other), jnp.where(pair == 0, other, full)])
        everything = lax.all_gather(ordered, "dp", axis=1, tiled=True)
        acc = jnp.concatenate(
            [jnp.dot(everything, h, preferred_element_type=F32) for h in (head, head_sibling)], axis=1
        )
        gains, weights_all = (lax.all_gather(t, "dp", axis=0, tiled=True) for t in table)
        wide = everything.astype(F32)
        square = jnp.sum(wide * wide * gains, axis=1, keepdims=True)
        reward = jnp.sum(wide * weights_all, axis=1, keepdims=True)
        stats = call(
            functools.partial(whole_kernel, width), stats_shape, [VMEM] * 4, (acc, square, reward, token_ids)
        )
        gathered = lax.all_gather(stats, "dp")
        stats = combine([gathered[i] for i in range(groups)])
        stats = combine([stats, lax.ppermute(stats, "section", over)])
    lp = stats[2:3] - (stats[0:1] + jnp.log(stats[1:2]))
    lp = jnp.concatenate([lp, stats[3:4], jnp.zeros((6, lp.shape[1]), F32)])
    both = lambda v, u: jnp.stack([jnp.where(core == 0, v, u), jnp.where(core == 0, u, v)])
    stats = both(lp, lax.ppermute(lp, "section", swap))
    logprob, score = call(
        functools.partial(final_kernel, count),
        [jax.ShapeDtypeStruct((1, positions), F32), jax.ShapeDtypeStruct((1, 1), F32)],
        [SMEM, VMEM],
        (lengths, stats),
    )
    return (logprob, score[0])


def solution(mesh):
    groups = mesh.shape["dp"]
    return jax.shard_map(
        lambda *args: per_device(groups, *args),
        mesh=mesh,
        in_specs=(P("section", None, "dp"), P("dp"), P(None, ("section", "dp")), P("dp"), P(), P()),
        out_specs=(P("section", None), P("section")),
        check_vma=False,
    )
```

```python
import functools

import jax
import jax.numpy as jnp
from jax import lax
from jax.experimental import pallas as pl
from jax.experimental.pallas import tpu as pltpu
from jax.sharding import PartitionSpec as P

AXES = ("section", "dp")
F32 = jnp.float32
BF16 = jnp.bfloat16
I32 = jnp.int32
LANES = 128
VMEM = pl.BlockSpec(memory_space=pltpu.VMEM)
SMEM = pl.BlockSpec(memory_space=pltpu.SMEM)
ANY = pl.BlockSpec(memory_space=pl.ANY)


def row_map(lengths, pair, core, index, count):
    first, second = lengths[2 * pair], lengths[2 * pair + 1]
    other_first = lengths[2 - 2 * pair]
    j = core * count + index
    in_first = j < first
    in_second = j < first + second
    span = jnp.where(in_first, 2 * pair, jnp.where(in_second, 2 * pair + 1, 3 - 2 * pair))
    place = jnp.where(
        in_first, j, jnp.where(in_second, j - first, 2 * count - other_first + j - first - second)
    )
    return span, place


def as_rows(columns, count):
    lane = lax.broadcasted_iota(I32, (count, LANES), 1)
    wide = jnp.zeros((count, LANES), F32)
    for i, column in enumerate(columns):
        wide = jnp.where(lane == i, column, wide)
    return jnp.transpose(wide)[:8]


def as_column(rows, which):
    full = jnp.concatenate([rows, jnp.zeros((LANES - 8, rows.shape[1]), F32)], axis=0)
    return jnp.transpose(full)[:, which : which + 1]


def table_kernel(gain, reward, rows, table, rows_out):
    rows_out[...] = rows[...]
    value = gain[...].astype(F32)
    table[0:1, :] = 1.0 / (value * value)
    table[1:2, :] = reward[...].astype(F32)


def pick_kernel(count, lengths, rows, sibling, extra, gain, table, after, full, table_out):
    section = lax.axis_index("section")
    core, pair = lax.rem(section, 2), lax.div(section, 2)
    positions, half = rows.shape[0], extra.shape[0]
    index = lax.broadcasted_iota(I32, (count, 1), 0)
    span, place = row_map(lengths, pair, core, index, count)
    source = jnp.where(span == section, place, place + positions)
    source = jnp.where(span // 2 == pair, source, place + (2 * positions - (positions - half)))
    lane = lax.broadcasted_iota(I32, (count, 2 * positions + half), 1)
    pick = jnp.where(lane == source, F32(1.0), F32(0.0)).astype(BF16)
    picked = jnp.dot(pick[:, :positions], rows[...], preferred_element_type=F32)
    picked += jnp.dot(pick[:, positions : 2 * positions], sibling[...], preferred_element_type=F32)
    picked += jnp.dot(pick[:, 2 * positions :], extra[...], preferred_element_type=F32)
    full[...] = (picked * gain[...].astype(F32)).astype(BF16)
    table_out[...] = table[...]


def token_kernel(count, lengths, tokens, out, hit, per_row):
    section, core, _ = here()
    spans, positions = tokens.shape
    index = lax.broadcasted_iota(I32, (count, 1), 0)
    lane = lax.broadcasted_iota(I32, (count, positions), 1)
    hit[...] = jnp.zeros(hit.shape, F32)
    for pair in range(2):
        rows = slice(pair * count, pair * count + count)
        span, place = row_map(lengths, pair, core, index, count)
        found = jnp.zeros((count, positions), F32)
        for s in range(spans):
            found = jnp.where(span == s, tokens[s : s + 1, :].astype(F32), found)
        here_is = lane == place
        found = jnp.sum(jnp.where(here_is, found, F32(0.0)), axis=1, keepdims=True)
        out[rows, :] = found.astype(I32)
        hit[0, rows, :] = jnp.where(here_is & (span == section), F32(1.0), F32(0.0))
        span, place = row_map(lengths, pair, 1 - core, index, count)
        hit[1, rows, :] = jnp.where((lane == place) & (span == section), F32(1.0), F32(0.0))
    per_row[...] = jnp.zeros(per_row.shape, F32) + 1.0 / lengths[section].astype(F32)


def here():
    section = lax.axis_index("section")
    return section, lax.rem(section, 2), lax.div(section, 2)


def blocks(count):
    _, _, pair = here()
    return pl.multiple_of(pair * count, 16), pl.multiple_of((1 - pair) * count, 16)


def weights(head, sibling, depth, k, far):
    dp_index = lax.axis_index("dp")
    where = jnp.bitwise_xor(dp_index, 2 * k + (1 if far else 0))
    rows = pl.ds(pl.multiple_of(where * depth, depth), depth)
    return head[rows, :], sibling[rows, :]


def products(terms):
    value = jnp.concatenate([t[0] for t in terms], axis=1) if len(terms) > 1 else terms[0][0]
    out = []
    for side in range(2):
        w = [t[1][side] for t in terms]
        w = jnp.concatenate(w, axis=0) if len(w) > 1 else w[0]
        out.append(jnp.dot(value, w, preferred_element_type=F32))
    return jnp.concatenate(out, axis=1)


def add_sides(terms, base, side_in, side):
    step = 32
    count, depth = terms[0][0].shape

    def body(i, _):
        rows = pl.ds(pl.multiple_of(i * step, step), step)
        at = pl.ds(pl.multiple_of(base + i * step, step), step)
        square, reward = jnp.zeros((step, LANES), F32), jnp.zeros((step, LANES), F32)
        if side_in is not None:
            square, reward = side_in[at, :LANES], side_in[at, LANES:]
        for piece, table, k in terms:
            for c in range(depth // LANES):
                cols = slice(c * LANES, (c + 1) * LANES)
                value = piece[rows, cols].astype(F32)
                square += value * value * table[2 * k : 2 * k + 1, cols]
                reward += value * table[2 * k + 1 : 2 * k + 2, cols]
        side[at, :LANES] = square
        side[at, LANES:] = reward
        return 0

    lax.fori_loop(0, count // step, body, 0)


def both_weights(head, sibling, depth, k):
    return weights(head, sibling, depth, k, False), weights(head, sibling, depth, k, True)


def begin_kernel(head, sibling, table, z, a, b, c, z1, a1, b1, ids, after, acc, side, ids_out):
    count, depth = z.shape
    _, core, _ = here()
    mine, others = blocks(count)
    near0, far0 = both_weights(head, sibling, depth, 0)
    for which, k, same, cross, same1, cross1 in ((0, 1, a, b, a1, b1), (1, 3, b, a, b1, a1)):

        @pl.when(core == which)
        def _():
            near1, far1 = both_weights(head, sibling, depth, k)
            rows = pl.ds(mine, count)
            acc[rows, :] = products([(z[...], near0), (same[...], far0), (z1[...], near1), (same1[...], far1)])
            terms = [(z, table, 0), (same, table, 1), (z1, table, 2 * k), (same1, table, 2 * k + 1)]
            add_sides(terms, mine, None, side)
            rows = pl.ds(others, count)
            acc[rows, :] = products([(cross[...], near0), (c[...], far0), (cross1[...], near1)])
            add_sides([(cross, table, 0), (c, table, 1), (cross1, table, 2 * k)], others, None, side)

    ids_out[...] = ids[...]


def middle_kernel(head, sibling, table, acc_in, side_in, z, a, b, c, acc, side):
    count, depth = z.shape
    _, core, _ = here()
    mine, others = blocks(count)
    for which, k, same, cross in ((0, 3, a, b), (1, 1, b, a)):

        @pl.when(core == which)
        def _():
            near3, far3 = both_weights(head, sibling, depth, k)
            rows = pl.ds(mine, count)
            acc[rows, :] = acc_in[rows, :] + products([(z[...], near3), (same[...], far3)])
            add_sides([(z, table, 2 * k), (same, table, 2 * k + 1)], mine, side_in, side)
            rows = pl.ds(others, count)
            acc[rows, :] = acc_in[rows, :] + products([(cross[...], near3), (c[...], far3)])
            add_sides([(cross, table, 2 * k), (c, table, 2 * k + 1)], others, side_in, side)


def gate_kernel(value, *refs):
    refs[-1][...] = value[: refs[-1].shape[0], :]


def padded_kernel(value, after, out):
    out[: value.shape[0], :] = value[...]
    out[value.shape[0] :, :] = jnp.zeros((out.shape[0] - value.shape[0], out.shape[1]), out.dtype)


def column_ids(block):
    section, core, _ = here()
    dp_index, groups = lax.axis_index("dp"), lax.axis_size("dp")
    lane = lax.broadcasted_iota(I32, (1, block), 1)
    own = (section * groups + dp_index) * block
    other = ((section + 1 - 2 * core) * groups + dp_index) * block
    return jnp.concatenate([lane + own, lane + other], axis=1)


def summary(logits, square, reward, token_ids, ids, width):
    scale = lax.rsqrt(square / width + 1e-05)
    logits = logits * scale
    top = jnp.max(logits, axis=1, keepdims=True)
    total = jnp.sum(jnp.exp(logits - top), axis=1, keepdims=True)
    target = jnp.sum(jnp.where(ids == token_ids, logits, F32(0.0)), axis=1, keepdims=True)
    lane = lax.broadcasted_iota(I32, (logits.shape[0], LANES), 1)
    wide = jnp.where(lane == 2, target, jnp.where(lane == 3, reward * scale, F32(0.0)))
    return jnp.where(lane == 0, top, jnp.where(lane == 1, total, wide))


def added(side):
    return jnp.sum(side[:, :LANES], axis=1, keepdims=True), jnp.sum(side[:, LANES:], axis=1, keepdims=True)


def own_kernel(width, head, sibling, table, acc_in, side_in, z, a, b, c1, token_ids, left, left_side, far_out, wide, side):
    count, depth = z.shape
    _, core, _ = here()
    mine, others = blocks(count)
    near2, far2 = weights(head, sibling, depth, 2, False), weights(head, sibling, depth, 2, True)
    block = head.shape[1]
    far_out[:, :block] = far2[0]
    far_out[:, block:] = far2[1]
    ids = column_ids(block)
    wide[...] = jnp.zeros(wide.shape, F32)
    for which, k, same, cross in ((0, 1, a, b), (1, 3, b, a)):

        @pl.when(core == which)
        def _():
            far1 = weights(head, sibling, depth, k, True)
            rows = pl.ds(mine, count)
            logits = acc_in[rows, :] + products([(z[...], near2), (same[...], far2)])
            add_sides([(z, table, 4), (same, table, 5)], mine, side_in, side)
            square, reward = added(side[rows, :])
            wide[rows, :] = summary(logits, square, reward, token_ids[rows, :], ids, width)
            rows = pl.ds(others, count)
            left[...] = acc_in[rows, :] + products([(cross[...], near2), (c1[...], far1)])
            add_sides([(cross, table, 4), (c1, table, 2 * k + 1)], others, side_in, side)
            left_side[...] = side[rows, :]


def last_kernel(width, far_weights, table, left, left_side, c, wide_in, token_ids, out, wide, side):
    count = c.shape[0]
    _, others = blocks(count)
    ids = column_ids(far_weights.shape[1] // 2)
    wide[...] = wide_in[...]
    logits = left[...] + jnp.dot(c[...], far_weights[...], preferred_element_type=F32)
    add_sides([(c, table, 5)], 0, left_side, side)
    square, reward = added(side[...])
    rows = pl.ds(others, count)
    wide[rows, :] = summary(logits, square, reward, token_ids[rows, :], ids, width)
    out[...] = jnp.transpose(wide[...])[:8]


def whole_kernel(width, acc, square, reward, token_ids, out):
    count = acc.shape[0] // 2
    ids = column_ids(acc.shape[1] // 2)
    wide = summary(acc[...], square[...], reward[...], token_ids[...], ids, width)
    wide = jnp.concatenate([wide, jnp.zeros((out.shape[1] - 2 * count, LANES), F32)])
    out[...] = jnp.transpose(wide)[:8]


def final_kernel(mine, sibling, hit, per_row, out_ref, score_ref):
    exact = functools.partial(jnp.dot, precision=lax.Precision.HIGHEST, preferred_element_type=F32)
    picked = exact(mine[...], hit[0]) + exact(sibling[...], hit[1])
    out_ref[...] = picked[0:1, :]
    score_ref[...] = jnp.sum(picked[1:2, :], axis=1, keepdims=True) * per_row[0:1, 0:1]


def combine(parts):
    top = parts[0][0]
    for part in parts[1:]:
        top = jnp.maximum(top, part[0])
    total = sum(part[1] * jnp.exp(part[0] - top) for part in parts)
    target = sum(part[2] for part in parts)
    return jnp.concatenate([jnp.stack([top, total, target, parts[0][3]]), jnp.zeros((4,) + top.shape, F32)])


def call(body, outs, in_specs, args, limit=16, scratch=()):
    many = isinstance(outs, (list, tuple))
    return pl.pallas_call(
        body,
        out_shape=outs,
        in_specs=in_specs,
        out_specs=[VMEM] * len(outs) if many else VMEM,
        scratch_shapes=scratch,
        compiler_params=pltpu.CompilerParams(vmem_limit_bytes=limit << 20),
    )(*args)


def up(value):
    return -(-value // LANES) * LANES


def per_device(groups, hidden, norm_gain, head, reward_head, tokens, lengths):
    section = lax.axis_index("section")
    core, pair = section % 2, section // 2
    sections = lax.axis_size("section")
    spans, positions = tokens.shape
    block, width, part = head.shape[1], head.shape[0], hidden.shape[2]
    count = 3 * spans * positions // 4 // sections
    half = positions // 2
    rows = hidden[0]

    def mesh_perm(move):
        pairs = []
        for s in range(sections):
            for d in range(groups):
                s2, d2 = move(s, d)
                pairs.append((s * groups + d, s2 * groups + d2))
        return pairs

    send = lambda value, perm: lax.ppermute(value, AXES, perm)
    like = lambda v: jax.ShapeDtypeStruct(v.shape, v.dtype)
    acc_shape = jax.ShapeDtypeStruct((2 * count, 2 * block), F32)
    stats_shape = jax.ShapeDtypeStruct((8, up(2 * count)), F32)
    ids_shape = jax.ShapeDtypeStruct((2 * count, 1), I32)
    perm_z = {k: mesh_perm(lambda s, d, k=k: (s, d ^ (2 * k))) for k in (1, 2, 3)}
    perm_x = mesh_perm(lambda s, d: (s, d ^ 1))
    gain = norm_gain[None]

    swap = [(s, s ^ 1) for s in range(sections)]
    over = [(s, s ^ 2) for s in range(sections)]
    extra = lax.ppermute(rows[half:], "section", [(1, 3), (3, 1)])
    sibling = lax.ppermute(rows, "section", swap)
    head_sibling = lax.ppermute(head, "section", swap)
    table, rows = call(
        table_kernel, [jax.ShapeDtypeStruct((2, part), F32), like(rows)], [VMEM] * 3, (gain, reward_head[None], rows)
    )

    if groups == 8:
        table = jnp.concatenate([table, send(table, perm_x)])
    full, table = call(
        functools.partial(pick_kernel, count),
        [jax.ShapeDtypeStruct((count, part), BF16), like(table)],
        [SMEM] + [VMEM] * 5 + [ANY],
        (lengths, rows, sibling, extra, gain, table, head_sibling),
    )
    token_ids, hit, per_row = call(
        functools.partial(token_kernel, count),
        [
            ids_shape,
            jax.ShapeDtypeStruct((2, up(2 * count), positions), F32),
            jax.ShapeDtypeStruct((8, LANES), F32),
        ],
        [SMEM, VMEM],
        (lengths, tokens),
    )

    if groups == 8:
        perm_a = mesh_perm(lambda s, d: (s, d ^ 1) if s % 2 == 0 else (s ^ 2, d))
        perm_b = mesh_perm(lambda s, d: (s ^ 2, d) if s % 2 == 0 else (s, d ^ 1))

        def gate(value, *after):
            return call(gate_kernel, like(value), [VMEM] + [ANY] * len(after), (value,) + after)

        side_shape = jax.ShapeDtypeStruct((2 * count, 2 * LANES), F32)
        perm_e = mesh_perm(lambda s, d: (s, d ^ (2 if s % 2 == 0 else 6)))
        perm_f = mesh_perm(lambda s, d: (s, d ^ (6 if s % 2 == 0 else 2)))
        z1 = send(full, perm_e)
        a0 = send(full, perm_a)
        b0 = send(full, perm_b)
        table = jnp.concatenate([table, send(table, perm_z[1])])
        z3 = send(call(padded_kernel, jax.ShapeDtypeStruct((count + 16, part), BF16), [VMEM, ANY], (full, z1)), perm_f)
        z1 = gate(z1, b0, table, token_ids)
        a1 = send(z1, perm_a)
        b1 = send(z1, perm_b)
        c0 = send(a0, perm_b)
        table = jnp.concatenate([table, send(table, perm_z[2])])
        z3 = call(gate_kernel, like(full), [VMEM] + [ANY] * 4, (z3, a1, b1, c0, table))
        a3 = send(z3, perm_a)
        z3 = gate(z3)
        b3 = send(z3, perm_b)
        z2 = send(z1, perm_f)
        acc, side, token_ids = call(
            begin_kernel,
            [acc_shape, side_shape, ids_shape],
            [VMEM] * 11 + [ANY],
            (head, head_sibling, table, full, a0, b0, c0, z1, a1, b1, token_ids, z3),
        )
        a3 = gate(a3, token_ids)
        c3 = send(a3, perm_b)
        a2 = send(z2, perm_a)
        b2 = send(z2, perm_b)
        c1 = send(c0, perm_e)
        acc, side = call(
            middle_kernel,
            [acc_shape, side_shape],
            [VMEM] * 9,
            (head, head_sibling, table, acc, side, z3, a3, b3, c3),
        )
        a2 = gate(a2, side)
        c2 = send(a2, perm_b)
        left, left_side, far_weights, wide = call(
            functools.partial(own_kernel, width),
            [
                jax.ShapeDtypeStruct((count, 2 * block), F32),
                jax.ShapeDtypeStruct((count, 2 * LANES), F32),
                jax.ShapeDtypeStruct((part, 2 * block), BF16),
                jax.ShapeDtypeStruct((up(2 * count), LANES), F32),
            ],
            [VMEM] * 10,
            (head, head_sibling, table, acc, side, z2, a2, b2, c1, token_ids),
            scratch=[pltpu.VMEM((2 * count, 2 * LANES), F32)],
        )
        stats = call(
            functools.partial(last_kernel, width),
            stats_shape,
            [VMEM] * 7,
            (far_weights, table, left, left_side, c2, wide, token_ids),
            scratch=[pltpu.VMEM((up(2 * count), LANES), F32), pltpu.VMEM((count, 2 * LANES), F32)],
        )
        stats = combine([stats] + [send(stats, perm_z[k]) for k in (1, 2, 3)])
        stats = combine(
            [stats]
            + [send(stats, mesh_perm(lambda s, d, v=v: (s ^ v[0], d ^ v[1]))) for v in ((0, 1), (2, 0), (2, 1))]
        )
    else:
        other = lax.ppermute(full, "section", over)
        ordered = jnp.concatenate([jnp.where(pair == 0, full, other), jnp.where(pair == 0, other, full)])
        everything = lax.all_gather(ordered, "dp", axis=1, tiled=True)
        acc = jnp.concatenate(
            [jnp.dot(everything, h, preferred_element_type=F32) for h in (head, head_sibling)], axis=1
        )
        gains, weights_all = (lax.all_gather(table[i], "dp", axis=0, tiled=True) for i in range(2))
        wide = everything.astype(F32)
        square = jnp.sum(wide * wide * gains, axis=1, keepdims=True)
        reward = jnp.sum(wide * weights_all, axis=1, keepdims=True)
        stats = call(
            functools.partial(whole_kernel, width), stats_shape, [VMEM] * 4, (acc, square, reward, token_ids)
        )
        gathered = lax.all_gather(stats, "dp")
        stats = combine([gathered[i] for i in range(groups)])
        stats = combine([stats, lax.ppermute(stats, "section", over)])
    filled = jnp.arange(stats.shape[1], dtype=jnp.int32)[None, :] < 2 * count
    lp = jnp.where(filled, stats[2:3] - (stats[0:1] + jnp.log(stats[1:2])), F32(0.0))
    lp = jnp.concatenate([lp, stats[3:4], jnp.zeros((6, lp.shape[1]), F32)])
    logprob, score = call(
        final_kernel,
        [jax.ShapeDtypeStruct((1, positions), F32), jax.ShapeDtypeStruct((1, 1), F32)],
        [VMEM] * 4,
        (lp, lax.ppermute(lp, "section", swap), hit, per_row),
    )
    return (logprob, score[0])


def solution(mesh):
    groups = mesh.shape["dp"]
    return jax.shard_map(
        lambda *args: per_device(groups, *args),
        mesh=mesh,
        in_specs=(P("section", None, "dp"), P("dp"), P(None, ("section", "dp")), P("dp"), P(), P()),
        out_specs=(P("section", None), P("section")),
        check_vma=False,
    )
```

```python
import functools

import jax
import jax.numpy as jnp
from jax import lax
from jax.experimental import pallas as pl
from jax.experimental.pallas import tpu as pltpu
from jax.sharding import PartitionSpec as P

AXES = ("section", "dp")
F32 = jnp.float32
BF16 = jnp.bfloat16
I32 = jnp.int32
LANES = 128
VMEM = pl.BlockSpec(memory_space=pltpu.VMEM)
SMEM = pl.BlockSpec(memory_space=pltpu.SMEM)
ANY = pl.BlockSpec(memory_space=pl.ANY)


def row_map(lengths, pair, core, index, count):
    first, second = lengths[2 * pair], lengths[2 * pair + 1]
    other_first = lengths[2 - 2 * pair]
    j = core * count + index
    in_first = j < first
    in_second = j < first + second
    span = jnp.where(in_first, 2 * pair, jnp.where(in_second, 2 * pair + 1, 3 - 2 * pair))
    place = jnp.where(
        in_first, j, jnp.where(in_second, j - first, 2 * count - other_first + j - first - second)
    )
    return span, place


def as_rows(columns, count):
    lane = lax.broadcasted_iota(I32, (count, LANES), 1)
    wide = jnp.zeros((count, LANES), F32)
    for i, column in enumerate(columns):
        wide = jnp.where(lane == i, column, wide)
    return jnp.transpose(wide)[:8]


def as_column(rows, which):
    full = jnp.concatenate([rows, jnp.zeros((LANES - 8, rows.shape[1]), F32)], axis=0)
    return jnp.transpose(full)[:, which : which + 1]


def table_kernel(gain, reward, rows, table, rows_out):
    rows_out[...] = rows[...]
    value = gain[...].astype(F32)
    table[0:1, :] = 1.0 / (value * value)
    table[1:2, :] = reward[...].astype(F32)


def pick_kernel(count, lengths, rows, sibling, extra, gain, table, after, full, table_out):
    section = lax.axis_index("section")
    core, pair = lax.rem(section, 2), lax.div(section, 2)
    positions, half = rows.shape[0], extra.shape[0]
    index = lax.broadcasted_iota(I32, (count, 1), 0)
    span, place = row_map(lengths, pair, core, index, count)
    source = jnp.where(span == section, place, place + positions)
    source = jnp.where(span // 2 == pair, source, place + (2 * positions - (positions - half)))
    lane = lax.broadcasted_iota(I32, (count, 2 * positions + half), 1)
    pick = jnp.where(lane == source, F32(1.0), F32(0.0)).astype(BF16)
    picked = jnp.dot(pick[:, :positions], rows[...], preferred_element_type=F32)
    picked += jnp.dot(pick[:, positions : 2 * positions], sibling[...], preferred_element_type=F32)
    picked += jnp.dot(pick[:, 2 * positions :], extra[...], preferred_element_type=F32)
    full[...] = (picked * gain[...].astype(F32)).astype(BF16)
    table_out[...] = table[...]


def token_kernel(count, lengths, tokens, out, hit, per_row):
    section, core, _ = here()
    spans, positions = tokens.shape
    index = lax.broadcasted_iota(I32, (count, 1), 0)
    lane = lax.broadcasted_iota(I32, (count, positions), 1)
    hit[...] = jnp.zeros(hit.shape, F32)
    for pair in range(2):
        rows = slice(pair * count, pair * count + count)
        span, place = row_map(lengths, pair, core, index, count)
        found = jnp.zeros((count, positions), F32)
        for s in range(spans):
            found = jnp.where(span == s, tokens[s : s + 1, :].astype(F32), found)
        here_is = lane == place
        found = jnp.sum(jnp.where(here_is, found, F32(0.0)), axis=1, keepdims=True)
        out[rows, :] = found.astype(I32)
        hit[0, rows, :] = jnp.where(here_is & (span == section), F32(1.0), F32(0.0))
        span, place = row_map(lengths, pair, 1 - core, index, count)
        hit[1, rows, :] = jnp.where((lane == place) & (span == section), F32(1.0), F32(0.0))
    per_row[...] = jnp.zeros(per_row.shape, F32) + 1.0 / lengths[section].astype(F32)


def here():
    section = lax.axis_index("section")
    return section, lax.rem(section, 2), lax.div(section, 2)


def blocks(count):
    _, _, pair = here()
    return pl.multiple_of(pair * count, 16), pl.multiple_of((1 - pair) * count, 16)


def weights(head, sibling, depth, k, far):
    dp_index = lax.axis_index("dp")
    where = jnp.bitwise_xor(dp_index, 2 * k + (1 if far else 0))
    rows = pl.ds(pl.multiple_of(where * depth, depth), depth)
    return head[rows, :], sibling[rows, :]


def products(terms):
    value = jnp.concatenate([t[0] for t in terms], axis=1) if len(terms) > 1 else terms[0][0]
    out = []
    for side in range(2):
        w = [t[1][side] for t in terms]
        w = jnp.concatenate(w, axis=0) if len(w) > 1 else w[0]
        out.append(jnp.dot(value, w, preferred_element_type=F32))
    return jnp.concatenate(out, axis=1)


def add_sides(terms, base, side_in, side):
    step = 32
    count, depth = terms[0][0].shape

    def body(i, _):
        rows = pl.ds(pl.multiple_of(i * step, step), step)
        at = pl.ds(pl.multiple_of(base + i * step, step), step)
        square, reward = jnp.zeros((step, LANES), F32), jnp.zeros((step, LANES), F32)
        if side_in is not None:
            square, reward = side_in[at, :LANES], side_in[at, LANES:]
        for piece, table, k in terms:
            for c in range(depth // LANES):
                cols = slice(c * LANES, (c + 1) * LANES)
                value = piece[rows, cols].astype(F32)
                square += value * value * table[2 * k : 2 * k + 1, cols]
                reward += value * table[2 * k + 1 : 2 * k + 2, cols]
        side[at, :LANES] = square
        side[at, LANES:] = reward
        return 0

    lax.fori_loop(0, count // step, body, 0)


def both_weights(head, sibling, depth, k):
    return weights(head, sibling, depth, k, False), weights(head, sibling, depth, k, True)


def begin_kernel(head, sibling, table, z, a, b, c, z1, a1, b1, ids, after, acc, side, ids_out):
    count, depth = z.shape
    _, core, _ = here()
    mine, others = blocks(count)
    near0, far0 = both_weights(head, sibling, depth, 0)
    for which, k, same, cross, same1, cross1 in ((0, 1, a, b, a1, b1), (1, 3, b, a, b1, a1)):

        @pl.when(core == which)
        def _():
            near1, far1 = both_weights(head, sibling, depth, k)
            rows = pl.ds(mine, count)
            acc[rows, :] = products([(z[...], near0), (same[...], far0), (z1[...], near1), (same1[...], far1)])
            terms = [(z, table, 0), (same, table, 1), (z1, table, 2 * k), (same1, table, 2 * k + 1)]
            add_sides(terms, mine, None, side)
            rows = pl.ds(others, count)
            acc[rows, :] = products([(cross[...], near0), (c[...], far0), (cross1[...], near1)])
            add_sides([(cross, table, 0), (c, table, 1), (cross1, table, 2 * k)], others, None, side)

    ids_out[...] = ids[...]


def middle_kernel(head, sibling, table, acc_in, side_in, z, a, b, c, acc, side):
    count, depth = z.shape
    _, core, _ = here()
    mine, others = blocks(count)
    for which, k, same, cross in ((0, 3, a, b), (1, 1, b, a)):

        @pl.when(core == which)
        def _():
            near3, far3 = both_weights(head, sibling, depth, k)
            rows = pl.ds(mine, count)
            acc[rows, :] = acc_in[rows, :] + products([(z[...], near3), (same[...], far3)])
            add_sides([(z, table, 2 * k), (same, table, 2 * k + 1)], mine, side_in, side)
            rows = pl.ds(others, count)
            acc[rows, :] = acc_in[rows, :] + products([(cross[...], near3), (c[...], far3)])
            add_sides([(cross, table, 2 * k), (c, table, 2 * k + 1)], others, side_in, side)


def gate_kernel(value, *refs):
    refs[-1][...] = value[: refs[-1].shape[0], :]


def padded_kernel(value, after, out):
    out[: value.shape[0], :] = value[...]
    out[value.shape[0] :, :] = jnp.zeros((out.shape[0] - value.shape[0], out.shape[1]), out.dtype)


def column_ids(block):
    section, core, _ = here()
    dp_index, groups = lax.axis_index("dp"), lax.axis_size("dp")
    lane = lax.broadcasted_iota(I32, (1, block), 1)
    own = (section * groups + dp_index) * block
    other = ((section + 1 - 2 * core) * groups + dp_index) * block
    return jnp.concatenate([lane + own, lane + other], axis=1)


def summary(logits, square, reward, token_ids, ids, width):
    scale = lax.rsqrt(square / width + 1e-05)
    logits = logits * scale
    top = jnp.max(logits, axis=1, keepdims=True)
    total = jnp.sum(jnp.exp(logits - top), axis=1, keepdims=True)
    target = jnp.sum(jnp.where(ids == token_ids, logits, F32(0.0)), axis=1, keepdims=True)
    lane = lax.broadcasted_iota(I32, (logits.shape[0], LANES), 1)
    wide = jnp.where(lane == 2, target, jnp.where(lane == 3, reward * scale, F32(0.0)))
    return jnp.where(lane == 0, top, jnp.where(lane == 1, total, wide))


def added(side):
    return jnp.sum(side[:, :LANES], axis=1, keepdims=True), jnp.sum(side[:, LANES:], axis=1, keepdims=True)


def own_kernel(width, head, sibling, table, acc_in, side_in, z, a, b, c1, token_ids, left, left_side, far_out, wide, side):
    count, depth = z.shape
    _, core, _ = here()
    mine, others = blocks(count)
    near2, far2 = weights(head, sibling, depth, 2, False), weights(head, sibling, depth, 2, True)
    block = head.shape[1]
    far_out[:, :block] = far2[0]
    far_out[:, block:] = far2[1]
    ids = column_ids(block)
    wide[...] = jnp.zeros(wide.shape, F32)
    for which, k, same, cross in ((0, 1, a, b), (1, 3, b, a)):

        @pl.when(core == which)
        def _():
            far1 = weights(head, sibling, depth, k, True)
            rows = pl.ds(mine, count)
            logits = acc_in[rows, :] + products([(z[...], near2), (same[...], far2)])
            add_sides([(z, table, 4), (same, table, 5)], mine, side_in, side)
            square, reward = added(side[rows, :])
            wide[rows, :] = summary(logits, square, reward, token_ids[rows, :], ids, width)
            rows = pl.ds(others, count)
            left[...] = acc_in[rows, :] + products([(cross[...], near2), (c1[...], far1)])
            add_sides([(cross, table, 4), (c1, table, 2 * k + 1)], others, side_in, side)
            left_side[...] = side[rows, :]


def last_kernel(width, far_weights, table, left, left_side, c, wide_in, token_ids, out, wide, side):
    count = c.shape[0]
    _, others = blocks(count)
    ids = column_ids(far_weights.shape[1] // 2)
    wide[...] = wide_in[...]
    logits = left[...] + jnp.dot(c[...], far_weights[...], preferred_element_type=F32)
    add_sides([(c, table, 5)], 0, left_side, side)
    square, reward = added(side[...])
    rows = pl.ds(others, count)
    wide[rows, :] = summary(logits, square, reward, token_ids[rows, :], ids, width)
    out[...] = jnp.transpose(wide[...])[:8]


def whole_kernel(width, acc, square, reward, token_ids, out):
    count = acc.shape[0] // 2
    ids = column_ids(acc.shape[1] // 2)
    wide = summary(acc[...], square[...], reward[...], token_ids[...], ids, width)
    wide = jnp.concatenate([wide, jnp.zeros((out.shape[1] - 2 * count, LANES), F32)])
    out[...] = jnp.transpose(wide)[:8]


def final_kernel(mine, sibling, hit, per_row, out_ref, score_ref):
    exact = functools.partial(jnp.dot, precision=lax.Precision.HIGHEST, preferred_element_type=F32)
    picked = exact(mine[...], hit[0]) + exact(sibling[...], hit[1])
    out_ref[...] = picked[0:1, :]
    score_ref[...] = jnp.sum(picked[1:2, :], axis=1, keepdims=True) * per_row[0:1, 0:1]


def combine(parts):
    top = parts[0][0]
    for part in parts[1:]:
        top = jnp.maximum(top, part[0])
    total = sum(part[1] * jnp.exp(part[0] - top) for part in parts)
    target = sum(part[2] for part in parts)
    return jnp.concatenate([jnp.stack([top, total, target, parts[0][3]]), jnp.zeros((4,) + top.shape, F32)])


def call(body, outs, in_specs, args, limit=16, scratch=()):
    many = isinstance(outs, (list, tuple))
    return pl.pallas_call(
        body,
        out_shape=outs,
        in_specs=in_specs,
        out_specs=[VMEM] * len(outs) if many else VMEM,
        scratch_shapes=scratch,
        compiler_params=pltpu.CompilerParams(vmem_limit_bytes=limit << 20),
    )(*args)


def up(value):
    return -(-value // LANES) * LANES


def per_device(groups, hidden, norm_gain, head, reward_head, tokens, lengths):
    section = lax.axis_index("section")
    core, pair = section % 2, section // 2
    sections = lax.axis_size("section")
    spans, positions = tokens.shape
    block, width, part = head.shape[1], head.shape[0], hidden.shape[2]
    count = 3 * spans * positions // 4 // sections
    half = positions // 2
    rows = hidden[0]

    def mesh_perm(move):
        pairs = []
        for s in range(sections):
            for d in range(groups):
                s2, d2 = move(s, d)
                pairs.append((s * groups + d, s2 * groups + d2))
        return pairs

    send = lambda value, perm: lax.ppermute(value, AXES, perm)
    like = lambda v: jax.ShapeDtypeStruct(v.shape, v.dtype)
    acc_shape = jax.ShapeDtypeStruct((2 * count, 2 * block), F32)
    stats_shape = jax.ShapeDtypeStruct((8, up(2 * count)), F32)
    ids_shape = jax.ShapeDtypeStruct((2 * count, 1), I32)
    perm_z = {k: mesh_perm(lambda s, d, k=k: (s, d ^ (2 * k))) for k in (1, 2, 3)}
    perm_x = mesh_perm(lambda s, d: (s, d ^ 1))
    gain = norm_gain[None]

    swap = [(s, s ^ 1) for s in range(sections)]
    over = [(s, s ^ 2) for s in range(sections)]
    extra = lax.ppermute(rows[half:], "section", [(1, 3), (3, 1)])
    sibling = lax.ppermute(rows, "section", swap)
    head_sibling = lax.ppermute(head, "section", swap)
    table, rows = call(
        table_kernel, [jax.ShapeDtypeStruct((2, part), F32), like(rows)], [VMEM] * 3, (gain, reward_head[None], rows)
    )

    if groups == 8:
        table = jnp.concatenate([table, send(table, perm_x)])
    full, table = call(
        functools.partial(pick_kernel, count),
        [jax.ShapeDtypeStruct((count, part), BF16), like(table)],
        [SMEM] + [VMEM] * 5 + [ANY],
        (lengths, rows, sibling, extra, gain, table, head_sibling),
    )
    token_ids, hit, per_row = call(
        functools.partial(token_kernel, count),
        [
            ids_shape,
            jax.ShapeDtypeStruct((2, up(2 * count), positions), F32),
            jax.ShapeDtypeStruct((8, LANES), F32),
        ],
        [SMEM, VMEM],
        (lengths, tokens),
    )

    if groups == 8:
        perm_a = mesh_perm(lambda s, d: (s, d ^ 1) if s % 2 == 0 else (s ^ 2, d))
        perm_b = mesh_perm(lambda s, d: (s ^ 2, d) if s % 2 == 0 else (s, d ^ 1))

        def gate(value, *after):
            return call(gate_kernel, like(value), [VMEM] + [ANY] * len(after), (value,) + after)

        side_shape = jax.ShapeDtypeStruct((2 * count, 2 * LANES), F32)
        perm_e = mesh_perm(lambda s, d: (s, d ^ (2 if s % 2 == 0 else 6)))
        perm_f = mesh_perm(lambda s, d: (s, d ^ (6 if s % 2 == 0 else 2)))
        z1 = send(full, perm_e)
        a0 = send(full, perm_a)
        b0 = send(full, perm_b)
        table = jnp.concatenate([table, send(table, perm_z[1])])
        z3 = send(call(padded_kernel, jax.ShapeDtypeStruct((count + 16, part), BF16), [VMEM, ANY], (full, z1)), perm_f)
        z1 = gate(z1, b0, table, token_ids)
        a1 = send(z1, perm_a)
        b1 = send(z1, perm_b)
        c0 = send(a0, perm_b)
        z3 = call(gate_kernel, like(full), [VMEM] + [ANY], (z3, a1))
        a3 = send(z3, perm_a)
        table = jnp.concatenate([table, send(table, perm_z[2])])
        z3 = gate(z3, b1, c0, table)
        b3 = send(z3, perm_b)
        z2 = send(gate(z1, z3), perm_f)
        acc, side, token_ids = call(
            begin_kernel,
            [acc_shape, side_shape, ids_shape],
            [VMEM] * 11 + [ANY],
            (head, head_sibling, table, full, a0, b0, c0, z1, a1, b1, token_ids, z3),
        )
        a3 = gate(a3, token_ids)
        c3 = send(a3, perm_b)
        a2 = send(z2, perm_a)
        b2 = send(z2, perm_b)
        c1 = send(c0, perm_e)
        acc, side = call(
            middle_kernel,
            [acc_shape, side_shape],
            [VMEM] * 9,
            (head, head_sibling, table, acc, side, z3, a3, b3, c3),
        )
        a2 = gate(a2, side)
        c2 = send(a2, perm_b)
        left, left_side, far_weights, wide = call(
            functools.partial(own_kernel, width),
            [
                jax.ShapeDtypeStruct((count, 2 * block), F32),
                jax.ShapeDtypeStruct((count, 2 * LANES), F32),
                jax.ShapeDtypeStruct((part, 2 * block), BF16),
                jax.ShapeDtypeStruct((up(2 * count), LANES), F32),
            ],
            [VMEM] * 10,
            (head, head_sibling, table, acc, side, z2, a2, b2, c1, token_ids),
            scratch=[pltpu.VMEM((2 * count, 2 * LANES), F32)],
        )
        stats = call(
            functools.partial(last_kernel, width),
            stats_shape,
            [VMEM] * 7,
            (far_weights, table, left, left_side, c2, wide, token_ids),
            scratch=[pltpu.VMEM((up(2 * count), LANES), F32), pltpu.VMEM((count, 2 * LANES), F32)],
        )
        stats = combine([stats] + [send(stats, perm_z[k]) for k in (1, 2, 3)])
        stats = combine(
            [stats]
            + [send(stats, mesh_perm(lambda s, d, v=v: (s ^ v[0], d ^ v[1]))) for v in ((0, 1), (2, 0), (2, 1))]
        )
    else:
        other = lax.ppermute(full, "section", over)
        ordered = jnp.concatenate([jnp.where(pair == 0, full, other), jnp.where(pair == 0, other, full)])
        everything = lax.all_gather(ordered, "dp", axis=1, tiled=True)
        acc = jnp.concatenate(
            [jnp.dot(everything, h, preferred_element_type=F32) for h in (head, head_sibling)], axis=1
        )
        gains, weights_all = (lax.all_gather(table[i], "dp", axis=0, tiled=True) for i in range(2))
        wide = everything.astype(F32)
        square = jnp.sum(wide * wide * gains, axis=1, keepdims=True)
        reward = jnp.sum(wide * weights_all, axis=1, keepdims=True)
        stats = call(
            functools.partial(whole_kernel, width), stats_shape, [VMEM] * 4, (acc, square, reward, token_ids)
        )
        gathered = lax.all_gather(stats, "dp")
        stats = combine([gathered[i] for i in range(groups)])
        stats = combine([stats, lax.ppermute(stats, "section", over)])
    filled = jnp.arange(stats.shape[1], dtype=jnp.int32)[None, :] < 2 * count
    lp = jnp.where(filled, stats[2:3] - (stats[0:1] + jnp.log(stats[1:2])), F32(0.0))
    lp = jnp.concatenate([lp, stats[3:4], jnp.zeros((6, lp.shape[1]), F32)])
    logprob, score = call(
        final_kernel,
        [jax.ShapeDtypeStruct((1, positions), F32), jax.ShapeDtypeStruct((1, 1), F32)],
        [VMEM] * 4,
        (lp, lax.ppermute(lp, "section", swap), hit, per_row),
    )
    return (logprob, score[0])


def solution(mesh):
    groups = mesh.shape["dp"]
    return jax.shard_map(
        lambda *args: per_device(groups, *args),
        mesh=mesh,
        in_specs=(P("section", None, "dp"), P("dp"), P(None, ("section", "dp")), P("dp"), P(), P()),
        out_specs=(P("section", None), P("section")),
        check_vma=False,
    )
```

```python
import functools

import jax
import jax.numpy as jnp
from jax import lax
from jax.experimental import pallas as pl
from jax.experimental.pallas import tpu as pltpu
from jax.sharding import PartitionSpec as P

AXES = ("section", "dp")
F32 = jnp.float32
BF16 = jnp.bfloat16
I32 = jnp.int32
LANES = 128
VMEM = pl.BlockSpec(memory_space=pltpu.VMEM)
SMEM = pl.BlockSpec(memory_space=pltpu.SMEM)
ANY = pl.BlockSpec(memory_space=pl.ANY)


def row_map(lengths, pair, core, index, count):
    first, second = lengths[2 * pair], lengths[2 * pair + 1]
    other_first = lengths[2 - 2 * pair]
    j = core * count + index
    in_first = j < first
    in_second = j < first + second
    span = jnp.where(in_first, 2 * pair, jnp.where(in_second, 2 * pair + 1, 3 - 2 * pair))
    place = jnp.where(
        in_first, j, jnp.where(in_second, j - first, 2 * count - other_first + j - first - second)
    )
    return span, place


def as_rows(columns, count):
    lane = lax.broadcasted_iota(I32, (count, LANES), 1)
    wide = jnp.zeros((count, LANES), F32)
    for i, column in enumerate(columns):
        wide = jnp.where(lane == i, column, wide)
    return jnp.transpose(wide)[:8]


def as_column(rows, which):
    full = jnp.concatenate([rows, jnp.zeros((LANES - 8, rows.shape[1]), F32)], axis=0)
    return jnp.transpose(full)[:, which : which + 1]


def table_kernel(gain, reward, rows, table, rows_out):
    rows_out[...] = rows[...]
    value = gain[...].astype(F32)
    table[0:1, :] = 1.0 / (value * value)
    table[1:2, :] = reward[...].astype(F32)


def pick_kernel(count, lengths, rows, sibling, extra, gain, table, after, full, table_out):
    section = lax.axis_index("section")
    core, pair = lax.rem(section, 2), lax.div(section, 2)
    positions, half = rows.shape[0], extra.shape[0]
    index = lax.broadcasted_iota(I32, (count, 1), 0)
    span, place = row_map(lengths, pair, core, index, count)
    source = jnp.where(span == section, place, place + positions)
    source = jnp.where(span // 2 == pair, source, place + (2 * positions - (positions - half)))
    lane = lax.broadcasted_iota(I32, (count, 2 * positions + half), 1)
    pick = jnp.where(lane == source, F32(1.0), F32(0.0)).astype(BF16)
    picked = jnp.dot(pick[:, :positions], rows[...], preferred_element_type=F32)
    picked += jnp.dot(pick[:, positions : 2 * positions], sibling[...], preferred_element_type=F32)
    picked += jnp.dot(pick[:, 2 * positions :], extra[...], preferred_element_type=F32)
    full[...] = (picked * gain[...].astype(F32)).astype(BF16)
    table_out[...] = table[...]


def token_kernel(count, lengths, tokens, out, hit, per_row):
    section, core, _ = here()
    spans, positions = tokens.shape
    index = lax.broadcasted_iota(I32, (count, 1), 0)
    lane = lax.broadcasted_iota(I32, (count, positions), 1)
    hit[...] = jnp.zeros(hit.shape, F32)
    for pair in range(2):
        rows = slice(pair * count, pair * count + count)
        span, place = row_map(lengths, pair, core, index, count)
        found = jnp.zeros((count, positions), F32)
        for s in range(spans):
            found = jnp.where(span == s, tokens[s : s + 1, :].astype(F32), found)
        here_is = lane == place
        found = jnp.sum(jnp.where(here_is, found, F32(0.0)), axis=1, keepdims=True)
        out[rows, :] = found.astype(I32)
        hit[0, rows, :] = jnp.where(here_is & (span == section), F32(1.0), F32(0.0))
        span, place = row_map(lengths, pair, 1 - core, index, count)
        hit[1, rows, :] = jnp.where((lane == place) & (span == section), F32(1.0), F32(0.0))
    per_row[...] = jnp.zeros(per_row.shape, F32) + 1.0 / lengths[section].astype(F32)


def here():
    section = lax.axis_index("section")
    return section, lax.rem(section, 2), lax.div(section, 2)


def blocks(count):
    _, _, pair = here()
    return pl.multiple_of(pair * count, 16), pl.multiple_of((1 - pair) * count, 16)


def weights(head, sibling, depth, k, far):
    dp_index = lax.axis_index("dp")
    where = jnp.bitwise_xor(dp_index, 2 * k + (1 if far else 0))
    rows = pl.ds(pl.multiple_of(where * depth, depth), depth)
    return head[rows, :], sibling[rows, :]


def products(terms):
    value = jnp.concatenate([t[0] for t in terms], axis=1) if len(terms) > 1 else terms[0][0]
    out = []
    for side in range(2):
        w = [t[1][side] for t in terms]
        w = jnp.concatenate(w, axis=0) if len(w) > 1 else w[0]
        out.append(jnp.dot(value, w, preferred_element_type=F32))
    return jnp.concatenate(out, axis=1)


def add_sides(terms, base, side_in, side):
    step = 32
    count, depth = terms[0][0].shape

    def body(i, _):
        rows = pl.ds(pl.multiple_of(i * step, step), step)
        at = pl.ds(pl.multiple_of(base + i * step, step), step)
        square, reward = jnp.zeros((step, LANES), F32), jnp.zeros((step, LANES), F32)
        if side_in is not None:
            square, reward = side_in[at, :LANES], side_in[at, LANES:]
        for piece, table, k in terms:
            for c in range(depth // LANES):
                cols = slice(c * LANES, (c + 1) * LANES)
                value = piece[rows, cols].astype(F32)
                square += value * value * table[2 * k : 2 * k + 1, cols]
                reward += value * table[2 * k + 1 : 2 * k + 2, cols]
        side[at, :LANES] = square
        side[at, LANES:] = reward
        return 0

    lax.fori_loop(0, count // step, body, 0)


def both_weights(head, sibling, depth, k):
    return weights(head, sibling, depth, k, False), weights(head, sibling, depth, k, True)


def begin_kernel(head, sibling, table, z, a, b, c, z1, a1, b1, ids, after, acc, side, ids_out):
    count, depth = z.shape
    _, core, _ = here()
    mine, others = blocks(count)
    near0, far0 = both_weights(head, sibling, depth, 0)
    for which, k, same, cross, same1, cross1 in ((0, 1, a, b, a1, b1), (1, 3, b, a, b1, a1)):

        @pl.when(core == which)
        def _():
            near1, far1 = both_weights(head, sibling, depth, k)
            rows = pl.ds(mine, count)
            acc[rows, :] = products([(z[...], near0), (same[...], far0), (z1[...], near1), (same1[...], far1)])
            terms = [(z, table, 0), (same, table, 1), (z1, table, 2 * k), (same1, table, 2 * k + 1)]
            add_sides(terms, mine, None, side)
            rows = pl.ds(others, count)
            acc[rows, :] = products([(cross[...], near0), (c[...], far0), (cross1[...], near1)])
            add_sides([(cross, table, 0), (c, table, 1), (cross1, table, 2 * k)], others, None, side)

    ids_out[...] = ids[...]


def middle_kernel(head, sibling, table, acc_in, side_in, z, a, b, c, acc, side):
    count, depth = z.shape
    _, core, _ = here()
    mine, others = blocks(count)
    for which, k, same, cross in ((0, 3, a, b), (1, 1, b, a)):

        @pl.when(core == which)
        def _():
            near3, far3 = both_weights(head, sibling, depth, k)
            rows = pl.ds(mine, count)
            acc[rows, :] = acc_in[rows, :] + products([(z[...], near3), (same[...], far3)])
            add_sides([(z, table, 2 * k), (same, table, 2 * k + 1)], mine, side_in, side)
            rows = pl.ds(others, count)
            acc[rows, :] = acc_in[rows, :] + products([(cross[...], near3), (c[...], far3)])
            add_sides([(cross, table, 2 * k), (c, table, 2 * k + 1)], others, side_in, side)


def gate_kernel(value, *refs):
    refs[-1][...] = value[: refs[-1].shape[0], :]


def padded_kernel(value, after, out):
    out[: value.shape[0], :] = value[...]
    out[value.shape[0] :, :] = jnp.zeros((out.shape[0] - value.shape[0], out.shape[1]), out.dtype)


def column_ids(block):
    section, core, _ = here()
    dp_index, groups = lax.axis_index("dp"), lax.axis_size("dp")
    lane = lax.broadcasted_iota(I32, (1, block), 1)
    own = (section * groups + dp_index) * block
    other = ((section + 1 - 2 * core) * groups + dp_index) * block
    return jnp.concatenate([lane + own, lane + other], axis=1)


def summary(logits, square, reward, token_ids, ids, width):
    scale = lax.rsqrt(square / width + 1e-05)
    logits = logits * scale
    top = jnp.max(logits, axis=1, keepdims=True)
    total = jnp.sum(jnp.exp(logits - top), axis=1, keepdims=True)
    target = jnp.sum(jnp.where(ids == token_ids, logits, F32(0.0)), axis=1, keepdims=True)
    lane = lax.broadcasted_iota(I32, (logits.shape[0], LANES), 1)
    wide = jnp.where(lane == 2, target, jnp.where(lane == 3, reward * scale, F32(0.0)))
    return jnp.where(lane == 0, top, jnp.where(lane == 1, total, wide))


def added(side):
    return jnp.sum(side[:, :LANES], axis=1, keepdims=True), jnp.sum(side[:, LANES:], axis=1, keepdims=True)


def own_kernel(width, head, sibling, table, acc_in, side_in, z, a, b, c1, token_ids, left, left_side, far_out, wide, side):
    count, depth = z.shape
    _, core, _ = here()
    mine, others = blocks(count)
    near2, far2 = weights(head, sibling, depth, 2, False), weights(head, sibling, depth, 2, True)
    block = head.shape[1]
    far_out[:, :block] = far2[0]
    far_out[:, block:] = far2[1]
    ids = column_ids(block)
    wide[...] = jnp.zeros(wide.shape, F32)
    for which, k, same, cross in ((0, 1, a, b), (1, 3, b, a)):

        @pl.when(core == which)
        def _():
            far1 = weights(head, sibling, depth, k, True)
            rows = pl.ds(mine, count)
            logits = acc_in[rows, :] + products([(z[...], near2), (same[...], far2)])
            add_sides([(z, table, 4), (same, table, 5)], mine, side_in, side)
            square, reward = added(side[rows, :])
            wide[rows, :] = summary(logits, square, reward, token_ids[rows, :], ids, width)
            rows = pl.ds(others, count)
            left[...] = acc_in[rows, :] + products([(cross[...], near2), (c1[...], far1)])
            add_sides([(cross, table, 4), (c1, table, 2 * k + 1)], others, side_in, side)
            left_side[...] = side[rows, :]


def last_kernel(width, far_weights, table, left, left_side, c, wide_in, token_ids, out, wide, side):
    count = c.shape[0]
    _, others = blocks(count)
    ids = column_ids(far_weights.shape[1] // 2)
    wide[...] = wide_in[...]
    logits = left[...] + jnp.dot(c[...], far_weights[...], preferred_element_type=F32)
    add_sides([(c, table, 5)], 0, left_side, side)
    square, reward = added(side[...])
    rows = pl.ds(others, count)
    wide[rows, :] = summary(logits, square, reward, token_ids[rows, :], ids, width)
    out[...] = jnp.transpose(wide[...])[:8]


def whole_kernel(width, acc, square, reward, token_ids, out):
    count = acc.shape[0] // 2
    ids = column_ids(acc.shape[1] // 2)
    wide = summary(acc[...], square[...], reward[...], token_ids[...], ids, width)
    wide = jnp.concatenate([wide, jnp.zeros((out.shape[1] - 2 * count, LANES), F32)])
    out[...] = jnp.transpose(wide)[:8]


def final_kernel(mine, sibling, hit, per_row, out_ref, score_ref):
    exact = functools.partial(jnp.dot, precision=lax.Precision.HIGHEST, preferred_element_type=F32)
    picked = exact(mine[...], hit[0]) + exact(sibling[...], hit[1])
    out_ref[...] = picked[0:1, :]
    score_ref[...] = jnp.sum(picked[1:2, :], axis=1, keepdims=True) * per_row[0:1, 0:1]


def combine(parts):
    top = parts[0][0]
    for part in parts[1:]:
        top = jnp.maximum(top, part[0])
    total = sum(part[1] * jnp.exp(part[0] - top) for part in parts)
    target = sum(part[2] for part in parts)
    return jnp.concatenate([jnp.stack([top, total, target, parts[0][3]]), jnp.zeros((4,) + top.shape, F32)])


def call(body, outs, in_specs, args, limit=16, scratch=()):
    many = isinstance(outs, (list, tuple))
    return pl.pallas_call(
        body,
        out_shape=outs,
        in_specs=in_specs,
        out_specs=[VMEM] * len(outs) if many else VMEM,
        scratch_shapes=scratch,
        compiler_params=pltpu.CompilerParams(vmem_limit_bytes=limit << 20),
    )(*args)


def up(value):
    return -(-value // LANES) * LANES


def per_device(groups, hidden, norm_gain, head, reward_head, tokens, lengths):
    section = lax.axis_index("section")
    core, pair = section % 2, section // 2
    sections = lax.axis_size("section")
    spans, positions = tokens.shape
    block, width, part = head.shape[1], head.shape[0], hidden.shape[2]
    count = 3 * spans * positions // 4 // sections
    half = positions // 2
    rows = hidden[0]

    def mesh_perm(move):
        pairs = []
        for s in range(sections):
            for d in range(groups):
                s2, d2 = move(s, d)
                pairs.append((s * groups + d, s2 * groups + d2))
        return pairs

    send = lambda value, perm: lax.ppermute(value, AXES, perm)
    like = lambda v: jax.ShapeDtypeStruct(v.shape, v.dtype)
    acc_shape = jax.ShapeDtypeStruct((2 * count, 2 * block), F32)
    stats_shape = jax.ShapeDtypeStruct((8, up(2 * count)), F32)
    ids_shape = jax.ShapeDtypeStruct((2 * count, 1), I32)
    perm_z = {k: mesh_perm(lambda s, d, k=k: (s, d ^ (2 * k))) for k in (1, 2, 3)}
    perm_x = mesh_perm(lambda s, d: (s, d ^ 1))
    gain = norm_gain[None]

    swap = [(s, s ^ 1) for s in range(sections)]
    over = [(s, s ^ 2) for s in range(sections)]
    extra = lax.ppermute(rows[half:], "section", [(1, 3), (3, 1)])
    sibling = lax.ppermute(rows, "section", swap)
    head_sibling = lax.ppermute(head, "section", swap)
    table, rows = call(
        table_kernel, [jax.ShapeDtypeStruct((2, part), F32), like(rows)], [VMEM] * 3, (gain, reward_head[None], rows)
    )

    if groups == 8:
        table = jnp.concatenate([table, send(table, perm_x)])
    full, table = call(
        functools.partial(pick_kernel, count),
        [jax.ShapeDtypeStruct((count, part), BF16), like(table)],
        [SMEM] + [VMEM] * 5 + [ANY],
        (lengths, rows, sibling, extra, gain, table, head_sibling),
    )
    token_ids, hit, per_row = call(
        functools.partial(token_kernel, count),
        [
            ids_shape,
            jax.ShapeDtypeStruct((2, up(2 * count), positions), F32),
            jax.ShapeDtypeStruct((8, LANES), F32),
        ],
        [SMEM, VMEM],
        (lengths, tokens),
    )

    if groups == 8:
        perm_a = mesh_perm(lambda s, d: (s, d ^ 1) if s % 2 == 0 else (s ^ 2, d))
        perm_b = mesh_perm(lambda s, d: (s ^ 2, d) if s % 2 == 0 else (s, d ^ 1))

        def gate(value, *after):
            return call(gate_kernel, like(value), [VMEM] + [ANY] * len(after), (value,) + after)

        side_shape = jax.ShapeDtypeStruct((2 * count, 2 * LANES), F32)
        perm_e = mesh_perm(lambda s, d: (s, d ^ (2 if s % 2 == 0 else 6)))
        perm_f = mesh_perm(lambda s, d: (s, d ^ (6 if s % 2 == 0 else 2)))
        z1 = send(full, perm_e)
        a0 = send(full, perm_a)
        b0 = send(full, perm_b)
        table = jnp.concatenate([table, send(table, perm_z[1])])
        z3 = send(call(padded_kernel, jax.ShapeDtypeStruct((count + 16, part), BF16), [VMEM, ANY], (full, z1)), perm_f)
        z1 = gate(z1, b0, table, token_ids)
        a1 = send(z1, perm_a)
        b1 = send(z1, perm_b)
        c0 = send(a0, perm_b)
        z3 = call(gate_kernel, like(full), [VMEM] + [ANY], (z3, a1))
        a3 = send(z3, perm_a)
        table = jnp.concatenate([table, send(table, perm_z[2])])
        z2 = send(gate(z1, table), perm_f)
        z3 = gate(z3, b1, c0)
        b3 = send(z3, perm_b)
        acc, side, token_ids = call(
            begin_kernel,
            [acc_shape, side_shape, ids_shape],
            [VMEM] * 11 + [ANY],
            (head, head_sibling, table, full, a0, b0, c0, z1, a1, b1, token_ids, z3),
        )
        a3 = gate(a3, token_ids)
        c3 = send(a3, perm_b)
        a2 = send(z2, perm_a)
        b2 = send(z2, perm_b)
        c1 = send(c0, perm_e)
        acc, side = call(
            middle_kernel,
            [acc_shape, side_shape],
            [VMEM] * 9,
            (head, head_sibling, table, acc, side, z3, a3, b3, c3),
        )
        a2 = gate(a2, side)
        c2 = send(a2, perm_b)
        left, left_side, far_weights, wide = call(
            functools.partial(own_kernel, width),
            [
                jax.ShapeDtypeStruct((count, 2 * block), F32),
                jax.ShapeDtypeStruct((count, 2 * LANES), F32),
                jax.ShapeDtypeStruct((part, 2 * block), BF16),
                jax.ShapeDtypeStruct((up(2 * count), LANES), F32),
            ],
            [VMEM] * 10,
            (head, head_sibling, table, acc, side, z2, a2, b2, c1, token_ids),
            scratch=[pltpu.VMEM((2 * count, 2 * LANES), F32)],
        )
        stats = call(
            functools.partial(last_kernel, width),
            stats_shape,
            [VMEM] * 7,
            (far_weights, table, left, left_side, c2, wide, token_ids),
            scratch=[pltpu.VMEM((up(2 * count), LANES), F32), pltpu.VMEM((count, 2 * LANES), F32)],
        )
        stats = combine([stats] + [send(stats, perm_z[k]) for k in (1, 2, 3)])
        stats = combine(
            [stats]
            + [send(stats, mesh_perm(lambda s, d, v=v: (s ^ v[0], d ^ v[1]))) for v in ((0, 1), (2, 0), (2, 1))]
        )
    else:
        other = lax.ppermute(full, "section", over)
        ordered = jnp.concatenate([jnp.where(pair == 0, full, other), jnp.where(pair == 0, other, full)])
        everything = lax.all_gather(ordered, "dp", axis=1, tiled=True)
        acc = jnp.concatenate(
            [jnp.dot(everything, h, preferred_element_type=F32) for h in (head, head_sibling)], axis=1
        )
        gains, weights_all = (lax.all_gather(table[i], "dp", axis=0, tiled=True) for i in range(2))
        wide = everything.astype(F32)
        square = jnp.sum(wide * wide * gains, axis=1, keepdims=True)
        reward = jnp.sum(wide * weights_all, axis=1, keepdims=True)
        stats = call(
            functools.partial(whole_kernel, width), stats_shape, [VMEM] * 4, (acc, square, reward, token_ids)
        )
        gathered = lax.all_gather(stats, "dp")
        stats = combine([gathered[i] for i in range(groups)])
        stats = combine([stats, lax.ppermute(stats, "section", over)])
    filled = jnp.arange(stats.shape[1], dtype=jnp.int32)[None, :] < 2 * count
    lp = jnp.where(filled, stats[2:3] - (stats[0:1] + jnp.log(stats[1:2])), F32(0.0))
    lp = jnp.concatenate([lp, stats[3:4], jnp.zeros((6, lp.shape[1]), F32)])
    logprob, score = call(
        final_kernel,
        [jax.ShapeDtypeStruct((1, positions), F32), jax.ShapeDtypeStruct((1, 1), F32)],
        [VMEM] * 4,
        (lp, lax.ppermute(lp, "section", swap), hit, per_row),
    )
    return (logprob, score[0])


def solution(mesh):
    groups = mesh.shape["dp"]
    return jax.shard_map(
        lambda *args: per_device(groups, *args),
        mesh=mesh,
        in_specs=(P("section", None, "dp"), P("dp"), P(None, ("section", "dp")), P("dp"), P(), P()),
        out_specs=(P("section", None), P("section")),
        check_vma=False,
    )
```

```python
import functools

import jax
import jax.numpy as jnp
from jax import lax
from jax.experimental import pallas as pl
from jax.experimental.pallas import tpu as pltpu
from jax.sharding import PartitionSpec as P

AXES = ("section", "dp")
F32 = jnp.float32
BF16 = jnp.bfloat16
I32 = jnp.int32
LANES = 128
VMEM = pl.BlockSpec(memory_space=pltpu.VMEM)
SMEM = pl.BlockSpec(memory_space=pltpu.SMEM)
ANY = pl.BlockSpec(memory_space=pl.ANY)


def row_map(lengths, pair, core, index, count):
    first, second = lengths[2 * pair], lengths[2 * pair + 1]
    other_first = lengths[2 - 2 * pair]
    j = core * count + index
    in_first = j < first
    in_second = j < first + second
    span = jnp.where(in_first, 2 * pair, jnp.where(in_second, 2 * pair + 1, 3 - 2 * pair))
    place = jnp.where(
        in_first, j, jnp.where(in_second, j - first, 2 * count - other_first + j - first - second)
    )
    return span, place


def as_rows(columns, count):
    lane = lax.broadcasted_iota(I32, (count, LANES), 1)
    wide = jnp.zeros((count, LANES), F32)
    for i, column in enumerate(columns):
        wide = jnp.where(lane == i, column, wide)
    return jnp.transpose(wide)[:8]


def as_column(rows, which):
    full = jnp.concatenate([rows, jnp.zeros((LANES - 8, rows.shape[1]), F32)], axis=0)
    return jnp.transpose(full)[:, which : which + 1]


def table_kernel(gain, reward, rows, table, rows_out):
    rows_out[...] = rows[...]
    value = gain[...].astype(F32)
    table[0:1, :] = 1.0 / (value * value)
    table[1:2, :] = reward[...].astype(F32)


def pick_kernel(count, lengths, rows, sibling, extra, gain, table, after, full, table_out):
    section = lax.axis_index("section")
    core, pair = lax.rem(section, 2), lax.div(section, 2)
    positions, half = rows.shape[0], extra.shape[0]
    index = lax.broadcasted_iota(I32, (count, 1), 0)
    span, place = row_map(lengths, pair, core, index, count)
    source = jnp.where(span == section, place, place + positions)
    source = jnp.where(span // 2 == pair, source, place + (2 * positions - (positions - half)))
    lane = lax.broadcasted_iota(I32, (count, 2 * positions + half), 1)
    pick = jnp.where(lane == source, F32(1.0), F32(0.0)).astype(BF16)
    picked = jnp.dot(pick[:, :positions], rows[...], preferred_element_type=F32)
    picked += jnp.dot(pick[:, positions : 2 * positions], sibling[...], preferred_element_type=F32)
    picked += jnp.dot(pick[:, 2 * positions :], extra[...], preferred_element_type=F32)
    full[...] = (picked * gain[...].astype(F32)).astype(BF16)
    table_out[...] = table[...]


def token_kernel(count, lengths, tokens, out, hit, per_row):
    section, core, _ = here()
    spans, positions = tokens.shape
    index = lax.broadcasted_iota(I32, (count, 1), 0)
    lane = lax.broadcasted_iota(I32, (count, positions), 1)
    hit[...] = jnp.zeros(hit.shape, BF16)
    for pair in range(2):
        rows = slice(pair * count, pair * count + count)
        span, place = row_map(lengths, pair, core, index, count)
        found = jnp.zeros((count, positions), F32)
        for s in range(spans):
            found = jnp.where(span == s, tokens[s : s + 1, :].astype(F32), found)
        here_is = lane == place
        found = jnp.sum(jnp.where(here_is, found, F32(0.0)), axis=1, keepdims=True)
        out[rows, :] = found.astype(I32)
        hit[0, rows, :] = jnp.where(here_is & (span == section), F32(1.0), F32(0.0)).astype(BF16)
        span, place = row_map(lengths, pair, 1 - core, index, count)
        hit[1, rows, :] = jnp.where((lane == place) & (span == section), F32(1.0), F32(0.0)).astype(BF16)
    per_row[...] = jnp.zeros(per_row.shape, F32) + 1.0 / lengths[section].astype(F32)


def here():
    section = lax.axis_index("section")
    return section, lax.rem(section, 2), lax.div(section, 2)


def blocks(count):
    _, _, pair = here()
    return pl.multiple_of(pair * count, 16), pl.multiple_of((1 - pair) * count, 16)


def weights(head, sibling, depth, k, far):
    dp_index = lax.axis_index("dp")
    where = jnp.bitwise_xor(dp_index, 2 * k + (1 if far else 0))
    rows = pl.ds(pl.multiple_of(where * depth, depth), depth)
    return head[rows, :], sibling[rows, :]


def products(terms):
    value = jnp.concatenate([t[0] for t in terms], axis=1) if len(terms) > 1 else terms[0][0]
    out = []
    for side in range(2):
        w = [t[1][side] for t in terms]
        w = jnp.concatenate(w, axis=0) if len(w) > 1 else w[0]
        out.append(jnp.dot(value, w, preferred_element_type=F32))
    return jnp.concatenate(out, axis=1)


def add_sides(terms, base, side_in, side):
    step = 32
    count, depth = terms[0][0].shape

    def body(i, _):
        rows = pl.ds(pl.multiple_of(i * step, step), step)
        at = pl.ds(pl.multiple_of(base + i * step, step), step)
        square, reward = jnp.zeros((step, LANES), F32), jnp.zeros((step, LANES), F32)
        if side_in is not None:
            square, reward = side_in[at, :LANES], side_in[at, LANES:]
        for piece, table, k in terms:
            for c in range(depth // LANES):
                cols = slice(c * LANES, (c + 1) * LANES)
                value = piece[rows, cols].astype(F32)
                square += value * value * table[2 * k : 2 * k + 1, cols]
                reward += value * table[2 * k + 1 : 2 * k + 2, cols]
        side[at, :LANES] = square
        side[at, LANES:] = reward
        return 0

    lax.fori_loop(0, count // step, body, 0)


def both_weights(head, sibling, depth, k):
    return weights(head, sibling, depth, k, False), weights(head, sibling, depth, k, True)


def begin_kernel(head, sibling, table, z, a, b, c, z1, a1, b1, ids, after, acc, side, ids_out):
    count, depth = z.shape
    _, core, _ = here()
    mine, others = blocks(count)
    near0, far0 = both_weights(head, sibling, depth, 0)
    for which, k, same, cross, same1, cross1 in ((0, 1, a, b, a1, b1), (1, 3, b, a, b1, a1)):

        @pl.when(core == which)
        def _():
            near1, far1 = both_weights(head, sibling, depth, k)
            rows = pl.ds(mine, count)
            acc[rows, :] = products([(z[...], near0), (same[...], far0), (z1[...], near1), (same1[...], far1)])
            terms = [(z, table, 0), (same, table, 1), (z1, table, 2 * k), (same1, table, 2 * k + 1)]
            add_sides(terms, mine, None, side)
            rows = pl.ds(others, count)
            acc[rows, :] = products([(cross[...], near0), (c[...], far0), (cross1[...], near1)])
            add_sides([(cross, table, 0), (c, table, 1), (cross1, table, 2 * k)], others, None, side)

    ids_out[...] = ids[...]


def middle_kernel(head, sibling, table, acc_in, side_in, z, a, b, c, acc, side):
    count, depth = z.shape
    _, core, _ = here()
    mine, others = blocks(count)
    for which, k, same, cross in ((0, 3, a, b), (1, 1, b, a)):

        @pl.when(core == which)
        def _():
            near3, far3 = both_weights(head, sibling, depth, k)
            rows = pl.ds(mine, count)
            acc[rows, :] = acc_in[rows, :] + products([(z[...], near3), (same[...], far3)])
            add_sides([(z, table, 2 * k), (same, table, 2 * k + 1)], mine, side_in, side)
            rows = pl.ds(others, count)
            acc[rows, :] = acc_in[rows, :] + products([(cross[...], near3), (c[...], far3)])
            add_sides([(cross, table, 2 * k), (c, table, 2 * k + 1)], others, side_in, side)


def gate_kernel(value, *refs):
    refs[-1][...] = value[: refs[-1].shape[0], :]


def padded_kernel(value, after, out):
    out[: value.shape[0], :] = value[...]
    out[value.shape[0] :, :] = jnp.zeros((out.shape[0] - value.shape[0], out.shape[1]), out.dtype)


def column_ids(block):
    section, core, _ = here()
    dp_index, groups = lax.axis_index("dp"), lax.axis_size("dp")
    lane = lax.broadcasted_iota(I32, (1, block), 1)
    own = (section * groups + dp_index) * block
    other = ((section + 1 - 2 * core) * groups + dp_index) * block
    return jnp.concatenate([lane + own, lane + other], axis=1)


def summary(logits, square, reward, token_ids, ids, width):
    scale = lax.rsqrt(square / width + 1e-05)
    logits = logits * scale
    top = jnp.max(logits, axis=1, keepdims=True)
    total = jnp.sum(jnp.exp(logits - top), axis=1, keepdims=True)
    target = jnp.sum(jnp.where(ids == token_ids, logits, F32(0.0)), axis=1, keepdims=True)
    lane = lax.broadcasted_iota(I32, (logits.shape[0], LANES), 1)
    wide = jnp.where(lane == 2, target, jnp.where(lane == 3, reward * scale, F32(0.0)))
    return jnp.where(lane == 0, top, jnp.where(lane == 1, total, wide))


def added(side):
    return jnp.sum(side[:, :LANES], axis=1, keepdims=True), jnp.sum(side[:, LANES:], axis=1, keepdims=True)


def own_kernel(width, head, sibling, table, acc_in, side_in, z, a, b, c1, token_ids, left, left_side, far_out, wide, side):
    count, depth = z.shape
    _, core, _ = here()
    mine, others = blocks(count)
    near2, far2 = weights(head, sibling, depth, 2, False), weights(head, sibling, depth, 2, True)
    block = head.shape[1]
    far_out[:, :block] = far2[0]
    far_out[:, block:] = far2[1]
    ids = column_ids(block)
    wide[...] = jnp.zeros(wide.shape, F32)
    for which, k, same, cross in ((0, 1, a, b), (1, 3, b, a)):

        @pl.when(core == which)
        def _():
            far1 = weights(head, sibling, depth, k, True)
            rows = pl.ds(mine, count)
            logits = acc_in[rows, :] + products([(z[...], near2), (same[...], far2)])
            add_sides([(z, table, 4), (same, table, 5)], mine, side_in, side)
            square, reward = added(side[rows, :])
            wide[rows, :] = summary(logits, square, reward, token_ids[rows, :], ids, width)
            rows = pl.ds(others, count)
            left[...] = acc_in[rows, :] + products([(cross[...], near2), (c1[...], far1)])
            add_sides([(cross, table, 4), (c1, table, 2 * k + 1)], others, side_in, side)
            left_side[...] = side[rows, :]


def last_kernel(width, far_weights, table, left, left_side, c, wide_in, token_ids, out, wide, side):
    count = c.shape[0]
    _, others = blocks(count)
    ids = column_ids(far_weights.shape[1] // 2)
    wide[...] = wide_in[...]
    logits = left[...] + jnp.dot(c[...], far_weights[...], preferred_element_type=F32)
    add_sides([(c, table, 5)], 0, left_side, side)
    square, reward = added(side[...])
    rows = pl.ds(others, count)
    wide[rows, :] = summary(logits, square, reward, token_ids[rows, :], ids, width)
    out[...] = jnp.transpose(wide[...])[:8]


def whole_kernel(width, acc, square, reward, token_ids, out):
    count = acc.shape[0] // 2
    ids = column_ids(acc.shape[1] // 2)
    wide = summary(acc[...], square[...], reward[...], token_ids[...], ids, width)
    wide = jnp.concatenate([wide, jnp.zeros((out.shape[1] - 2 * count, LANES), F32)])
    out[...] = jnp.transpose(wide)[:8]


def final_kernel(mine, sibling, hit, per_row, out_ref, score_ref):
    picked = jnp.zeros((8, hit.shape[2]), F32)
    for core, values in enumerate((mine, sibling)):
        rest, terms = values[0:2, :], []
        for _ in range(3):
            terms.append(rest.astype(BF16).astype(F32))
            rest = rest - terms[-1]
        stacked = jnp.concatenate(terms + [jnp.zeros_like(rest)], axis=0).astype(BF16)
        picked += jnp.dot(stacked, hit[core], preferred_element_type=F32)
    picked = picked[0:2, :] + (picked[2:4, :] + picked[4:6, :])
    out_ref[...] = picked[0:1, :]
    score_ref[...] = jnp.sum(picked[1:2, :], axis=1, keepdims=True) * per_row[0:1, 0:1]


def combine(parts):
    top = parts[0][0]
    for part in parts[1:]:
        top = jnp.maximum(top, part[0])
    total = sum(part[1] * jnp.exp(part[0] - top) for part in parts)
    target = sum(part[2] for part in parts)
    return jnp.concatenate([jnp.stack([top, total, target, parts[0][3]]), jnp.zeros((4,) + top.shape, F32)])


def call(body, outs, in_specs, args, limit=16, scratch=()):
    many = isinstance(outs, (list, tuple))
    return pl.pallas_call(
        body,
        out_shape=outs,
        in_specs=in_specs,
        out_specs=[VMEM] * len(outs) if many else VMEM,
        scratch_shapes=scratch,
        compiler_params=pltpu.CompilerParams(vmem_limit_bytes=limit << 20),
    )(*args)


def up(value):
    return -(-value // LANES) * LANES


def per_device(groups, hidden, norm_gain, head, reward_head, tokens, lengths):
    section = lax.axis_index("section")
    core, pair = section % 2, section // 2
    sections = lax.axis_size("section")
    spans, positions = tokens.shape
    block, width, part = head.shape[1], head.shape[0], hidden.shape[2]
    count = 3 * spans * positions // 4 // sections
    half = positions // 2
    rows = hidden[0]

    def mesh_perm(move):
        pairs = []
        for s in range(sections):
            for d in range(groups):
                s2, d2 = move(s, d)
                pairs.append((s * groups + d, s2 * groups + d2))
        return pairs

    send = lambda value, perm: lax.ppermute(value, AXES, perm)
    like = lambda v: jax.ShapeDtypeStruct(v.shape, v.dtype)
    acc_shape = jax.ShapeDtypeStruct((2 * count, 2 * block), F32)
    stats_shape = jax.ShapeDtypeStruct((8, up(2 * count)), F32)
    ids_shape = jax.ShapeDtypeStruct((2 * count, 1), I32)
    perm_z = {k: mesh_perm(lambda s, d, k=k: (s, d ^ (2 * k))) for k in (1, 2, 3)}
    perm_x = mesh_perm(lambda s, d: (s, d ^ 1))
    gain = norm_gain[None]

    swap = [(s, s ^ 1) for s in range(sections)]
    over = [(s, s ^ 2) for s in range(sections)]
    extra = lax.ppermute(rows[half:], "section", [(1, 3), (3, 1)])
    sibling = lax.ppermute(rows, "section", swap)
    head_sibling = lax.ppermute(head, "section", swap)
    table, rows = call(
        table_kernel, [jax.ShapeDtypeStruct((2, part), F32), like(rows)], [VMEM] * 3, (gain, reward_head[None], rows)
    )

    if groups == 8:
        table = jnp.concatenate([table, send(table, perm_x)])
    full, table = call(
        functools.partial(pick_kernel, count),
        [jax.ShapeDtypeStruct((count, part), BF16), like(table)],
        [SMEM] + [VMEM] * 5 + [ANY],
        (lengths, rows, sibling, extra, gain, table, head_sibling),
    )
    token_ids, hit, per_row = call(
        functools.partial(token_kernel, count),
        [
            ids_shape,
            jax.ShapeDtypeStruct((2, up(2 * count), positions), BF16),
            jax.ShapeDtypeStruct((8, LANES), F32),
        ],
        [SMEM, VMEM],
        (lengths, tokens),
    )

    if groups == 8:
        perm_a = mesh_perm(lambda s, d: (s, d ^ 1) if s % 2 == 0 else (s ^ 2, d))
        perm_b = mesh_perm(lambda s, d: (s ^ 2, d) if s % 2 == 0 else (s, d ^ 1))

        def gate(value, *after):
            return call(gate_kernel, like(value), [VMEM] + [ANY] * len(after), (value,) + after)

        side_shape = jax.ShapeDtypeStruct((2 * count, 2 * LANES), F32)
        perm_e = mesh_perm(lambda s, d: (s, d ^ (2 if s % 2 == 0 else 6)))
        perm_f = mesh_perm(lambda s, d: (s, d ^ (6 if s % 2 == 0 else 2)))
        z1 = send(full, perm_e)
        a0 = send(full, perm_a)
        b0 = send(full, perm_b)
        table = jnp.concatenate([table, send(table, perm_z[1])])
        z3 = send(call(padded_kernel, jax.ShapeDtypeStruct((count + 16, part), BF16), [VMEM, ANY], (full, z1)), perm_f)
        z1 = gate(z1, b0, table, token_ids)
        a1 = send(z1, perm_a)
        b1 = send(z1, perm_b)
        c0 = send(a0, perm_b)
        z3 = call(gate_kernel, like(full), [VMEM] + [ANY], (z3, a1))
        a3 = send(z3, perm_a)
        table = jnp.concatenate([table, send(table, perm_z[2])])
        z2 = send(gate(z1, table), perm_f)
        z3 = gate(z3, b1, c0)
        b3 = send(z3, perm_b)
        acc, side, token_ids = call(
            begin_kernel,
            [acc_shape, side_shape, ids_shape],
            [VMEM] * 11 + [ANY],
            (head, head_sibling, table, full, a0, b0, c0, z1, a1, b1, token_ids, z3),
        )
        a3 = gate(a3, token_ids)
        c3 = send(a3, perm_b)
        a2 = send(z2, perm_a)
        b2 = send(z2, perm_b)
        c1 = send(c0, perm_e)
        acc, side = call(
            middle_kernel,
            [acc_shape, side_shape],
            [VMEM] * 9,
            (head, head_sibling, table, acc, side, z3, a3, b3, c3),
        )
        a2 = gate(a2, side)
        c2 = send(a2, perm_b)
        left, left_side, far_weights, wide = call(
            functools.partial(own_kernel, width),
            [
                jax.ShapeDtypeStruct((count, 2 * block), F32),
                jax.ShapeDtypeStruct((count, 2 * LANES), F32),
                jax.ShapeDtypeStruct((part, 2 * block), BF16),
                jax.ShapeDtypeStruct((up(2 * count), LANES), F32),
            ],
            [VMEM] * 10,
            (head, head_sibling, table, acc, side, z2, a2, b2, c1, token_ids),
            scratch=[pltpu.VMEM((2 * count, 2 * LANES), F32)],
        )
        stats = call(
            functools.partial(last_kernel, width),
            stats_shape,
            [VMEM] * 7,
            (far_weights, table, left, left_side, c2, wide, token_ids),
            scratch=[pltpu.VMEM((up(2 * count), LANES), F32), pltpu.VMEM((count, 2 * LANES), F32)],
        )
        stats = combine([stats] + [send(stats, perm_z[k]) for k in (1, 2, 3)])
        stats = combine(
            [stats]
            + [send(stats, mesh_perm(lambda s, d, v=v: (s ^ v[0], d ^ v[1]))) for v in ((0, 1), (2, 0), (2, 1))]
        )
    else:
        other = lax.ppermute(full, "section", over)
        ordered = jnp.concatenate([jnp.where(pair == 0, full, other), jnp.where(pair == 0, other, full)])
        everything = lax.all_gather(ordered, "dp", axis=1, tiled=True)
        acc = jnp.concatenate(
            [jnp.dot(everything, h, preferred_element_type=F32) for h in (head, head_sibling)], axis=1
        )
        gains, weights_all = (lax.all_gather(table[i], "dp", axis=0, tiled=True) for i in range(2))
        wide = everything.astype(F32)
        square = jnp.sum(wide * wide * gains, axis=1, keepdims=True)
        reward = jnp.sum(wide * weights_all, axis=1, keepdims=True)
        stats = call(
            functools.partial(whole_kernel, width), stats_shape, [VMEM] * 4, (acc, square, reward, token_ids)
        )
        gathered = lax.all_gather(stats, "dp")
        stats = combine([gathered[i] for i in range(groups)])
        stats = combine([stats, lax.ppermute(stats, "section", over)])
    filled = jnp.arange(stats.shape[1], dtype=jnp.int32)[None, :] < 2 * count
    lp = jnp.where(filled, stats[2:3] - (stats[0:1] + jnp.log(stats[1:2])), F32(0.0))
    lp = jnp.concatenate([lp, stats[3:4], jnp.zeros((6, lp.shape[1]), F32)])
    logprob, score = call(
        final_kernel,
        [jax.ShapeDtypeStruct((1, positions), F32), jax.ShapeDtypeStruct((1, 1), F32)],
        [VMEM] * 4,
        (lp, lax.ppermute(lp, "section", swap), hit, per_row),
    )
    return (logprob, score[0])


def solution(mesh):
    groups = mesh.shape["dp"]
    return jax.shard_map(
        lambda *args: per_device(groups, *args),
        mesh=mesh,
        in_specs=(P("section", None, "dp"), P("dp"), P(None, ("section", "dp")), P("dp"), P(), P()),
        out_specs=(P("section", None), P("section")),
        check_vma=False,
    )
```

```python
import functools

import jax
import jax.numpy as jnp
from jax import lax
from jax.experimental import pallas as pl
from jax.experimental.pallas import tpu as pltpu
from jax.sharding import PartitionSpec as P

AXES = ("section", "dp")
F32 = jnp.float32
BF16 = jnp.bfloat16
I32 = jnp.int32
LANES = 128
VMEM = pl.BlockSpec(memory_space=pltpu.VMEM)
SMEM = pl.BlockSpec(memory_space=pltpu.SMEM)
ANY = pl.BlockSpec(memory_space=pl.ANY)


def row_map(lengths, pair, core, index, count):
    first, second = lengths[2 * pair], lengths[2 * pair + 1]
    other_first = lengths[2 - 2 * pair]
    j = core * count + index
    in_first = j < first
    in_second = j < first + second
    span = jnp.where(in_first, 2 * pair, jnp.where(in_second, 2 * pair + 1, 3 - 2 * pair))
    place = jnp.where(
        in_first, j, jnp.where(in_second, j - first, 2 * count - other_first + j - first - second)
    )
    return span, place


def as_rows(columns, count):
    lane = lax.broadcasted_iota(I32, (count, LANES), 1)
    wide = jnp.zeros((count, LANES), F32)
    for i, column in enumerate(columns):
        wide = jnp.where(lane == i, column, wide)
    return jnp.transpose(wide)[:8]


def as_column(rows, which):
    full = jnp.concatenate([rows, jnp.zeros((LANES - 8, rows.shape[1]), F32)], axis=0)
    return jnp.transpose(full)[:, which : which + 1]


def table_kernel(gain, reward, rows, table, rows_out):
    rows_out[...] = rows[...]
    value = gain[...].astype(F32)
    table[0:1, :] = 1.0 / (value * value)
    table[1:2, :] = reward[...].astype(F32)


def pick_kernel(count, lengths, rows, sibling, extra, gain, table, after, ids, full, table_out):
    section = lax.axis_index("section")
    core, pair = lax.rem(section, 2), lax.div(section, 2)
    positions, half = rows.shape[0], extra.shape[0]
    index = lax.broadcasted_iota(I32, (count, 1), 0)
    span, place = row_map(lengths, pair, core, index, count)
    source = jnp.where(span == section, place, place + positions)
    source = jnp.where(span // 2 == pair, source, place + (2 * positions - (positions - half)))
    lane = lax.broadcasted_iota(I32, (count, 2 * positions + half), 1)
    pick = jnp.where(lane == source, F32(1.0), F32(0.0)).astype(BF16)
    picked = jnp.dot(pick[:, :positions], rows[...], preferred_element_type=F32)
    picked += jnp.dot(pick[:, positions : 2 * positions], sibling[...], preferred_element_type=F32)
    picked += jnp.dot(pick[:, 2 * positions :], extra[...], preferred_element_type=F32)
    full[...] = (picked * gain[...].astype(F32)).astype(BF16)
    table_out[...] = table[...]


def token_kernel(count, lengths, tokens, out, hit, per_row):
    section, core, _ = here()
    spans, positions = tokens.shape
    index = lax.broadcasted_iota(I32, (count, 1), 0)
    lane = lax.broadcasted_iota(I32, (count, positions), 1)
    hit[...] = jnp.zeros(hit.shape, BF16)
    for pair in range(2):
        rows = slice(pair * count, pair * count + count)
        span, place = row_map(lengths, pair, core, index, count)
        found = jnp.zeros((count, positions), F32)
        for s in range(spans):
            found = jnp.where(span == s, tokens[s : s + 1, :].astype(F32), found)
        here_is = lane == place
        found = jnp.sum(jnp.where(here_is, found, F32(0.0)), axis=1, keepdims=True)
        out[rows, :] = found.astype(I32)
        hit[0, rows, :] = jnp.where(here_is & (span == section), F32(1.0), F32(0.0)).astype(BF16)
        span, place = row_map(lengths, pair, 1 - core, index, count)
        hit[1, rows, :] = jnp.where((lane == place) & (span == section), F32(1.0), F32(0.0)).astype(BF16)
    per_row[...] = jnp.zeros(per_row.shape, F32) + 1.0 / lengths[section].astype(F32)


def here():
    section = lax.axis_index("section")
    return section, lax.rem(section, 2), lax.div(section, 2)


def blocks(count):
    _, _, pair = here()
    return pl.multiple_of(pair * count, 16), pl.multiple_of((1 - pair) * count, 16)


def weights(head, sibling, depth, k, far):
    dp_index = lax.axis_index("dp")
    where = jnp.bitwise_xor(dp_index, 2 * k + (1 if far else 0))
    rows = pl.ds(pl.multiple_of(where * depth, depth), depth)
    return head[rows, :], sibling[rows, :]


def products(terms):
    value = jnp.concatenate([t[0] for t in terms], axis=1) if len(terms) > 1 else terms[0][0]
    out = []
    for side in range(2):
        w = [t[1][side] for t in terms]
        w = jnp.concatenate(w, axis=0) if len(w) > 1 else w[0]
        out.append(jnp.dot(value, w, preferred_element_type=F32))
    return jnp.concatenate(out, axis=1)


def add_sides(terms, base, side_in, side):
    step = 32
    count, depth = terms[0][0].shape

    def body(i, _):
        rows = pl.ds(pl.multiple_of(i * step, step), step)
        at = pl.ds(pl.multiple_of(base + i * step, step), step)
        square, reward = jnp.zeros((step, LANES), F32), jnp.zeros((step, LANES), F32)
        if side_in is not None:
            square, reward = side_in[at, :LANES], side_in[at, LANES:]
        for piece, table, k in terms:
            for c in range(depth // LANES):
                cols = slice(c * LANES, (c + 1) * LANES)
                value = piece[rows, cols].astype(F32)
                square += value * value * table[2 * k : 2 * k + 1, cols]
                reward += value * table[2 * k + 1 : 2 * k + 2, cols]
        side[at, :LANES] = square
        side[at, LANES:] = reward
        return 0

    lax.fori_loop(0, count // step, body, 0)


def both_weights(head, sibling, depth, k):
    return weights(head, sibling, depth, k, False), weights(head, sibling, depth, k, True)


def begin_kernel(head, sibling, table, z, a, b, c, z1, a1, b1, ids, after, acc, side, ids_out):
    count, depth = z.shape
    _, core, _ = here()
    mine, others = blocks(count)
    near0, far0 = both_weights(head, sibling, depth, 0)
    for which, k, same, cross, same1, cross1 in ((0, 1, a, b, a1, b1), (1, 3, b, a, b1, a1)):

        @pl.when(core == which)
        def _():
            near1, far1 = both_weights(head, sibling, depth, k)
            rows = pl.ds(mine, count)
            acc[rows, :] = products([(z[...], near0), (same[...], far0), (z1[...], near1), (same1[...], far1)])
            terms = [(z, table, 0), (same, table, 1), (z1, table, 2 * k), (same1, table, 2 * k + 1)]
            add_sides(terms, mine, None, side)
            rows = pl.ds(others, count)
            acc[rows, :] = products([(cross[...], near0), (c[...], far0), (cross1[...], near1)])
            add_sides([(cross, table, 0), (c, table, 1), (cross1, table, 2 * k)], others, None, side)

    ids_out[...] = ids[...]


def middle_kernel(head, sibling, table, acc_in, side_in, z, a, b, c, acc, side):
    count, depth = z.shape
    _, core, _ = here()
    mine, others = blocks(count)
    for which, k, same, cross in ((0, 3, a, b), (1, 1, b, a)):

        @pl.when(core == which)
        def _():
            near3, far3 = both_weights(head, sibling, depth, k)
            rows = pl.ds(mine, count)
            acc[rows, :] = acc_in[rows, :] + products([(z[...], near3), (same[...], far3)])
            add_sides([(z, table, 2 * k), (same, table, 2 * k + 1)], mine, side_in, side)
            rows = pl.ds(others, count)
            acc[rows, :] = acc_in[rows, :] + products([(cross[...], near3), (c[...], far3)])
            add_sides([(cross, table, 2 * k), (c, table, 2 * k + 1)], others, side_in, side)


def gate_kernel(value, *refs):
    refs[-1][...] = value[: refs[-1].shape[0], :]


def padded_kernel(value, after, out):
    out[: value.shape[0], :] = value[...]
    out[value.shape[0] :, :] = jnp.zeros((out.shape[0] - value.shape[0], out.shape[1]), out.dtype)


def column_ids(block):
    section, core, _ = here()
    dp_index, groups = lax.axis_index("dp"), lax.axis_size("dp")
    lane = lax.broadcasted_iota(I32, (1, block), 1)
    own = (section * groups + dp_index) * block
    other = ((section + 1 - 2 * core) * groups + dp_index) * block
    return jnp.concatenate([lane + own, lane + other], axis=1)


def summary(logits, square, reward, token_ids, ids, width):
    scale = lax.rsqrt(square / width + 1e-05)
    logits = logits * scale
    top = jnp.max(logits, axis=1, keepdims=True)
    total = jnp.sum(jnp.exp(logits - top), axis=1, keepdims=True)
    target = jnp.sum(jnp.where(ids == token_ids, logits, F32(0.0)), axis=1, keepdims=True)
    lane = lax.broadcasted_iota(I32, (logits.shape[0], LANES), 1)
    wide = jnp.where(lane == 2, target, jnp.where(lane == 3, reward * scale, F32(0.0)))
    return jnp.where(lane == 0, top, jnp.where(lane == 1, total, wide))


def added(side):
    return jnp.sum(side[:, :LANES], axis=1, keepdims=True), jnp.sum(side[:, LANES:], axis=1, keepdims=True)


def own_kernel(width, head, sibling, table, acc_in, side_in, z, a, b, c1, token_ids, left, left_side, far_out, wide, side):
    count, depth = z.shape
    _, core, _ = here()
    mine, others = blocks(count)
    near2, far2 = weights(head, sibling, depth, 2, False), weights(head, sibling, depth, 2, True)
    block = head.shape[1]
    far_out[:, :block] = far2[0]
    far_out[:, block:] = far2[1]
    ids = column_ids(block)
    wide[...] = jnp.zeros(wide.shape, F32)
    for which, k, same, cross in ((0, 1, a, b), (1, 3, b, a)):

        @pl.when(core == which)
        def _():
            far1 = weights(head, sibling, depth, k, True)
            rows = pl.ds(mine, count)
            logits = acc_in[rows, :] + products([(z[...], near2), (same[...], far2)])
            add_sides([(z, table, 4), (same, table, 5)], mine, side_in, side)
            square, reward = added(side[rows, :])
            wide[rows, :] = summary(logits, square, reward, token_ids[rows, :], ids, width)
            rows = pl.ds(others, count)
            left[...] = acc_in[rows, :] + products([(cross[...], near2), (c1[...], far1)])
            add_sides([(cross, table, 4), (c1, table, 2 * k + 1)], others, side_in, side)
            left_side[...] = side[rows, :]


def last_kernel(width, far_weights, table, left, left_side, c, wide_in, token_ids, out, wide, side):
    count = c.shape[0]
    _, others = blocks(count)
    ids = column_ids(far_weights.shape[1] // 2)
    wide[...] = wide_in[...]
    logits = left[...] + jnp.dot(c[...], far_weights[...], preferred_element_type=F32)
    add_sides([(c, table, 5)], 0, left_side, side)
    square, reward = added(side[...])
    rows = pl.ds(others, count)
    wide[rows, :] = summary(logits, square, reward, token_ids[rows, :], ids, width)
    out[...] = jnp.transpose(wide[...])[:8]


def whole_kernel(width, acc, square, reward, token_ids, out):
    count = acc.shape[0] // 2
    ids = column_ids(acc.shape[1] // 2)
    wide = summary(acc[...], square[...], reward[...], token_ids[...], ids, width)
    wide = jnp.concatenate([wide, jnp.zeros((out.shape[1] - 2 * count, LANES), F32)])
    out[...] = jnp.transpose(wide)[:8]


def final_kernel(mine, sibling, hit, per_row, out_ref, score_ref):
    picked = jnp.zeros((8, hit.shape[2]), F32)
    for core, values in enumerate((mine, sibling)):
        rest, terms = values[0:2, :], []
        for _ in range(3):
            terms.append(rest.astype(BF16).astype(F32))
            rest = rest - terms[-1]
        stacked = jnp.concatenate(terms + [jnp.zeros_like(rest)], axis=0).astype(BF16)
        picked += jnp.dot(stacked, hit[core], preferred_element_type=F32)
    picked = picked[0:2, :] + (picked[2:4, :] + picked[4:6, :])
    out_ref[...] = picked[0:1, :]
    score_ref[...] = jnp.sum(picked[1:2, :], axis=1, keepdims=True) * per_row[0:1, 0:1]


def combine(parts):
    top = parts[0][0]
    for part in parts[1:]:
        top = jnp.maximum(top, part[0])
    total = sum(part[1] * jnp.exp(part[0] - top) for part in parts)
    target = sum(part[2] for part in parts)
    return jnp.concatenate([jnp.stack([top, total, target, parts[0][3]]), jnp.zeros((4,) + top.shape, F32)])


def call(body, outs, in_specs, args, limit=16, scratch=()):
    many = isinstance(outs, (list, tuple))
    return pl.pallas_call(
        body,
        out_shape=outs,
        in_specs=in_specs,
        out_specs=[VMEM] * len(outs) if many else VMEM,
        scratch_shapes=scratch,
        compiler_params=pltpu.CompilerParams(vmem_limit_bytes=limit << 20),
    )(*args)


def up(value):
    return -(-value // LANES) * LANES


def per_device(groups, hidden, norm_gain, head, reward_head, tokens, lengths):
    section = lax.axis_index("section")
    core, pair = section % 2, section // 2
    sections = lax.axis_size("section")
    spans, positions = tokens.shape
    block, width, part = head.shape[1], head.shape[0], hidden.shape[2]
    count = 3 * spans * positions // 4 // sections
    half = positions // 2
    rows = hidden[0]

    def mesh_perm(move):
        pairs = []
        for s in range(sections):
            for d in range(groups):
                s2, d2 = move(s, d)
                pairs.append((s * groups + d, s2 * groups + d2))
        return pairs

    send = lambda value, perm: lax.ppermute(value, AXES, perm)
    like = lambda v: jax.ShapeDtypeStruct(v.shape, v.dtype)
    acc_shape = jax.ShapeDtypeStruct((2 * count, 2 * block), F32)
    stats_shape = jax.ShapeDtypeStruct((8, up(2 * count)), F32)
    ids_shape = jax.ShapeDtypeStruct((2 * count, 1), I32)
    perm_z = {k: mesh_perm(lambda s, d, k=k: (s, d ^ (2 * k))) for k in (1, 2, 3)}
    perm_x = mesh_perm(lambda s, d: (s, d ^ 1))
    gain = norm_gain[None]

    swap = [(s, s ^ 1) for s in range(sections)]
    over = [(s, s ^ 2) for s in range(sections)]
    extra = lax.ppermute(rows[half:], "section", [(1, 3), (3, 1)])
    sibling = lax.ppermute(rows, "section", swap)
    head_sibling = lax.ppermute(head, "section", swap)
    table, rows = call(
        table_kernel, [jax.ShapeDtypeStruct((2, part), F32), like(rows)], [VMEM] * 3, (gain, reward_head[None], rows)
    )

    if groups == 8:
        table = jnp.concatenate([table, send(table, perm_x)])
    token_ids, hit, per_row = call(
        functools.partial(token_kernel, count),
        [
            ids_shape,
            jax.ShapeDtypeStruct((2, up(2 * count), positions), BF16),
            jax.ShapeDtypeStruct((8, LANES), F32),
        ],
        [SMEM, VMEM],
        (lengths, tokens),
    )
    full, table = call(
        functools.partial(pick_kernel, count),
        [jax.ShapeDtypeStruct((count, part), BF16), like(table)],
        [SMEM] + [VMEM] * 5 + [ANY] * 2,
        (lengths, rows, sibling, extra, gain, table, head_sibling, token_ids),
    )

    if groups == 8:
        perm_a = mesh_perm(lambda s, d: (s, d ^ 1) if s % 2 == 0 else (s ^ 2, d))
        perm_b = mesh_perm(lambda s, d: (s ^ 2, d) if s % 2 == 0 else (s, d ^ 1))

        def gate(value, *after):
            return call(gate_kernel, like(value), [VMEM] + [ANY] * len(after), (value,) + after)

        side_shape = jax.ShapeDtypeStruct((2 * count, 2 * LANES), F32)
        perm_e = mesh_perm(lambda s, d: (s, d ^ (2 if s % 2 == 0 else 6)))
        perm_f = mesh_perm(lambda s, d: (s, d ^ (6 if s % 2 == 0 else 2)))
        z1 = send(full, perm_e)
        a0 = send(full, perm_a)
        b0 = send(full, perm_b)
        table = jnp.concatenate([table, send(table, perm_z[1])])
        z3 = send(call(padded_kernel, jax.ShapeDtypeStruct((count + 16, part), BF16), [VMEM, ANY], (full, z1)), perm_f)
        z1 = gate(z1, b0, table)
        a1 = send(z1, perm_a)
        b1 = send(z1, perm_b)
        c0 = send(a0, perm_b)
        z3 = call(gate_kernel, like(full), [VMEM] + [ANY], (z3, a1))
        a3 = send(z3, perm_a)
        table = jnp.concatenate([table, send(table, perm_z[2])])
        z2 = send(gate(z1, table), perm_f)
        z3 = gate(z3, b1, c0)
        b3 = send(z3, perm_b)
        acc, side, token_ids = call(
            begin_kernel,
            [acc_shape, side_shape, ids_shape],
            [VMEM] * 11 + [ANY],
            (head, head_sibling, table, full, a0, b0, c0, z1, a1, b1, token_ids, z3),
        )
        a3 = gate(a3, token_ids)
        c3 = send(a3, perm_b)
        a2 = send(z2, perm_a)
        b2 = send(z2, perm_b)
        c1 = send(c0, perm_e)
        acc, side = call(
            middle_kernel,
            [acc_shape, side_shape],
            [VMEM] * 9,
            (head, head_sibling, table, acc, side, z3, a3, b3, c3),
        )
        a2 = gate(a2, side)
        c2 = send(a2, perm_b)
        left, left_side, far_weights, wide = call(
            functools.partial(own_kernel, width),
            [
                jax.ShapeDtypeStruct((count, 2 * block), F32),
                jax.ShapeDtypeStruct((count, 2 * LANES), F32),
                jax.ShapeDtypeStruct((part, 2 * block), BF16),
                jax.ShapeDtypeStruct((up(2 * count), LANES), F32),
            ],
            [VMEM] * 10,
            (head, head_sibling, table, acc, side, z2, a2, b2, c1, token_ids),
            scratch=[pltpu.VMEM((2 * count, 2 * LANES), F32)],
        )
        stats = call(
            functools.partial(last_kernel, width),
            stats_shape,
            [VMEM] * 7,
            (far_weights, table, left, left_side, c2, wide, token_ids),
            scratch=[pltpu.VMEM((up(2 * count), LANES), F32), pltpu.VMEM((count, 2 * LANES), F32)],
        )
        stats = combine([stats] + [send(stats, perm_z[k]) for k in (1, 2, 3)])
        stats = combine(
            [stats]
            + [send(stats, mesh_perm(lambda s, d, v=v: (s ^ v[0], d ^ v[1]))) for v in ((0, 1), (2, 0), (2, 1))]
        )
    else:
        other = lax.ppermute(full, "section", over)
        ordered = jnp.concatenate([jnp.where(pair == 0, full, other), jnp.where(pair == 0, other, full)])
        everything = lax.all_gather(ordered, "dp", axis=1, tiled=True)
        acc = jnp.concatenate(
            [jnp.dot(everything, h, preferred_element_type=F32) for h in (head, head_sibling)], axis=1
        )
        gains, weights_all = (lax.all_gather(table[i], "dp", axis=0, tiled=True) for i in range(2))
        wide = everything.astype(F32)
        square = jnp.sum(wide * wide * gains, axis=1, keepdims=True)
        reward = jnp.sum(wide * weights_all, axis=1, keepdims=True)
        stats = call(
            functools.partial(whole_kernel, width), stats_shape, [VMEM] * 4, (acc, square, reward, token_ids)
        )
        gathered = lax.all_gather(stats, "dp")
        stats = combine([gathered[i] for i in range(groups)])
        stats = combine([stats, lax.ppermute(stats, "section", over)])
    filled = jnp.arange(stats.shape[1], dtype=jnp.int32)[None, :] < 2 * count
    lp = jnp.where(filled, stats[2:3] - (stats[0:1] + jnp.log(stats[1:2])), F32(0.0))
    lp = jnp.concatenate([lp, stats[3:4], jnp.zeros((6, lp.shape[1]), F32)])
    logprob, score = call(
        final_kernel,
        [jax.ShapeDtypeStruct((1, positions), F32), jax.ShapeDtypeStruct((1, 1), F32)],
        [VMEM] * 4,
        (lp, lax.ppermute(lp, "section", swap), hit, per_row),
    )
    return (logprob, score[0])


def solution(mesh):
    groups = mesh.shape["dp"]
    return jax.shard_map(
        lambda *args: per_device(groups, *args),
        mesh=mesh,
        in_specs=(P("section", None, "dp"), P("dp"), P(None, ("section", "dp")), P("dp"), P(), P()),
        out_specs=(P("section", None), P("section")),
        check_vma=False,
    )
```

```python
import functools

import jax
import jax.numpy as jnp
from jax import lax
from jax.experimental import pallas as pl
from jax.experimental.pallas import tpu as pltpu
from jax.sharding import PartitionSpec as P

AXES = ("section", "dp")
F32 = jnp.float32
BF16 = jnp.bfloat16
I32 = jnp.int32
LANES = 128
VMEM = pl.BlockSpec(memory_space=pltpu.VMEM)
SMEM = pl.BlockSpec(memory_space=pltpu.SMEM)
ANY = pl.BlockSpec(memory_space=pl.ANY)


def row_map(lengths, pair, core, index, count):
    first, second = lengths[2 * pair], lengths[2 * pair + 1]
    other_first = lengths[2 - 2 * pair]
    j = core * count + index
    in_first = j < first
    in_second = j < first + second
    span = jnp.where(in_first, 2 * pair, jnp.where(in_second, 2 * pair + 1, 3 - 2 * pair))
    place = jnp.where(
        in_first, j, jnp.where(in_second, j - first, 2 * count - other_first + j - first - second)
    )
    return span, place


def as_rows(columns, count):
    lane = lax.broadcasted_iota(I32, (count, LANES), 1)
    wide = jnp.zeros((count, LANES), F32)
    for i, column in enumerate(columns):
        wide = jnp.where(lane == i, column, wide)
    return jnp.transpose(wide)[:8]


def as_column(rows, which):
    full = jnp.concatenate([rows, jnp.zeros((LANES - 8, rows.shape[1]), F32)], axis=0)
    return jnp.transpose(full)[:, which : which + 1]


def table_kernel(gain, reward, rows, table, rows_out):
    rows_out[...] = rows[...]
    value = gain[...].astype(F32)
    table[0:1, :] = 1.0 / (value * value)
    table[1:2, :] = reward[...].astype(F32)


def pick_kernel(count, lengths, rows, sibling, extra, gain, table, after, ids, full, table_out):
    section = lax.axis_index("section")
    core, pair = lax.rem(section, 2), lax.div(section, 2)
    positions, half = rows.shape[0], extra.shape[0]
    index = lax.broadcasted_iota(I32, (count, 1), 0)
    span, place = row_map(lengths, pair, core, index, count)
    source = jnp.where(span == section, place, place + positions)
    source = jnp.where(span // 2 == pair, source, place + (2 * positions - (positions - half)))
    lane = lax.broadcasted_iota(I32, (count, 2 * positions + half), 1)
    pick = jnp.where(lane == source, F32(1.0), F32(0.0)).astype(BF16)
    picked = jnp.dot(pick[:, :positions], rows[...], preferred_element_type=F32)
    picked += jnp.dot(pick[:, positions : 2 * positions], sibling[...], preferred_element_type=F32)
    picked += jnp.dot(pick[:, 2 * positions :], extra[...], preferred_element_type=F32)
    full[...] = (picked * gain[...].astype(F32)).astype(BF16)
    table_out[...] = table[...]


def token_kernel(count, lengths, tokens, out):
    _, core, _ = here()
    spans, positions = tokens.shape
    index = lax.broadcasted_iota(I32, (count, 1), 0)
    lane = lax.broadcasted_iota(I32, (count, positions), 1)
    for pair in range(2):
        span, place = row_map(lengths, pair, core, index, count)
        found = jnp.zeros((count, positions), F32)
        for s in range(spans):
            found = jnp.where(span == s, tokens[s : s + 1, :].astype(F32), found)
        found = jnp.sum(jnp.where(lane == place, found, F32(0.0)), axis=1, keepdims=True)
        out[pair * count : pair * count + count, :] = found.astype(I32)


def mask_kernel(count, lengths, hit, per_row):
    section, core, _ = here()
    positions = hit.shape[2]
    index = lax.broadcasted_iota(I32, (count, 1), 0)
    lane = lax.broadcasted_iota(I32, (count, positions), 1)
    hit[...] = jnp.zeros(hit.shape, BF16)
    for pair in range(2):
        rows = slice(pair * count, pair * count + count)
        for which in range(2):
            span, place = row_map(lengths, pair, core + which - 2 * core * which, index, count)
            here_is = (lane == place) & (span == section)
            hit[which, rows, :] = jnp.where(here_is, F32(1.0), F32(0.0)).astype(BF16)
    per_row[...] = jnp.zeros(per_row.shape, F32) + 1.0 / lengths[section].astype(F32)


def here():
    section = lax.axis_index("section")
    return section, lax.rem(section, 2), lax.div(section, 2)


def blocks(count):
    _, _, pair = here()
    return pl.multiple_of(pair * count, 16), pl.multiple_of((1 - pair) * count, 16)


def weights(head, sibling, depth, k, far):
    dp_index = lax.axis_index("dp")
    where = jnp.bitwise_xor(dp_index, 2 * k + (1 if far else 0))
    rows = pl.ds(pl.multiple_of(where * depth, depth), depth)
    return head[rows, :], sibling[rows, :]


def products(terms):
    value = jnp.concatenate([t[0] for t in terms], axis=1) if len(terms) > 1 else terms[0][0]
    out = []
    for side in range(2):
        w = [t[1][side] for t in terms]
        w = jnp.concatenate(w, axis=0) if len(w) > 1 else w[0]
        out.append(jnp.dot(value, w, preferred_element_type=F32))
    return jnp.concatenate(out, axis=1)


def add_sides(terms, base, side_in, side):
    step = 32
    count, depth = terms[0][0].shape

    def body(i, _):
        rows = pl.ds(pl.multiple_of(i * step, step), step)
        at = pl.ds(pl.multiple_of(base + i * step, step), step)
        square, reward = jnp.zeros((step, LANES), F32), jnp.zeros((step, LANES), F32)
        if side_in is not None:
            square, reward = side_in[at, :LANES], side_in[at, LANES:]
        for piece, table, k in terms:
            for c in range(depth // LANES):
                cols = slice(c * LANES, (c + 1) * LANES)
                value = piece[rows, cols].astype(F32)
                square += value * value * table[2 * k : 2 * k + 1, cols]
                reward += value * table[2 * k + 1 : 2 * k + 2, cols]
        side[at, :LANES] = square
        side[at, LANES:] = reward
        return 0

    lax.fori_loop(0, count // step, body, 0)


def both_weights(head, sibling, depth, k):
    return weights(head, sibling, depth, k, False), weights(head, sibling, depth, k, True)


def begin_kernel(head, sibling, table, z, a, b, c, z1, a1, b1, ids, after, acc, side, ids_out):
    count, depth = z.shape
    _, core, _ = here()
    mine, others = blocks(count)
    near0, far0 = both_weights(head, sibling, depth, 0)
    for which, k, same, cross, same1, cross1 in ((0, 1, a, b, a1, b1), (1, 3, b, a, b1, a1)):

        @pl.when(core == which)
        def _():
            near1, far1 = both_weights(head, sibling, depth, k)
            rows = pl.ds(mine, count)
            acc[rows, :] = products([(z[...], near0), (same[...], far0), (z1[...], near1), (same1[...], far1)])
            terms = [(z, table, 0), (same, table, 1), (z1, table, 2 * k), (same1, table, 2 * k + 1)]
            add_sides(terms, mine, None, side)
            rows = pl.ds(others, count)
            acc[rows, :] = products([(cross[...], near0), (c[...], far0), (cross1[...], near1)])
            add_sides([(cross, table, 0), (c, table, 1), (cross1, table, 2 * k)], others, None, side)

    ids_out[...] = ids[...]


def middle_kernel(head, sibling, table, acc_in, side_in, z, a, b, c, acc, side):
    count, depth = z.shape
    _, core, _ = here()
    mine, others = blocks(count)
    for which, k, same, cross in ((0, 3, a, b), (1, 1, b, a)):

        @pl.when(core == which)
        def _():
            near3, far3 = both_weights(head, sibling, depth, k)
            rows = pl.ds(mine, count)
            acc[rows, :] = acc_in[rows, :] + products([(z[...], near3), (same[...], far3)])
            add_sides([(z, table, 2 * k), (same, table, 2 * k + 1)], mine, side_in, side)
            rows = pl.ds(others, count)
            acc[rows, :] = acc_in[rows, :] + products([(cross[...], near3), (c[...], far3)])
            add_sides([(cross, table, 2 * k), (c, table, 2 * k + 1)], others, side_in, side)


def gate_kernel(value, *refs):
    refs[-1][...] = value[: refs[-1].shape[0], :]


def padded_kernel(value, after, out):
    out[: value.shape[0], :] = value[...]
    out[value.shape[0] :, :] = jnp.zeros((out.shape[0] - value.shape[0], out.shape[1]), out.dtype)


def column_ids(block):
    section, core, _ = here()
    dp_index, groups = lax.axis_index("dp"), lax.axis_size("dp")
    lane = lax.broadcasted_iota(I32, (1, block), 1)
    own = (section * groups + dp_index) * block
    other = ((section + 1 - 2 * core) * groups + dp_index) * block
    return jnp.concatenate([lane + own, lane + other], axis=1)


def summary(logits, square, reward, token_ids, ids, width):
    scale = lax.rsqrt(square / width + 1e-05)
    logits = logits * scale
    top = jnp.max(logits, axis=1, keepdims=True)
    total = jnp.sum(jnp.exp(logits - top), axis=1, keepdims=True)
    target = jnp.sum(jnp.where(ids == token_ids, logits, F32(0.0)), axis=1, keepdims=True)
    lane = lax.broadcasted_iota(I32, (logits.shape[0], LANES), 1)
    wide = jnp.where(lane == 2, target, jnp.where(lane == 3, reward * scale, F32(0.0)))
    return jnp.where(lane == 0, top, jnp.where(lane == 1, total, wide))


def added(side):
    return jnp.sum(side[:, :LANES], axis=1, keepdims=True), jnp.sum(side[:, LANES:], axis=1, keepdims=True)


def own_kernel(width, head, sibling, table, acc_in, side_in, z, a, b, c1, token_ids, left, left_side, far_out, wide, side):
    count, depth = z.shape
    _, core, _ = here()
    mine, others = blocks(count)
    near2, far2 = weights(head, sibling, depth, 2, False), weights(head, sibling, depth, 2, True)
    block = head.shape[1]
    far_out[:, :block] = far2[0]
    far_out[:, block:] = far2[1]
    ids = column_ids(block)
    wide[...] = jnp.zeros(wide.shape, F32)
    for which, k, same, cross in ((0, 1, a, b), (1, 3, b, a)):

        @pl.when(core == which)
        def _():
            far1 = weights(head, sibling, depth, k, True)
            rows = pl.ds(mine, count)
            logits = acc_in[rows, :] + products([(z[...], near2), (same[...], far2)])
            add_sides([(z, table, 4), (same, table, 5)], mine, side_in, side)
            square, reward = added(side[rows, :])
            wide[rows, :] = summary(logits, square, reward, token_ids[rows, :], ids, width)
            rows = pl.ds(others, count)
            left[...] = acc_in[rows, :] + products([(cross[...], near2), (c1[...], far1)])
            add_sides([(cross, table, 4), (c1, table, 2 * k + 1)], others, side_in, side)
            left_side[...] = side[rows, :]


def last_kernel(width, far_weights, table, left, left_side, c, wide_in, token_ids, out, wide, side):
    count = c.shape[0]
    _, others = blocks(count)
    ids = column_ids(far_weights.shape[1] // 2)
    wide[...] = wide_in[...]
    logits = left[...] + jnp.dot(c[...], far_weights[...], preferred_element_type=F32)
    add_sides([(c, table, 5)], 0, left_side, side)
    square, reward = added(side[...])
    rows = pl.ds(others, count)
    wide[rows, :] = summary(logits, square, reward, token_ids[rows, :], ids, width)
    out[...] = jnp.transpose(wide[...])[:8]


def whole_kernel(width, acc, square, reward, token_ids, out):
    count = acc.shape[0] // 2
    ids = column_ids(acc.shape[1] // 2)
    wide = summary(acc[...], square[...], reward[...], token_ids[...], ids, width)
    wide = jnp.concatenate([wide, jnp.zeros((out.shape[1] - 2 * count, LANES), F32)])
    out[...] = jnp.transpose(wide)[:8]


def final_kernel(mine, sibling, hit, per_row, out_ref, score_ref):
    picked = jnp.zeros((8, hit.shape[2]), F32)
    for core, values in enumerate((mine, sibling)):
        rest, terms = values[0:2, :], []
        for _ in range(3):
            terms.append(rest.astype(BF16).astype(F32))
            rest = rest - terms[-1]
        stacked = jnp.concatenate(terms + [jnp.zeros_like(rest)], axis=0).astype(BF16)
        picked += jnp.dot(stacked, hit[core], preferred_element_type=F32)
    picked = picked[0:2, :] + (picked[2:4, :] + picked[4:6, :])
    out_ref[...] = picked[0:1, :]
    score_ref[...] = jnp.sum(picked[1:2, :], axis=1, keepdims=True) * per_row[0:1, 0:1]


def combine(parts):
    top = parts[0][0]
    for part in parts[1:]:
        top = jnp.maximum(top, part[0])
    total = sum(part[1] * jnp.exp(part[0] - top) for part in parts)
    target = sum(part[2] for part in parts)
    return jnp.concatenate([jnp.stack([top, total, target, parts[0][3]]), jnp.zeros((4,) + top.shape, F32)])


def call(body, outs, in_specs, args, limit=16, scratch=()):
    many = isinstance(outs, (list, tuple))
    return pl.pallas_call(
        body,
        out_shape=outs,
        in_specs=in_specs,
        out_specs=[VMEM] * len(outs) if many else VMEM,
        scratch_shapes=scratch,
        compiler_params=pltpu.CompilerParams(vmem_limit_bytes=limit << 20),
    )(*args)


def up(value):
    return -(-value // LANES) * LANES


def per_device(groups, hidden, norm_gain, head, reward_head, tokens, lengths):
    section = lax.axis_index("section")
    core, pair = section % 2, section // 2
    sections = lax.axis_size("section")
    spans, positions = tokens.shape
    block, width, part = head.shape[1], head.shape[0], hidden.shape[2]
    count = 3 * spans * positions // 4 // sections
    half = positions // 2
    rows = hidden[0]

    def mesh_perm(move):
        pairs = []
        for s in range(sections):
            for d in range(groups):
                s2, d2 = move(s, d)
                pairs.append((s * groups + d, s2 * groups + d2))
        return pairs

    send = lambda value, perm: lax.ppermute(value, AXES, perm)
    like = lambda v: jax.ShapeDtypeStruct(v.shape, v.dtype)
    acc_shape = jax.ShapeDtypeStruct((2 * count, 2 * block), F32)
    stats_shape = jax.ShapeDtypeStruct((8, up(2 * count)), F32)
    ids_shape = jax.ShapeDtypeStruct((2 * count, 1), I32)
    perm_z = {k: mesh_perm(lambda s, d, k=k: (s, d ^ (2 * k))) for k in (1, 2, 3)}
    perm_x = mesh_perm(lambda s, d: (s, d ^ 1))
    gain = norm_gain[None]

    swap = [(s, s ^ 1) for s in range(sections)]
    over = [(s, s ^ 2) for s in range(sections)]
    extra = lax.ppermute(rows[half:], "section", [(1, 3), (3, 1)])
    sibling = lax.ppermute(rows, "section", swap)
    head_sibling = lax.ppermute(head, "section", swap)
    table, rows = call(
        table_kernel, [jax.ShapeDtypeStruct((2, part), F32), like(rows)], [VMEM] * 3, (gain, reward_head[None], rows)
    )

    if groups == 8:
        table = jnp.concatenate([table, send(table, perm_x)])
    token_ids = call(functools.partial(token_kernel, count), ids_shape, [SMEM, VMEM], (lengths, tokens))
    hit, per_row = call(
        functools.partial(mask_kernel, count),
        [
            jax.ShapeDtypeStruct((2, up(2 * count), positions), BF16),
            jax.ShapeDtypeStruct((8, LANES), F32),
        ],
        [SMEM],
        (lengths,),
    )
    full, table = call(
        functools.partial(pick_kernel, count),
        [jax.ShapeDtypeStruct((count, part), BF16), like(table)],
        [SMEM] + [VMEM] * 5 + [ANY] * 2,
        (lengths, rows, sibling, extra, gain, table, head_sibling, per_row),
    )

    if groups == 8:
        perm_a = mesh_perm(lambda s, d: (s, d ^ 1) if s % 2 == 0 else (s ^ 2, d))
        perm_b = mesh_perm(lambda s, d: (s ^ 2, d) if s % 2 == 0 else (s, d ^ 1))

        def gate(value, *after):
            return call(gate_kernel, like(value), [VMEM] + [ANY] * len(after), (value,) + after)

        side_shape = jax.ShapeDtypeStruct((2 * count, 2 * LANES), F32)
        perm_e = mesh_perm(lambda s, d: (s, d ^ (2 if s % 2 == 0 else 6)))
        perm_f = mesh_perm(lambda s, d: (s, d ^ (6 if s % 2 == 0 else 2)))
        z1 = send(full, perm_e)
        a0 = send(full, perm_a)
        b0 = send(full, perm_b)
        table = jnp.concatenate([table, send(table, perm_z[1])])
        z3 = send(call(padded_kernel, jax.ShapeDtypeStruct((count + 16, part), BF16), [VMEM, ANY], (full, z1)), perm_f)
        z1 = gate(z1, b0, table)
        a1 = send(z1, perm_a)
        b1 = send(z1, perm_b)
        c0 = send(a0, perm_b)
        z3 = call(gate_kernel, like(full), [VMEM] + [ANY], (z3, a1))
        a3 = send(z3, perm_a)
        table = jnp.concatenate([table, send(table, perm_z[2])])
        z2 = send(gate(z1, table), perm_f)
        z3 = gate(z3, b1, c0)
        b3 = send(z3, perm_b)
        acc, side, token_ids = call(
            begin_kernel,
            [acc_shape, side_shape, ids_shape],
            [VMEM] * 11 + [ANY],
            (head, head_sibling, table, full, a0, b0, c0, z1, a1, b1, token_ids, z3),
        )
        a3 = gate(a3, token_ids)
        c3 = send(a3, perm_b)
        a2 = send(z2, perm_a)
        b2 = send(z2, perm_b)
        c1 = send(c0, perm_e)
        acc, side = call(
            middle_kernel,
            [acc_shape, side_shape],
            [VMEM] * 9,
            (head, head_sibling, table, acc, side, z3, a3, b3, c3),
        )
        a2 = gate(a2, side)
        c2 = send(a2, perm_b)
        left, left_side, far_weights, wide = call(
            functools.partial(own_kernel, width),
            [
                jax.ShapeDtypeStruct((count, 2 * block), F32),
                jax.ShapeDtypeStruct((count, 2 * LANES), F32),
                jax.ShapeDtypeStruct((part, 2 * block), BF16),
                jax.ShapeDtypeStruct((up(2 * count), LANES), F32),
            ],
            [VMEM] * 10,
            (head, head_sibling, table, acc, side, z2, a2, b2, c1, token_ids),
            scratch=[pltpu.VMEM((2 * count, 2 * LANES), F32)],
        )
        stats = call(
            functools.partial(last_kernel, width),
            stats_shape,
            [VMEM] * 7,
            (far_weights, table, left, left_side, c2, wide, token_ids),
            scratch=[pltpu.VMEM((up(2 * count), LANES), F32), pltpu.VMEM((count, 2 * LANES), F32)],
        )
        stats = combine([stats] + [send(stats, perm_z[k]) for k in (1, 2, 3)])
        stats = combine(
            [stats]
            + [send(stats, mesh_perm(lambda s, d, v=v: (s ^ v[0], d ^ v[1]))) for v in ((0, 1), (2, 0), (2, 1))]
        )
    else:
        other = lax.ppermute(full, "section", over)
        ordered = jnp.concatenate([jnp.where(pair == 0, full, other), jnp.where(pair == 0, other, full)])
        everything = lax.all_gather(ordered, "dp", axis=1, tiled=True)
        acc = jnp.concatenate(
            [jnp.dot(everything, h, preferred_element_type=F32) for h in (head, head_sibling)], axis=1
        )
        gains, weights_all = (lax.all_gather(table[i], "dp", axis=0, tiled=True) for i in range(2))
        wide = everything.astype(F32)
        square = jnp.sum(wide * wide * gains, axis=1, keepdims=True)
        reward = jnp.sum(wide * weights_all, axis=1, keepdims=True)
        stats = call(
            functools.partial(whole_kernel, width), stats_shape, [VMEM] * 4, (acc, square, reward, token_ids)
        )
        gathered = lax.all_gather(stats, "dp")
        stats = combine([gathered[i] for i in range(groups)])
        stats = combine([stats, lax.ppermute(stats, "section", over)])
    filled = jnp.arange(stats.shape[1], dtype=jnp.int32)[None, :] < 2 * count
    lp = jnp.where(filled, stats[2:3] - (stats[0:1] + jnp.log(stats[1:2])), F32(0.0))
    lp = jnp.concatenate([lp, stats[3:4], jnp.zeros((6, lp.shape[1]), F32)])
    logprob, score = call(
        final_kernel,
        [jax.ShapeDtypeStruct((1, positions), F32), jax.ShapeDtypeStruct((1, 1), F32)],
        [VMEM] * 4,
        (lp, lax.ppermute(lp, "section", swap), hit, per_row),
    )
    return (logprob, score[0])


def solution(mesh):
    groups = mesh.shape["dp"]
    return jax.shard_map(
        lambda *args: per_device(groups, *args),
        mesh=mesh,
        in_specs=(P("section", None, "dp"), P("dp"), P(None, ("section", "dp")), P("dp"), P(), P()),
        out_specs=(P("section", None), P("section")),
        check_vma=False,
    )
```

```python
import functools

import jax
import jax.numpy as jnp
from jax import lax
from jax.experimental import pallas as pl
from jax.experimental.pallas import tpu as pltpu
from jax.sharding import PartitionSpec as P

AXES = ("section", "dp")
F32 = jnp.float32
BF16 = jnp.bfloat16
I32 = jnp.int32
LANES = 128
VMEM = pl.BlockSpec(memory_space=pltpu.VMEM)
SMEM = pl.BlockSpec(memory_space=pltpu.SMEM)
ANY = pl.BlockSpec(memory_space=pl.ANY)


def row_map(lengths, pair, core, index, count):
    first, second = lengths[2 * pair], lengths[2 * pair + 1]
    other_first = lengths[2 - 2 * pair]
    j = core * count + index
    in_first = j < first
    in_second = j < first + second
    span = jnp.where(in_first, 2 * pair, jnp.where(in_second, 2 * pair + 1, 3 - 2 * pair))
    place = jnp.where(
        in_first, j, jnp.where(in_second, j - first, 2 * count - other_first + j - first - second)
    )
    return span, place


def as_rows(columns, count):
    lane = lax.broadcasted_iota(I32, (count, LANES), 1)
    wide = jnp.zeros((count, LANES), F32)
    for i, column in enumerate(columns):
        wide = jnp.where(lane == i, column, wide)
    return jnp.transpose(wide)[:8]


def as_column(rows, which):
    full = jnp.concatenate([rows, jnp.zeros((LANES - 8, rows.shape[1]), F32)], axis=0)
    return jnp.transpose(full)[:, which : which + 1]


def table_kernel(gain, reward, rows, table, rows_out):
    rows_out[...] = rows[...]
    value = gain[...].astype(F32)
    table[0:1, :] = 1.0 / (value * value)
    table[1:2, :] = reward[...].astype(F32)


def pick_kernel(count, lengths, rows, sibling, extra, gain, table, after, ids, full, table_out):
    section = lax.axis_index("section")
    core, pair = lax.rem(section, 2), lax.div(section, 2)
    positions, half = rows.shape[0], extra.shape[0]
    index = lax.broadcasted_iota(I32, (count, 1), 0)
    span, place = row_map(lengths, pair, core, index, count)
    source = jnp.where(span == section, place, place + positions)
    source = jnp.where(span // 2 == pair, source, place + (2 * positions - (positions - half)))
    lane = lax.broadcasted_iota(I32, (count, 2 * positions + half), 1)
    pick = jnp.where(lane == source, F32(1.0), F32(0.0)).astype(BF16)
    picked = jnp.dot(pick[:, :positions], rows[...], preferred_element_type=F32)
    picked += jnp.dot(pick[:, positions : 2 * positions], sibling[...], preferred_element_type=F32)
    picked += jnp.dot(pick[:, 2 * positions :], extra[...], preferred_element_type=F32)
    full[...] = (picked * gain[...].astype(F32)).astype(BF16)
    table_out[...] = table[...]


def token_kernel(count, lengths, tokens, out):
    _, core, _ = here()
    spans, positions = tokens.shape
    index = lax.broadcasted_iota(I32, (count, 1), 0)
    lane = lax.broadcasted_iota(I32, (count, positions), 1)
    for pair in range(2):
        span, place = row_map(lengths, pair, core, index, count)
        found = jnp.zeros((count, positions), F32)
        for s in range(spans):
            found = jnp.where(span == s, tokens[s : s + 1, :].astype(F32), found)
        found = jnp.sum(jnp.where(lane == place, found, F32(0.0)), axis=1, keepdims=True)
        out[pair * count : pair * count + count, :] = found.astype(I32)


def mask_kernel(count, lengths, hit, per_row):
    section, core, _ = here()
    positions = hit.shape[2]
    index = lax.broadcasted_iota(I32, (count, 1), 0)
    lane = lax.broadcasted_iota(I32, (count, positions), 1)
    hit[...] = jnp.zeros(hit.shape, BF16)
    for pair in range(2):
        rows = slice(pair * count, pair * count + count)
        for which in range(2):
            span, place = row_map(lengths, pair, core + which - 2 * core * which, index, count)
            here_is = (lane == place) & (span == section)
            hit[which, rows, :] = jnp.where(here_is, F32(1.0), F32(0.0)).astype(BF16)
    per_row[...] = jnp.zeros(per_row.shape, F32) + 1.0 / lengths[section].astype(F32)


def here():
    section = lax.axis_index("section")
    return section, lax.rem(section, 2), lax.div(section, 2)


def blocks(count):
    _, _, pair = here()
    return pl.multiple_of(pair * count, 16), pl.multiple_of((1 - pair) * count, 16)


def weights(head, sibling, depth, k, far):
    dp_index = lax.axis_index("dp")
    where = jnp.bitwise_xor(dp_index, 2 * k + (1 if far else 0))
    rows = pl.ds(pl.multiple_of(where * depth, depth), depth)
    return head[rows, :], sibling[rows, :]


def products(terms):
    value = jnp.concatenate([t[0] for t in terms], axis=1) if len(terms) > 1 else terms[0][0]
    out = []
    for side in range(2):
        w = [t[1][side] for t in terms]
        w = jnp.concatenate(w, axis=0) if len(w) > 1 else w[0]
        out.append(jnp.dot(value, w, preferred_element_type=F32))
    return jnp.concatenate(out, axis=1)


def add_sides(terms, base, side_in, side):
    step = 32
    count, depth = terms[0][0].shape

    def body(i, _):
        rows = pl.ds(pl.multiple_of(i * step, step), step)
        at = pl.ds(pl.multiple_of(base + i * step, step), step)
        square, reward = jnp.zeros((step, LANES), F32), jnp.zeros((step, LANES), F32)
        if side_in is not None:
            square, reward = side_in[at, :LANES], side_in[at, LANES:]
        for piece, table, k in terms:
            for c in range(depth // LANES):
                cols = slice(c * LANES, (c + 1) * LANES)
                value = piece[rows, cols].astype(F32)
                square += value * value * table[2 * k : 2 * k + 1, cols]
                reward += value * table[2 * k + 1 : 2 * k + 2, cols]
        side[at, :LANES] = square
        side[at, LANES:] = reward
        return 0

    lax.fori_loop(0, count // step, body, 0, unroll=3)


def both_weights(head, sibling, depth, k):
    return weights(head, sibling, depth, k, False), weights(head, sibling, depth, k, True)


def begin_kernel(head, sibling, table, z, a, b, c, z1, a1, b1, ids, after, acc, side, ids_out):
    count, depth = z.shape
    _, core, _ = here()
    mine, others = blocks(count)
    near0, far0 = both_weights(head, sibling, depth, 0)
    for which, k, same, cross, same1, cross1 in ((0, 1, a, b, a1, b1), (1, 3, b, a, b1, a1)):

        @pl.when(core == which)
        def _():
            near1, far1 = both_weights(head, sibling, depth, k)
            rows = pl.ds(mine, count)
            acc[rows, :] = products([(z[...], near0), (same[...], far0), (z1[...], near1), (same1[...], far1)])
            terms = [(z, table, 0), (same, table, 1), (z1, table, 2 * k), (same1, table, 2 * k + 1)]
            add_sides(terms, mine, None, side)
            rows = pl.ds(others, count)
            acc[rows, :] = products([(cross[...], near0), (c[...], far0), (cross1[...], near1)])
            add_sides([(cross, table, 0), (c, table, 1), (cross1, table, 2 * k)], others, None, side)

    ids_out[...] = ids[...]


def middle_kernel(head, sibling, table, acc_in, side_in, z, a, b, c, acc, side):
    count, depth = z.shape
    _, core, _ = here()
    mine, others = blocks(count)
    for which, k, same, cross in ((0, 3, a, b), (1, 1, b, a)):

        @pl.when(core == which)
        def _():
            near3, far3 = both_weights(head, sibling, depth, k)
            rows = pl.ds(mine, count)
            acc[rows, :] = acc_in[rows, :] + products([(z[...], near3), (same[...], far3)])
            add_sides([(z, table, 2 * k), (same, table, 2 * k + 1)], mine, side_in, side)
            rows = pl.ds(others, count)
            acc[rows, :] = acc_in[rows, :] + products([(cross[...], near3), (c[...], far3)])
            add_sides([(cross, table, 2 * k), (c, table, 2 * k + 1)], others, side_in, side)


def gate_kernel(value, *refs):
    refs[-1][...] = value[: refs[-1].shape[0], :]


def padded_kernel(value, after, out):
    out[: value.shape[0], :] = value[...]
    out[value.shape[0] :, :] = jnp.zeros((out.shape[0] - value.shape[0], out.shape[1]), out.dtype)


def column_ids(block):
    section, core, _ = here()
    dp_index, groups = lax.axis_index("dp"), lax.axis_size("dp")
    lane = lax.broadcasted_iota(I32, (1, block), 1)
    own = (section * groups + dp_index) * block
    other = ((section + 1 - 2 * core) * groups + dp_index) * block
    return jnp.concatenate([lane + own, lane + other], axis=1)


def summary(logits, square, reward, token_ids, ids, width):
    scale = lax.rsqrt(square / width + 1e-05)
    logits = logits * scale
    top = jnp.max(logits, axis=1, keepdims=True)
    total = jnp.sum(jnp.exp(logits - top), axis=1, keepdims=True)
    target = jnp.sum(jnp.where(ids == token_ids, logits, F32(0.0)), axis=1, keepdims=True)
    lane = lax.broadcasted_iota(I32, (logits.shape[0], LANES), 1)
    wide = jnp.where(lane == 2, target, jnp.where(lane == 3, reward * scale, F32(0.0)))
    return jnp.where(lane == 0, top, jnp.where(lane == 1, total, wide))


def added(side):
    return jnp.sum(side[:, :LANES], axis=1, keepdims=True), jnp.sum(side[:, LANES:], axis=1, keepdims=True)


def own_kernel(width, head, sibling, table, acc_in, side_in, z, a, b, c1, token_ids, left, left_side, far_out, wide, side):
    count, depth = z.shape
    _, core, _ = here()
    mine, others = blocks(count)
    near2, far2 = weights(head, sibling, depth, 2, False), weights(head, sibling, depth, 2, True)
    block = head.shape[1]
    far_out[:, :block] = far2[0]
    far_out[:, block:] = far2[1]
    ids = column_ids(block)
    wide[...] = jnp.zeros(wide.shape, F32)
    for which, k, same, cross in ((0, 1, a, b), (1, 3, b, a)):

        @pl.when(core == which)
        def _():
            far1 = weights(head, sibling, depth, k, True)
            rows = pl.ds(mine, count)
            logits = acc_in[rows, :] + products([(z[...], near2), (same[...], far2)])
            add_sides([(z, table, 4), (same, table, 5)], mine, side_in, side)
            square, reward = added(side[rows, :])
            wide[rows, :] = summary(logits, square, reward, token_ids[rows, :], ids, width)
            rows = pl.ds(others, count)
            left[...] = acc_in[rows, :] + products([(cross[...], near2), (c1[...], far1)])
            add_sides([(cross, table, 4), (c1, table, 2 * k + 1)], others, side_in, side)
            left_side[...] = side[rows, :]


def last_kernel(width, far_weights, table, left, left_side, c, wide_in, token_ids, out, wide, side):
    count = c.shape[0]
    _, others = blocks(count)
    ids = column_ids(far_weights.shape[1] // 2)
    wide[...] = wide_in[...]
    logits = left[...] + jnp.dot(c[...], far_weights[...], preferred_element_type=F32)
    add_sides([(c, table, 5)], 0, left_side, side)
    square, reward = added(side[...])
    rows = pl.ds(others, count)
    wide[rows, :] = summary(logits, square, reward, token_ids[rows, :], ids, width)
    out[...] = jnp.transpose(wide[...])[:8]


def whole_kernel(width, acc, square, reward, token_ids, out):
    count = acc.shape[0] // 2
    ids = column_ids(acc.shape[1] // 2)
    wide = summary(acc[...], square[...], reward[...], token_ids[...], ids, width)
    wide = jnp.concatenate([wide, jnp.zeros((out.shape[1] - 2 * count, LANES), F32)])
    out[...] = jnp.transpose(wide)[:8]


def final_kernel(mine, sibling, hit, per_row, out_ref, score_ref):
    picked = jnp.zeros((8, hit.shape[2]), F32)
    for core, values in enumerate((mine, sibling)):
        rest, terms = values[0:2, :], []
        for _ in range(3):
            terms.append(rest.astype(BF16).astype(F32))
            rest = rest - terms[-1]
        stacked = jnp.concatenate(terms + [jnp.zeros_like(rest)], axis=0).astype(BF16)
        picked += jnp.dot(stacked, hit[core], preferred_element_type=F32)
    picked = picked[0:2, :] + (picked[2:4, :] + picked[4:6, :])
    out_ref[...] = picked[0:1, :]
    score_ref[...] = jnp.sum(picked[1:2, :], axis=1, keepdims=True) * per_row[0:1, 0:1]


def combine(parts):
    top = parts[0][0]
    for part in parts[1:]:
        top = jnp.maximum(top, part[0])
    total = sum(part[1] * jnp.exp(part[0] - top) for part in parts)
    target = sum(part[2] for part in parts)
    return jnp.concatenate([jnp.stack([top, total, target, parts[0][3]]), jnp.zeros((4,) + top.shape, F32)])


def call(body, outs, in_specs, args, limit=16, scratch=()):
    many = isinstance(outs, (list, tuple))
    return pl.pallas_call(
        body,
        out_shape=outs,
        in_specs=in_specs,
        out_specs=[VMEM] * len(outs) if many else VMEM,
        scratch_shapes=scratch,
        compiler_params=pltpu.CompilerParams(vmem_limit_bytes=limit << 20),
    )(*args)


def up(value):
    return -(-value // LANES) * LANES


def per_device(groups, hidden, norm_gain, head, reward_head, tokens, lengths):
    section = lax.axis_index("section")
    core, pair = section % 2, section // 2
    sections = lax.axis_size("section")
    spans, positions = tokens.shape
    block, width, part = head.shape[1], head.shape[0], hidden.shape[2]
    count = 3 * spans * positions // 4 // sections
    half = positions // 2
    rows = hidden[0]

    def mesh_perm(move):
        pairs = []
        for s in range(sections):
            for d in range(groups):
                s2, d2 = move(s, d)
                pairs.append((s * groups + d, s2 * groups + d2))
        return pairs

    send = lambda value, perm: lax.ppermute(value, AXES, perm)
    like = lambda v: jax.ShapeDtypeStruct(v.shape, v.dtype)
    acc_shape = jax.ShapeDtypeStruct((2 * count, 2 * block), F32)
    stats_shape = jax.ShapeDtypeStruct((8, up(2 * count)), F32)
    ids_shape = jax.ShapeDtypeStruct((2 * count, 1), I32)
    perm_z = {k: mesh_perm(lambda s, d, k=k: (s, d ^ (2 * k))) for k in (1, 2, 3)}
    perm_x = mesh_perm(lambda s, d: (s, d ^ 1))
    gain = norm_gain[None]

    swap = [(s, s ^ 1) for s in range(sections)]
    over = [(s, s ^ 2) for s in range(sections)]
    extra = lax.ppermute(rows[half:], "section", [(1, 3), (3, 1)])
    sibling = lax.ppermute(rows, "section", swap)
    head_sibling = lax.ppermute(head, "section", swap)
    table, rows = call(
        table_kernel, [jax.ShapeDtypeStruct((2, part), F32), like(rows)], [VMEM] * 3, (gain, reward_head[None], rows)
    )

    if groups == 8:
        table = jnp.concatenate([table, send(table, perm_x)])
    token_ids = call(functools.partial(token_kernel, count), ids_shape, [SMEM, VMEM], (lengths, tokens))
    hit, per_row = call(
        functools.partial(mask_kernel, count),
        [
            jax.ShapeDtypeStruct((2, up(2 * count), positions), BF16),
            jax.ShapeDtypeStruct((8, LANES), F32),
        ],
        [SMEM],
        (lengths,),
    )
    full, table = call(
        functools.partial(pick_kernel, count),
        [jax.ShapeDtypeStruct((count, part), BF16), like(table)],
        [SMEM] + [VMEM] * 5 + [ANY] * 2,
        (lengths, rows, sibling, extra, gain, table, head_sibling, per_row),
    )

    if groups == 8:
        perm_a = mesh_perm(lambda s, d: (s, d ^ 1) if s % 2 == 0 else (s ^ 2, d))
        perm_b = mesh_perm(lambda s, d: (s ^ 2, d) if s % 2 == 0 else (s, d ^ 1))

        def gate(value, *after):
            return call(gate_kernel, like(value), [VMEM] + [ANY] * len(after), (value,) + after)

        side_shape = jax.ShapeDtypeStruct((2 * count, 2 * LANES), F32)
        perm_e = mesh_perm(lambda s, d: (s, d ^ (2 if s % 2 == 0 else 6)))
        perm_f = mesh_perm(lambda s, d: (s, d ^ (6 if s % 2 == 0 else 2)))
        z1 = send(full, perm_e)
        a0 = send(full, perm_a)
        b0 = send(full, perm_b)
        table = jnp.concatenate([table, send(table, perm_z[1])])
        z3 = send(call(padded_kernel, jax.ShapeDtypeStruct((count + 16, part), BF16), [VMEM, ANY], (full, z1)), perm_f)
        z1 = gate(z1, b0, table)
        a1 = send(z1, perm_a)
        b1 = send(z1, perm_b)
        c0 = send(a0, perm_b)
        z3 = call(gate_kernel, like(full), [VMEM] + [ANY], (z3, a1))
        a3 = send(z3, perm_a)
        table = jnp.concatenate([table, send(table, perm_z[2])])
        z2 = send(gate(z1, table), perm_f)
        z3 = gate(z3, b1, c0)
        b3 = send(z3, perm_b)
        acc, side, token_ids = call(
            begin_kernel,
            [acc_shape, side_shape, ids_shape],
            [VMEM] * 11 + [ANY],
            (head, head_sibling, table, full, a0, b0, c0, z1, a1, b1, token_ids, z3),
        )
        a3 = gate(a3, token_ids)
        c3 = send(a3, perm_b)
        a2 = send(z2, perm_a)
        b2 = send(z2, perm_b)
        c1 = send(c0, perm_e)
        acc, side = call(
            middle_kernel,
            [acc_shape, side_shape],
            [VMEM] * 9,
            (head, head_sibling, table, acc, side, z3, a3, b3, c3),
        )
        a2 = gate(a2, side)
        c2 = send(a2, perm_b)
        left, left_side, far_weights, wide = call(
            functools.partial(own_kernel, width),
            [
                jax.ShapeDtypeStruct((count, 2 * block), F32),
                jax.ShapeDtypeStruct((count, 2 * LANES), F32),
                jax.ShapeDtypeStruct((part, 2 * block), BF16),
                jax.ShapeDtypeStruct((up(2 * count), LANES), F32),
            ],
            [VMEM] * 10,
            (head, head_sibling, table, acc, side, z2, a2, b2, c1, token_ids),
            scratch=[pltpu.VMEM((2 * count, 2 * LANES), F32)],
        )
        stats = call(
            functools.partial(last_kernel, width),
            stats_shape,
            [VMEM] * 7,
            (far_weights, table, left, left_side, c2, wide, token_ids),
            scratch=[pltpu.VMEM((up(2 * count), LANES), F32), pltpu.VMEM((count, 2 * LANES), F32)],
        )
        stats = combine([stats] + [send(stats, perm_z[k]) for k in (1, 2, 3)])
        stats = combine(
            [stats]
            + [send(stats, mesh_perm(lambda s, d, v=v: (s ^ v[0], d ^ v[1]))) for v in ((0, 1), (2, 0), (2, 1))]
        )
    else:
        other = lax.ppermute(full, "section", over)
        ordered = jnp.concatenate([jnp.where(pair == 0, full, other), jnp.where(pair == 0, other, full)])
        everything = lax.all_gather(ordered, "dp", axis=1, tiled=True)
        acc = jnp.concatenate(
            [jnp.dot(everything, h, preferred_element_type=F32) for h in (head, head_sibling)], axis=1
        )
        gains, weights_all = (lax.all_gather(table[i], "dp", axis=0, tiled=True) for i in range(2))
        wide = everything.astype(F32)
        square = jnp.sum(wide * wide * gains, axis=1, keepdims=True)
        reward = jnp.sum(wide * weights_all, axis=1, keepdims=True)
        stats = call(
            functools.partial(whole_kernel, width), stats_shape, [VMEM] * 4, (acc, square, reward, token_ids)
        )
        gathered = lax.all_gather(stats, "dp")
        stats = combine([gathered[i] for i in range(groups)])
        stats = combine([stats, lax.ppermute(stats, "section", over)])
    filled = jnp.arange(stats.shape[1], dtype=jnp.int32)[None, :] < 2 * count
    lp = jnp.where(filled, stats[2:3] - (stats[0:1] + jnp.log(stats[1:2])), F32(0.0))
    lp = jnp.concatenate([lp, stats[3:4], jnp.zeros((6, lp.shape[1]), F32)])
    logprob, score = call(
        final_kernel,
        [jax.ShapeDtypeStruct((1, positions), F32), jax.ShapeDtypeStruct((1, 1), F32)],
        [VMEM] * 4,
        (lp, lax.ppermute(lp, "section", swap), hit, per_row),
    )
    return (logprob, score[0])


def solution(mesh):
    groups = mesh.shape["dp"]
    return jax.shard_map(
        lambda *args: per_device(groups, *args),
        mesh=mesh,
        in_specs=(P("section", None, "dp"), P("dp"), P(None, ("section", "dp")), P("dp"), P(), P()),
        out_specs=(P("section", None), P("section")),
        check_vma=False,
    )
```
